128 devices in a mesh: expert: 4 (over z), dp: 32 (over x, y, core).
Axes of the slice: x: 4, y: 4, z: 4, core: 2. Of those that a mesh axis runs over, the one named last changes fastest.
Arguments:
- tokens: bfloat16 [65536, 512], P(('expert', 'dp')), may hold values from -6 to 6
- segments: int32 [128, 512], P(('expert', 'dp')), may hold values from 0 to 31, never falling along the last dimension, each value on 1 to 49 neighbouring positions
- routes: int32 [65536, 2], P(('expert', 'dp')), may hold values from 0 to 31, all different within a row; in each aligned block of 512 rows (0 to 511, 512 to 1023, ...) at most 64 rows name the same one
- priority: int32 [65536], P(('expert', 'dp')), may hold values from 0 to 65535, each once
- ln1_gain: float32 [512], replicated, may hold values from 0.1 to 1.9
- ln1_bias: float32 [512], replicated, may hold values from -3 to 3
- w_qkv: bfloat16 [512, 1536], replicated, may hold values from -0.25 to 0.25
- w_out: bfloat16 [512, 512], replicated, may hold values from -1 to 1
- ln2_gain: float32 [512], replicated, may hold values from 0.1 to 1.9
- ln2_bias: float32 [512], replicated, may hold values from -3 to 3
- w_router: bfloat16 [512, 32], replicated, may hold values from -0.1875 to 0.1875
- expert_in: bfloat16 [32, 512, 2048], P('dp', None, 'expert'), may hold values from -0.25 to 0.25
- expert_out: bfloat16 [32, 2048, 512], P('dp', 'expert'), may hold values from -2 to 2
- cotangent: bfloat16 [65536, 512], P(('expert', 'dp')), may hold values from -6 to 6
Outputs:
- output: bfloat16 [65536, 512], P(('expert', 'dp'))
- d_tokens: float32 [65536, 512], P(('expert', 'dp'))
- d_ln1_gain: float32 [512], replicated
- d_ln1_bias: float32 [512], replicated
- d_w_qkv: float32 [512, 1536], replicated
- d_w_out: float32 [512, 512], replicated
- d_ln2_gain: float32 [512], replicated
- d_ln2_bias: float32 [512], replicated
- d_w_router: float32 [512, 32], replicated
- d_expert_in: float32 [32, 512, 2048], P('dp', None, 'expert')
- d_expert_out: float32 [32, 2048, 512], P('dp', 'expert')
The draws below stay inside these ranges and needn't reach their ends.
Inputs may be any that keep to these rules, and one draw needn't show every extreme that they name: `routes`: of the rows of one device, each expert is named by at most 64, a bound that some block reaches. `segments`: ids never fall along a row; each id covers 1 to 49 slots, some exactly 49. `priority`: A permutation.
All inputs are finite; a program needn't handle non-finite values.
Results may differ from the reference program's by a relative error of at most 0.018.
Values may be sent and summed in bfloat16 or wider, within the bound.
No kernel may reach another device: no remote copies, remote signals or barrier semaphores. Data moves between devices by JAX's collectives and lax.ppermute only.
A program may use at most 192 MiB of HBM per device.

```python
import math
import jax
import jax.numpy as jnp
import numpy as np
from jax import lax

D = 512
HEADS = 8
HDIM = 64
FF = 2048
EXPERTS = 32
PATCHES = 49
TOK_DEV = 512
MOST = 64
SEQS = 128
TOKENS = 65536
CAP = 4301
N_EXPERT = 4
N_DP = 32


def steps_of(stream_key, extent, cuts, smallest, largest):
    loudness = 1.0
    for position, shards_of in cuts:
        draws = jax.random.uniform(jax.random.fold_in(jax.random.fold_in(stream_key, 6), position), (shards_of,), jnp.float32, smallest / len(cuts), largest / len(cuts))
        loudness = loudness * jnp.repeat(jnp.exp(draws), extent[position] // shards_of).reshape((-1,) + (1,) * (len(extent) - 1 - position))
    return loudness


def profile(amount, total, most, lean):
    loads = [(1 << 20) // math.isqrt(rank ** lean) + 1 for rank in range(2, amount + 1)]
    surplus, given = total - most - (amount - 1), [1] * (amount - 1)
    while surplus > 0:
        candidates = [i for i in range(amount - 1) if given[i] < most]
        whole, budget = sum([loads[i] for i in candidates]), surplus
        for i in candidates:
            more = min(most - given[i], max(1, budget * loads[i] // whole), surplus)
            given[i] = given[i] + more
            surplus = surplus - more
    return np.array([most] + given)


def uneven_parts(key, amount, total, most, lean):
    if amount == 2:
        one = jax.random.randint(key, (), max(1, total - most), min(most, total - 1) + 1)
        return jnp.stack([one, total - one])
    tallies = jnp.asarray(profile(amount, total, most, lean), jnp.int32)
    couples = (amount - 1) // 2
    donor, taker = tallies[1:1 + 2 * couples:2], tallies[2:2 + 2 * couples:2]
    slack = jnp.minimum(donor - 1, most - taker)
    shifted = jax.random.randint(jax.random.fold_in(key, 1), (couples,), 0, 1 << 20) % (slack + 1)
    tallies = tallies.at[1:1 + 2 * couples:2].set(donor - shifted).at[2:2 + 2 * couples:2].set(taker + shifted)
    return tallies[jax.random.permutation(jax.random.fold_in(key, 2), amount)]


def shared_out(stream_key, own, number, rows, number_of, top, reach, lean):
    order = jax.random.permutation(stream_key, number_of)
    heavy_load, usual = load_shares(number_of, rows * top, reach, lean, True), load_shares(number_of, rows * top, reach, lean, False)
    places = jnp.arange(number_of)

    def named(lengths, offset_by):
        used = int((lengths > 0).sum())
        fixed = max(1, used // 4)
        moved = fixed + (places - fixed + offset_by * (used - fixed)) % max(1, number_of - fixed)
        return jnp.zeros((number_of,), jnp.int32).at[order[jnp.where(places < fixed, places, moved)]].set(jnp.asarray(lengths, jnp.int32))

    lengths = jnp.where(number % 4 == 0, named(heavy_load, number // 4), named(usual, number - number // 4 - 1))
    mixed = jax.random.permutation(jax.random.fold_in(own, 3), number_of)
    giver, taker = mixed[0:number_of // 2 * 2:2], mixed[1:number_of // 2 * 2:2]
    room = jnp.minimum(lengths[giver] - 1, reach - lengths[taker]) // 2
    room = jnp.where((giver == order[0]) | (taker == order[0]) | (lengths[taker] == 0), 0, jnp.maximum(room, 0))
    moved = jax.random.randint(jax.random.fold_in(own, 4), (number_of // 2,), 0, 1 << 20) % (room + 1)
    lengths = lengths.at[giver].add(-moved).at[taker].add(moved)
    members = jnp.searchsorted(jnp.cumsum(lengths), jnp.arange(rows * top), side="right").astype(jnp.int32)
    table = members.reshape(top, rows).T
    table = table[jax.random.permutation(jax.random.fold_in(own, 1), rows)]
    offset_by = jax.random.randint(jax.random.fold_in(own, 2), (rows, 1), 0, top)
    return jnp.take_along_axis(table, (jnp.arange(top)[None, :] + offset_by) % top, axis=1)


def load_shares(amount, total, most, skew, full):
    loads = [(1 << 20) // math.isqrt(grade ** skew) + 1 for grade in range(1, amount + 1)]
    largest = most if full else min(most, max(-(-total // amount), total * loads[0] // sum(loads)))
    least = 1 if total - largest >= amount - 1 else 0
    counts, rest = [largest] + [least] * (amount - 1), total - largest - least * (amount - 1)
    while rest > 0:
        candidates = [i for i in range(1, amount) if counts[i] < largest] or [i for i in range(1, amount) if counts[i] < most]
        mass, left = sum([loads[i] for i in candidates]), rest
        for i in candidates:
            more = min(most - counts[i], max(1, left * loads[i] // mass), rest)
            counts[i] = counts[i] + more
            rest = rest - more
    return np.array(counts)


def normal_values(stream_key, shape, width, reach, shards=(), kind=jnp.bfloat16):
    drawn = width * jax.random.normal(stream_key, shape, jnp.float32)
    if shards:
        drawn = drawn * steps_of(stream_key, shape, shards, -0.22, 0.18)
    return jnp.clip(drawn, -reach, reach).astype(kind)


def setup_inputs(seed: int = 0) -> dict:
    arg_keys = jax.random.split(jax.random.key(seed), 15)
    tokens = normal_values(arg_keys[0], (TOKENS, D), 1.0, 6.0, ((0, 128),))
    segments = jax.vmap(lambda own: jnp.searchsorted(jnp.cumsum(uneven_parts(own, max(TOK_DEV // 16, 2 * ((TOK_DEV + PATCHES - 1) // PATCHES)), TOK_DEV, PATCHES, 1)), jnp.arange(TOK_DEV), side="right"))(jax.random.split(arg_keys[1], SEQS)).reshape((SEQS, TOK_DEV)).astype(jnp.int32)
    routes_keys = jax.random.split(jax.random.fold_in(arg_keys[2], 1), TOKENS // TOK_DEV)
    routes_turns = jax.random.permutation(jax.random.fold_in(arg_keys[2], 3), TOKENS // TOK_DEV)
    routes = jax.vmap(lambda own, number: shared_out(jax.random.fold_in(arg_keys[2], 2), own, number, TOK_DEV, EXPERTS, 2, MOST, 2))(routes_keys, routes_turns).reshape((TOKENS, 2))
    priority = jax.random.permutation(arg_keys[3], TOKENS).astype(jnp.int32)
    ln1_gain = jnp.clip(1.0 + 0.18 * jax.random.normal(arg_keys[4], (D,), jnp.float32), 0.1, 1.9)
    ln1_bias = normal_values(arg_keys[5], (D,), 0.5, 3.0, (), jnp.float32)
    w_qkv = normal_values(arg_keys[6], (D, 3 * D), D ** -0.5, 0.25)
    w_out = normal_values(arg_keys[7], (D, D), (D // 16) ** -0.5, 1.0)
    ln2_gain = jnp.clip(1.0 + 0.18 * jax.random.normal(arg_keys[8], (D,), jnp.float32), 0.1, 1.9)
    ln2_bias = normal_values(arg_keys[9], (D,), 0.5, 3.0, (), jnp.float32)
    w_router = normal_values(arg_keys[10], (D, EXPERTS), (2 * D) ** -0.5, 0.1875)
    expert_in = normal_values(arg_keys[11], (EXPERTS, D, FF), D ** -0.5, 0.25, ((0, 32), (2, 4)))
    expert_out = normal_values(arg_keys[12], (EXPERTS, FF, D), (max(FF // 256, 1)) ** -0.5, 2.0, ((0, 32), (1, 4)))
    cotangent = normal_values(arg_keys[13], (TOKENS, D), 1.0, 6.0, ((0, 128),))
    return {"tokens": tokens, "segments": segments, "routes": routes, "priority": priority, "ln1_gain": ln1_gain, "ln1_bias": ln1_bias, "w_qkv": w_qkv, "w_out": w_out, "ln2_gain": ln2_gain, "ln2_bias": ln2_bias, "w_router": w_router, "expert_in": expert_in, "expert_out": expert_out, "cotangent": cotangent}


@jax.custom_vjp
def low(v):
    return lax.optimization_barrier(v.astype(jnp.bfloat16)).astype(jnp.float32)

@jax.custom_vjp
def low_back(v):
    return v

def low_keep(v):
    return (low(v), None)

def low_pass(kept, grad):
    return (grad,)

def back_keep(v):
    return (v, None)

def back_low(kept, grad):
    return (low(grad),)
low.defvjp(low_keep, low_pass)
low_back.defvjp(back_keep, back_low)
highest_prec = lax.Precision.HIGHEST
eps_norm = 1e-06

def layer_norm(values, gain_vec, shift_vec):
    center = values - lax.optimization_barrier(jnp.mean(values, axis=-1, keepdims=True))
    factor = lax.rsqrt(lax.optimization_barrier(jnp.mean(center * center, axis=-1, keepdims=True)) + eps_norm)
    return center * factor * gain_vec + shift_vec

def reference(tokens, segments, routes, priority, ln1_gain, ln1_bias, w_qkv, w_out, ln2_gain, ln2_bias, w_router, expert_in, expert_out, cotangent):
    devices = N_EXPERT * N_DP
    per_group = math.gcd(devices, max(1, 4096 // TOK_DEV))
    labels = segments.reshape(devices // per_group, per_group, TOK_DEV)
    slot_route = routes.reshape(devices, 2 * TOK_DEV)
    experts_iota = jnp.arange(EXPERTS, dtype=jnp.int32)
    onehot = (slot_route[:, :, None] == experts_iota).astype(jnp.int32)
    within = lax.optimization_barrier(jnp.sum((jnp.cumsum(onehot, axis=1) - onehot) * onehot, axis=2))
    buffer_len = devices * MOST
    device_iota = jnp.arange(devices, dtype=jnp.int32)[:, None]
    slot_pos = (slot_route * buffer_len + device_iota * MOST + within).reshape(-1).astype(jnp.int32)
    gather_idx = jnp.zeros((EXPERTS * buffer_len,), jnp.int32).at[slot_pos].set(jnp.arange(2 * TOKENS, dtype=jnp.int32)).reshape(EXPERTS, buffer_len)
    flat_route = routes.reshape(-1)
    slot_keys = (jnp.arange(2, dtype=jnp.int32)[None, :] * TOKENS + priority[:, None]).reshape(-1)
    ordering = jnp.argsort(slot_keys)
    sorted_hot = (flat_route[ordering][:, None] == experts_iota).astype(jnp.int32)
    sorted_rank = lax.optimization_barrier(jnp.sum((jnp.cumsum(sorted_hot, axis=0) - sorted_hot) * sorted_hot, axis=1))
    slot_rank = jnp.zeros((2 * TOKENS,), jnp.int32).at[ordering].set(sorted_rank)
    kept_mask = (slot_rank < CAP).astype(jnp.float32).reshape(TOKENS, 2)

    def forward(inputs, gain1, shift1, qkv_weight, out_weight, gain2, shift2, router_weight, first_layer, second_layer):
        normed = low(layer_norm(inputs, gain1, shift1))
        grouped = normed.reshape(devices // per_group, per_group, TOK_DEV, D)

        def attend_group(group_pair):
            block_rows, seg_marks = group_pair
            packed = jnp.einsum('gsd,de->gse', block_rows, qkv_weight, precision=highest_prec)
            packed = packed.reshape(per_group, TOK_DEV, 3, HEADS, HDIM)
            queries = low_back(low(packed[:, :, 0]))
            keys_in = low_back(low(packed[:, :, 1]))
            values = low_back(low(packed[:, :, 2]))
            scores = jnp.einsum('gqhc,gkhc->ghqk', queries, keys_in, precision=highest_prec) * HDIM ** (-0.5)
            same_doc = seg_marks[:, :, None] == seg_marks[:, None, :]
            scores = low_back(jnp.where(same_doc[:, None], scores, -1e+30))
            raised = jnp.exp(scores - lax.optimization_barrier(jnp.max(scores, axis=-1, keepdims=True)))
            weights = raised / lax.optimization_barrier(jnp.sum(raised, axis=-1, keepdims=True))
            attended = jnp.einsum('ghqk,gkhc->gqhc', low(weights), values, precision=highest_prec)
            attended = low_back(low(attended)).reshape(per_group, TOK_DEV, D)
            return low_back(jnp.einsum('gsd,de->gse', attended, out_weight, precision=highest_prec))
        branch = lax.map(jax.checkpoint(attend_group), (grouped, labels)).reshape(TOKENS, D)
        residual = inputs + branch
        second = low(layer_norm(residual, gain2, shift2))
        logits = jnp.dot(second, router_weight, precision=highest_prec)
        raised = jnp.exp(logits - lax.optimization_barrier(jnp.max(logits, axis=-1, keepdims=True)))
        router_prob = raised / lax.optimization_barrier(jnp.sum(raised, axis=-1, keepdims=True))
        gate_pick = jnp.take_along_axis(router_prob, routes, axis=1)
        slot_rows = low_back(jnp.stack([second, second], axis=1)).reshape(2 * TOKENS, D)

        def run_expert(expert_pack):
            w_first, w_second, picks = expert_pack
            chosen = slot_rows[picks]
            hidden_act = low(jax.nn.gelu(low_back(jnp.dot(chosen, w_first, precision=highest_prec)), approximate=True))
            return low_back(low(jnp.dot(hidden_act, w_second, precision=highest_prec)))
        results = lax.map(jax.checkpoint(run_expert), (first_layer, second_layer, gather_idx))
        slot_out = results.reshape(EXPERTS * buffer_len, D)[slot_pos].reshape(TOKENS, 2, D)
        return residual + lax.optimization_barrier(jnp.sum((kept_mask * gate_pick)[:, :, None] * slot_out, axis=1))
    floats = tuple((item.astype(jnp.float32) for item in (tokens, ln1_gain, ln1_bias, w_qkv, w_out, ln2_gain, ln2_bias, w_router, expert_in, expert_out)))
    output, pullback = jax.vjp(forward, *floats)
    gradients = pullback(cotangent.astype(jnp.float32))
    return (output.astype(jnp.bfloat16), gradients[0], gradients[1], gradients[2], gradients[3], gradients[4], gradients[5], gradients[6], gradients[7], gradients[8], gradients[9])
```

```python
import functools

import jax
import jax.numpy as jnp
from jax import lax
from jax.experimental import pallas as pl
from jax.experimental.pallas import tpu as pltpu
from jax.sharding import PartitionSpec as P

D = 512
HEADS = 8
HDIM = 64
EXPERTS = 32
MOST = 64
ROWS = 512
SLOTS = EXPERTS * MOST
N_Z = 4
N_DP = 32
CAP = (21 * N_Z * N_DP * ROWS + 319) // 320
TOKENS = N_Z * N_DP * ROWS
EXTRA = 8
EPS = 1e-06
SCALE = HDIM ** (-0.5)
STARTS = (0, 64, 192, 256)
GELU_C = 0.7978845608028654
GELU_A = 0.044715

bf16 = jnp.bfloat16
f32 = jnp.float32
VMEM_LIMIT = 56 * 1024 * 1024


def dot(a, b):
    return lax.dot_general(a, b, (((1,), (0,)), ((), ())), preferred_element_type=f32)


def dot_nt(a, b):
    return lax.dot_general(a, b, (((1,), (1,)), ((), ())), preferred_element_type=f32)


def dot_tn(a, b):
    return lax.dot_general(a, b, (((0,), (0,)), ((), ())), preferred_element_type=f32)


def iota(shape, dim):
    return lax.broadcasted_iota(jnp.int32, shape, dim)


def normalize(values):
    center = values - jnp.mean(values, axis=-1, keepdims=True)
    factor = lax.rsqrt(jnp.mean(center * center, axis=-1, keepdims=True) + EPS)
    return center * factor, factor


def norm_backward(upstream, normal, factor, gain):
    scaled = upstream * gain
    inner = (
        scaled
        - jnp.mean(scaled, axis=-1, keepdims=True)
        - normal * jnp.mean(scaled * normal, axis=-1, keepdims=True)
    )
    return (
        inner * factor,
        jnp.sum(upstream * normal, axis=0, keepdims=True),
        jnp.sum(upstream, axis=0, keepdims=True),
    )


def pick_rows(csel_ref, rows, store):
    place = iota((MOST, ROWS), 0).astype(f32)
    for group in range(EXPERTS // 4):
        parts = []
        for j in range(4):
            line = csel_ref[group * 4 + j : group * 4 + j + 1, :]
            parts.append((place == line).astype(f32).astype(bf16))
        hot = jnp.concatenate(parts, axis=0)
        store(group, dot(hot, rows).astype(bf16))


def pack_kernel(routes_ref, prio_ref, seg_ref, cot_ref, send_ref, csel_ref, cols_ref, wide_ref):
    routes = routes_ref[...]
    experts = iota((EXPERTS, ROWS), 0)
    first = routes[0:1] == experts
    second = routes[1:2] == experts
    either = jnp.logical_or(first, second)
    before = (iota((ROWS, ROWS), 0) < iota((ROWS, ROWS), 1)).astype(f32).astype(bf16)
    count = dot(either.astype(f32).astype(bf16), before)
    slot = count + (experts * MOST).astype(f32)
    wide_ref[...] = jnp.zeros_like(wide_ref)
    wide_ref[0:1, :] = jnp.sum(jnp.where(first, slot, 0.0), axis=0, keepdims=True)
    wide_ref[1:2, :] = jnp.sum(jnp.where(second, slot, 0.0), axis=0, keepdims=True)
    wide_ref[2:3, :] = prio_ref[...].astype(f32)
    wide_ref[3:4, :] = seg_ref[...].astype(f32)
    csel_ref[...] = jnp.where(either, count, -1.0)
    cols = wide_ref[...].T
    cols_ref[...] = cols
    cols_int = cols[:, 0:3].astype(jnp.int32)
    pos0, pos1, key = cols_int[:, 0:1], cols_int[:, 1:2], cols_int[:, 2:3] + 1
    zeros = jnp.zeros((EXTRA, D), bf16)
    digit = iota((EXTRA, 256), 0)

    def store(group, rows):
        send_ref[group * 4 : group * 4 + 4, 0:MOST, :] = rows.reshape(4, MOST, D)
        spot = iota((ROWS, 256), 1) + group * 256
        keys = jnp.sum(
            jnp.where(spot == pos0, key, 0) + jnp.where(spot == pos1, key + TOKENS, 0),
            axis=0,
            keepdims=True,
        )
        low = jnp.bitwise_and(keys, 255)
        mid = jnp.bitwise_and(jnp.right_shift(keys, 8), 255)
        high = jnp.right_shift(keys, 16)
        digits = jnp.where(
            digit == 0, low, jnp.where(digit == 1, mid, jnp.where(digit == 2, high, 0))
        ).astype(f32)
        for j in range(4):
            send_ref[group * 4 + j, MOST : MOST + EXTRA, :] = zeros
            send_ref[group * 4 + j, MOST : MOST + EXTRA, 0:MOST] = digits[
                :, j * MOST : (j + 1) * MOST
            ].astype(bf16)

    pick_rows(csel_ref, cot_ref[...], store)


def stacked(pair):
    lanes = iota(pair.shape, 1)
    zero = jnp.zeros_like(pair)
    return jnp.concatenate(
        [jnp.where(lanes < HDIM, pair, zero), jnp.where(lanes >= HDIM, pair, zero)], axis=0
    )


def band_bias(cols_ref, seg_ref, block):
    start = STARTS[block]
    same = (
        cols_ref[block * 128 : block * 128 + 128, 3:4]
        == seg_ref[:, start : start + 256].astype(f32)
    )
    bias = jnp.where(same, 0.0, -1e30)
    return jnp.concatenate([bias, bias], axis=0)


def attend_kernel(
    tokens_ref,
    seg_ref,
    cols_ref,
    csel_ref,
    gain1_ref,
    bias1_ref,
    w_qkv_ref,
    w_out_ref,
    gain2_ref,
    bias2_ref,
    packed_ref,
    attended_ref,
    lse_ref,
    residual_ref,
    send_ref,
):
    inputs = tokens_ref[...].astype(f32)
    normal, _ = normalize(inputs)
    first = (normal * gain1_ref[...] + bias1_ref[...]).astype(bf16)
    for part in range(3):
        packed_ref[:, part * D : (part + 1) * D] = dot(
            first, w_qkv_ref[:, part * D : (part + 1) * D]
        ).astype(bf16)
    lanes = iota((128, 128), 1)
    for block in range(4):
        here = slice(block * 128, block * 128 + 128)
        window = slice(STARTS[block], STARTS[block] + 256)
        bias = band_bias(cols_ref, seg_ref, block)
        lse = jnp.zeros((128, 128), f32)
        for pair in range(4):
            at = pair * 128
            query = stacked(packed_ref[here, at : at + 128])
            scores = dot_nt(query, packed_ref[window, D + at : D + at + 128]) * SCALE + bias
            highest = jnp.max(scores, axis=-1, keepdims=True)
            raised = jnp.exp(scores - highest)
            total = jnp.sum(raised, axis=-1, keepdims=True)
            weights = (raised * (1.0 / total)).astype(bf16)
            mixed = dot(weights, packed_ref[window, 2 * D + at : 2 * D + at + 128])
            attended_ref[here, at : at + 128] = jnp.where(
                lanes < HDIM, mixed[0:128], mixed[128:256]
            ).astype(bf16)
            logsum = highest + jnp.log(total)
            lse = jnp.where(lanes == 2 * pair, logsum[0:128], lse)
            lse = jnp.where(lanes == 2 * pair + 1, logsum[128:256], lse)
        lse_ref[here, :] = lse
    residual = inputs + dot(attended_ref[...], w_out_ref[...])
    residual_ref[...] = residual
    normal2, _ = normalize(residual)
    second = (normal2 * gain2_ref[...] + bias2_ref[...]).astype(bf16)

    def store(group, rows):
        send_ref[group * 4 : group * 4 + 4] = rows.reshape(4, MOST, D)

    pick_rows(csel_ref, second, store)


def keep_kernel(all_ref, own_ref, kept_ref):
    empty = 2 * TOKENS + 1
    keys = all_ref[...]
    keys = jnp.where(keys == 0, empty, keys)

    def step(_, bounds):
        low, high = bounds
        middle = jnp.right_shift(low + high, 1)
        enough = jnp.sum((keys <= middle).astype(jnp.int32), keepdims=True) >= CAP
        return jnp.where(enough, low, middle + 1), jnp.where(enough, middle, high)

    low = jnp.zeros((1, 1), jnp.int32)
    high = jnp.full((1, 1), 2 * TOKENS, jnp.int32)
    low, high = lax.fori_loop(0, 18, step, (low, high))
    own = own_ref[...]
    kept_ref[...] = jnp.logical_and(own > 0, own <= high).astype(f32)


def back_kernel(grad_ref, w2_ref, out_ref):
    rows = grad_ref[...].reshape(256, D)
    for part in range(4):
        out_ref[:, part * 512 : part * 512 + 512] = dot_nt(rows, w2_ref[part]).astype(bf16)


def slot_kernel(
    expert_ref,
    x_ref,
    gw_ref,
    w1_ref,
    kept_ref,
    w_router_ref,
    dslot_ref,
    act_ref,
    dpre_ref,
    scale_ref,
    d_router_ref,
):
    rows = x_ref[...].reshape(256, D)
    logits = dot(rows, w_router_ref[...])
    raised = jnp.exp(logits - jnp.max(logits, axis=-1, keepdims=True))
    prob = raised / jnp.sum(raised, axis=-1, keepdims=True)
    mine = iota((256, EXPERTS), 1) == expert_ref[0]
    gate = jnp.sum(jnp.where(mine, prob, 0.0), axis=-1, keepdims=True)
    kept = kept_ref[...]
    scale = kept * gate
    scale_ref[...] = scale
    dslot = jnp.zeros((256, D), f32)
    dgate = jnp.zeros((256, 1), f32)
    for part in range(4):
        span = slice(part * 512, part * 512 + 512)
        weight = w1_ref[part]
        pre = dot(rows, weight)
        square = pre * pre
        bend = jnp.tanh(GELU_C * pre * (1.0 + GELU_A * square))
        half = 0.5 * (1.0 + bend)
        act = pre * half
        slope = half + 0.5 * pre * (1.0 - bend * bend) * (
            GELU_C + (3.0 * GELU_A * GELU_C) * square
        )
        upstream = gw_ref[:, span].astype(f32)
        dgate = dgate + jnp.sum(upstream * act, axis=-1, keepdims=True)
        dpre = (upstream * scale * slope).astype(bf16)
        act_ref[:, span] = act.astype(bf16)
        dpre_ref[:, span] = dpre
        dslot = dslot + dot_nt(dpre, weight)
    dlogit = (kept * dgate * gate * (mine.astype(f32) - prob)).astype(bf16)
    dslot = dslot + dot_nt(dlogit, w_router_ref[...])
    dslot_ref[...] = dslot.astype(bf16).reshape(4, MOST, D)

    @pl.when(pl.program_id(0) == 0)
    def _():
        d_router_ref[...] = jnp.zeros_like(d_router_ref)

    d_router_ref[...] += dot_tn(dlogit, rows)


def out_kernel(act_ref, w2_ref, scale_ref, y_ref):
    total = jnp.zeros((256, D), f32)
    for part in range(4):
        total = total + dot(act_ref[:, part * 512 : part * 512 + 512], w2_ref[part])
    y_ref[...] = (total * scale_ref[...]).astype(bf16).reshape(4, MOST, D)


def weight_kernel(x_ref, grad_ref, scale_ref, act_ref, dpre_ref, out_ref):
    rows = x_ref[...].reshape(SLOTS, D)
    out_ref[0, 0] = dot_tn(rows, dpre_ref[...]).astype(bf16)
    upstream = (grad_ref[...].reshape(SLOTS, D).astype(f32) * scale_ref[...]).astype(bf16)
    out_ref[0, 1] = dot_tn(act_ref[...], upstream).astype(bf16)


def gather_slots(cols_ref, rows_ref):
    pos0 = cols_ref[:, 0:1].astype(jnp.int32)
    pos1 = cols_ref[:, 1:2].astype(jnp.int32)
    total = jnp.zeros((ROWS, D), f32)
    for part in range(4):
        spot = iota((ROWS, 512), 1) + part * 512
        hot = jnp.logical_or(spot == pos0, spot == pos1).astype(f32).astype(bf16)
        total = total + dot(hot, rows_ref[part * 8 : part * 8 + 8].reshape(512, D))
    return total


def backward_kernel(
    dslot_ref,
    cols_ref,
    seg_ref,
    tokens_ref,
    cot_ref,
    residual_ref,
    packed_ref,
    attended_ref,
    lse_ref,
    gain1_ref,
    bias1_ref,
    w_qkv_ref,
    w_out_ref,
    gain2_ref,
    d_router_ref,
    grads_ref,
    d_tokens_ref,
    datt_ref,
    dpacked_ref,
    dkey_ref,
    dvalue_ref,
):
    d_second = gather_slots(cols_ref, dslot_ref)
    normal2, factor2 = normalize(residual_ref[...])
    d_norm2, d_gain2, d_shift2 = norm_backward(d_second, normal2, factor2, gain2_ref[...])
    d_residual = cot_ref[...].astype(f32) + d_norm2
    d_tokens_ref[...] = d_residual
    d_branch = d_residual.astype(bf16)
    grads_ref[3 * D : 4 * D, :] = dot_tn(attended_ref[...], d_branch).astype(bf16)
    datt_ref[...] = dot_nt(d_branch, w_out_ref[...]).astype(bf16)
    lanes = iota((128, 128), 1)
    for pair in range(4):
        at = pair * 128
        dkey_ref[...] = jnp.zeros_like(dkey_ref)
        dvalue_ref[...] = jnp.zeros_like(dvalue_ref)
        for block in range(4):
            here = slice(block * 128, block * 128 + 128)
            window = slice(STARTS[block], STARTS[block] + 256)
            bias = band_bias(cols_ref, seg_ref, block)
            query = stacked(packed_ref[here, at : at + 128])
            upstream = stacked(datt_ref[here, at : at + 128])
            keys = packed_ref[window, D + at : D + at + 128]
            values = packed_ref[window, 2 * D + at : 2 * D + at + 128]
            logsum = jnp.concatenate(
                [
                    lse_ref[here, 2 * pair : 2 * pair + 1],
                    lse_ref[here, 2 * pair + 1 : 2 * pair + 2],
                ],
                axis=0,
            )
            weights = jnp.exp(dot_nt(query, keys) * SCALE + bias - logsum)
            d_weights = dot_nt(upstream, values)
            inner = jnp.sum(weights * d_weights, axis=-1, keepdims=True)
            d_scores = (weights * (d_weights - inner)).astype(bf16)
            d_query = dot(d_scores, keys) * SCALE
            dpacked_ref[here, at : at + 128] = jnp.where(
                lanes < HDIM, d_query[0:128], d_query[128:256]
            ).astype(bf16)
            dkey_ref[window, :] += dot_tn(d_scores, query)
            dvalue_ref[window, :] += dot_tn(weights.astype(bf16), upstream)
        dpacked_ref[:, D + at : D + at + 128] = (dkey_ref[...] * SCALE).astype(bf16)
        dpacked_ref[:, 2 * D + at : 2 * D + at + 128] = dvalue_ref[...].astype(bf16)
    normal1, factor1 = normalize(tokens_ref[...].astype(f32))
    first = (normal1 * gain1_ref[...] + bias1_ref[...]).astype(bf16)
    for part in range(3):
        grads_ref[part * D : (part + 1) * D, :] = dot_tn(
            first, dpacked_ref[:, part * D : (part + 1) * D]
        ).astype(bf16)
    d_first = dot_nt(dpacked_ref[...], w_qkv_ref[...])
    d_norm1, d_gain1, d_shift1 = norm_backward(d_first, normal1, factor1, gain1_ref[...])
    d_tokens_ref[...] += d_norm1
    grads_ref[4 * D :, :] = jnp.zeros((grads_ref.shape[0] - 4 * D, D), bf16)
    row = iota((16, D), 0)
    small = jnp.where(
        row == 0,
        d_gain1,
        jnp.where(
            row == 1, d_shift1, jnp.where(row == 2, d_gain2, jnp.where(row == 3, d_shift2, 0.0))
        ),
    )
    grads_ref[4 * D : 4 * D + 16, :] = small.astype(bf16)
    grads_ref[4 * D + 16 : 4 * D + 16 + EXPERTS, :] = d_router_ref[...].astype(bf16)


def output_kernel(y_ref, cols_ref, residual_ref, out_ref):
    out_ref[...] = (residual_ref[...] + gather_slots(cols_ref, y_ref)).astype(bf16)


def params():
    return pltpu.CompilerParams(vmem_limit_bytes=VMEM_LIMIT)


def call(kernel, out_shape, *args, flops=0, scratch=()):
    shapes = jax.tree.leaves(out_shape)
    moved = sum(a.size * a.dtype.itemsize for a in args) + sum(
        s.size * s.dtype.itemsize for s in shapes
    )
    return pl.pallas_call(
        kernel,
        out_shape=out_shape,
        scratch_shapes=list(scratch),
        compiler_params=params(),
        cost_estimate=pl.CostEstimate(flops=flops, bytes_accessed=moved, transcendentals=0),
    )(*args)


def shape(dims, dtype):
    return jax.ShapeDtypeStruct(dims, dtype)


def shift(axis, distance):
    pairs = []
    for x in range(4):
        for y in range(4):
            for core in range(2):
                to = {
                    "x": ((x + distance) % 4, y, core),
                    "y": (x, (y + distance) % 4, core),
                    "core": (x, y, (core + distance) % 2),
                }[axis]
                pairs.append(((x * 4 + y) * 2 + core, (to[0] * 4 + to[1]) * 2 + to[2]))
    return pairs


def sum_everywhere(grads):
    index = lax.axis_index("dp")
    core, y, x = index % 2, (index // 2) % 4, index // 8
    half = grads.shape[0] // 2

    def piece(values, which, size):
        return lax.dynamic_slice_in_dim(values, which * size, size, axis=0)

    got = lax.ppermute(piece(grads, 1 - core, half), "dp", shift("core", 1))
    total = piece(grads, core, half).astype(f32) + got.astype(f32)
    for axis, where in (("x", x), ("y", y)):
        size = total.shape[0] // 4
        low = total.astype(bf16)
        got = [
            lax.ppermute(piece(low, (where + d) % 4, size), "dp", shift(axis, d))
            for d in (1, 2, 3)
        ]
        total = piece(total, where, size)
        for part in got:
            total = total + part.astype(f32)
    low = total.astype(bf16)
    got = [
        lax.ppermute(low, "expert", [(i, (i + d) % 4) for i in range(4)]).astype(f32)
        for d in (1, 2, 3)
    ]
    low = ((low.astype(f32) + got[1]) + (got[0] + got[2])).astype(bf16)
    for axis, where in (("y", y), ("x", x)):
        size = low.shape[0]
        whole = jnp.zeros((4 * size, D), bf16)
        whole = lax.dynamic_update_slice_in_dim(whole, low, where * size, axis=0)
        for d in (1, 2, 3):
            part = lax.ppermute(low, "dp", shift(axis, d))
            whole = lax.dynamic_update_slice_in_dim(
                whole, part, ((where - d) % 4) * size, axis=0
            )
        low = whole
    other = lax.ppermute(low, "dp", shift("core", 1))
    return jnp.where(
        core == 0,
        jnp.concatenate([low, other], axis=0),
        jnp.concatenate([other, low], axis=0),
    )


def per_device(
    tokens,
    segments,
    routes,
    priority,
    ln1_gain,
    ln1_bias,
    w_qkv,
    w_out,
    ln2_gain,
    ln2_bias,
    w_router,
    expert_in,
    expert_out,
    cotangent,
):
    gain1, bias1 = ln1_gain.reshape(1, D), ln1_bias.reshape(1, D)
    gain2, bias2 = ln2_gain.reshape(1, D), ln2_bias.reshape(1, D)
    w2 = lax.all_gather(expert_out[0], "expert", axis=0)
    w1 = lax.all_gather(expert_in[0], "expert", axis=0)

    send_grad, csel, cols = call(
        pack_kernel,
        (
            shape((EXPERTS, MOST + EXTRA, D), bf16),
            shape((EXPERTS, ROWS), f32),
            shape((ROWS, 128), f32),
        ),
        routes.T,
        priority.reshape(1, ROWS),
        segments,
        cotangent,
        flops=2 * SLOTS * D * D,
        scratch=[pltpu.VMEM((128, ROWS), f32)],
    )
    grad = lax.all_to_all(send_grad, "dp", split_axis=0, concat_axis=0, tiled=True)

    packed, attended, lse, residual, send_rows = call(
        attend_kernel,
        (
            shape((ROWS, 3 * D), bf16),
            shape((ROWS, D), bf16),
            shape((ROWS, 128), f32),
            shape((ROWS, D), f32),
            shape((EXPERTS, MOST, D), bf16),
        ),
        tokens,
        segments,
        cols,
        csel,
        gain1,
        bias1,
        w_qkv,
        w_out,
        gain2,
        bias2,
        flops=2 * SLOTS * D * D + 10 * ROWS * D * D,
    )
    rows = lax.all_to_all(send_rows, "dp", split_axis=0, concat_axis=0, tiled=True)

    digits = grad[:, MOST : MOST + 3, 0:MOST].astype(jnp.int32)
    keys = digits[:, 0] + 256 * digits[:, 1] + 65536 * digits[:, 2]
    all_keys = lax.all_gather(keys, "expert", axis=0, tiled=True)
    kept = call(
        keep_kernel,
        shape((N_DP // 2, 128), f32),
        all_keys.reshape(N_Z * N_DP // 2, 128),
        keys.reshape(N_DP // 2, 128),
    ).reshape(SLOTS, 1)

    steps = SLOTS // 256
    any_spec = pl.BlockSpec((4, D, 512), lambda i: (0, 0, 0))
    row_spec = pl.BlockSpec((4, MOST, D), lambda i: (i, 0, 0))
    wide_spec = pl.BlockSpec((256, 2048), lambda i: (i, 0))
    col_spec = pl.BlockSpec((256, 1), lambda i: (i, 0))
    big = 2 * SLOTS * D * 2048
    back = pl.pallas_call(
        back_kernel,
        grid=(steps,),
        in_specs=[row_spec, any_spec],
        out_specs=wide_spec,
        out_shape=shape((SLOTS, 2048), bf16),
        compiler_params=params(),
        cost_estimate=pl.CostEstimate(flops=big, bytes_accessed=12 << 20, transcendentals=0),
    )(grad, w2)
    expert = lax.axis_index("dp").astype(jnp.int32).reshape(1)
    dslot, act, dpre, scale, d_router = pl.pallas_call(
        slot_kernel,
        grid=(steps,),
        in_specs=[
            pl.BlockSpec(memory_space=pltpu.SMEM),
            row_spec,
            wide_spec,
            any_spec,
            col_spec,
            pl.BlockSpec((D, EXPERTS), lambda i: (0, 0)),
        ],
        out_specs=[
            row_spec,
            wide_spec,
            wide_spec,
            col_spec,
            pl.BlockSpec((EXPERTS, D), lambda i: (0, 0)),
        ],
        out_shape=(
            shape((EXPERTS, MOST, D), bf16),
            shape((SLOTS, 2048), bf16),
            shape((SLOTS, 2048), bf16),
            shape((SLOTS, 1), f32),
            shape((EXPERTS, D), f32),
        ),
        compiler_params=params(),
        cost_estimate=pl.CostEstimate(
            flops=2 * big, bytes_accessed=32 << 20, transcendentals=SLOTS * 2048
        ),
    )(expert, rows, back, w1, kept, w_router)
    dslot_home = lax.all_to_all(dslot, "dp", split_axis=0, concat_axis=0, tiled=True)

    y = pl.pallas_call(
        out_kernel,
        grid=(steps,),
        in_specs=[wide_spec, any_spec, col_spec],
        out_specs=row_spec,
        out_shape=shape((EXPERTS, MOST, D), bf16),
        compiler_params=params(),
        cost_estimate=pl.CostEstimate(flops=big, bytes_accessed=12 << 20, transcendentals=0),
    )(act, w2, scale)
    y_home = lax.all_to_all(y, "dp", split_axis=0, concat_axis=0, tiled=True)

    d_weights = pl.pallas_call(
        weight_kernel,
        grid=(N_Z,),
        in_specs=[
            pl.BlockSpec((EXPERTS, MOST, D), lambda i: (0, 0, 0)),
            pl.BlockSpec((EXPERTS, MOST, D), lambda i: (0, 0, 0)),
            pl.BlockSpec((SLOTS, 1), lambda i: (0, 0)),
            pl.BlockSpec((SLOTS, 512), lambda i: (0, i)),
            pl.BlockSpec((SLOTS, 512), lambda i: (0, i)),
        ],
        out_specs=pl.BlockSpec((1, 2, D, 512), lambda i: (i, 0, 0, 0)),
        out_shape=shape((N_Z, 2, D, 512), bf16),
        compiler_params=params(),
        cost_estimate=pl.CostEstimate(flops=2 * big, bytes_accessed=24 << 20, transcendentals=0),
    )(rows, grad, scale, act, dpre)
    d_own = lax.psum_scatter(d_weights, "expert", scatter_dimension=0, tiled=True)

    grads, d_tokens = call(
        backward_kernel,
        (shape((2304, D), bf16), shape((ROWS, D), f32)),
        dslot_home,
        cols,
        segments,
        tokens,
        cotangent,
        residual,
        packed,
        attended,
        lse,
        gain1,
        bias1,
        w_qkv,
        w_out,
        gain2,
        d_router,
        flops=2 * SLOTS * D * D + 20 * ROWS * D * D,
        scratch=[
            pltpu.VMEM((ROWS, D), bf16),
            pltpu.VMEM((ROWS, 3 * D), bf16),
            pltpu.VMEM((ROWS, 128), f32),
            pltpu.VMEM((ROWS, 128), f32),
        ],
    )
    output = call(
        output_kernel, shape((ROWS, D), bf16), y_home, cols, residual, flops=2 * SLOTS * D * D
    )
    summed = sum_everywhere(grads).astype(f32)
    d_w_qkv = jnp.concatenate([summed[0:D], summed[D : 2 * D], summed[2 * D : 3 * D]], axis=1)
    small = summed[4 * D :]
    d_own = d_own.astype(f32)
    return (
        output,
        d_tokens,
        small[0],
        small[1],
        d_w_qkv,
        summed[3 * D : 4 * D],
        small[2],
        small[3],
        small[16 : 16 + EXPERTS].T,
        d_own[:, 0],
        d_own[:, 1],
    )


def solution(mesh):
    both = P(("expert", "dp"), None)
    in_specs = (
        both,
        both,
        both,
        P(("expert", "dp")),
        P(),
        P(),
        P(),
        P(),
        P(),
        P(),
        P(),
        P("dp", None, "expert"),
        P("dp", "expert", None),
        both,
    )
    out_specs = (
        both,
        both,
        P(),
        P(),
        P(),
        P(),
        P(),
        P(),
        P(),
        P("dp", None, "expert"),
        P("dp", "expert", None),
    )
    return jax.shard_map(
        per_device, mesh=mesh, in_specs=in_specs, out_specs=out_specs, check_vma=False
    )
```

```python
import functools

import jax
import jax.numpy as jnp
from jax import lax
from jax.experimental import pallas as pl
from jax.experimental.pallas import tpu as pltpu
from jax.sharding import Mesh
from jax.sharding import PartitionSpec as P

D = 512
HEADS = 8
HDIM = 64
EXPERTS = 32
MOST = 64
ROWS = 512
SLOTS = EXPERTS * MOST
N_Z = 4
N_DP = 32
CAP = (21 * N_Z * N_DP * ROWS + 319) // 320
TOKENS = N_Z * N_DP * ROWS
EXTRA = 8
BLOCK = 512
WIDTH = 4 * D + 128
EPS = 1e-06
SCALE = HDIM ** (-0.5)
STARTS = (0, 64, 192, 256)
GELU_C = 0.7978845608028654
GELU_A = 0.044715

bf16 = jnp.bfloat16
f32 = jnp.float32
MIB = 1024 * 1024


def dot(a, b):
    return lax.dot_general(a, b, (((1,), (0,)), ((), ())), preferred_element_type=f32)


def dot_nt(a, b):
    return lax.dot_general(a, b, (((1,), (1,)), ((), ())), preferred_element_type=f32)


def dot_tn(a, b):
    return lax.dot_general(a, b, (((0,), (0,)), ((), ())), preferred_element_type=f32)


def iota(shape, dim):
    return lax.broadcasted_iota(jnp.int32, shape, dim)


def normalize(values):
    center = values - jnp.mean(values, axis=-1, keepdims=True)
    factor = lax.rsqrt(jnp.mean(center * center, axis=-1, keepdims=True) + EPS)
    return center * factor, factor


def norm_backward(upstream, normal, factor, gain):
    scaled = upstream * gain
    inner = (
        scaled
        - jnp.mean(scaled, axis=-1, keepdims=True)
        - normal * jnp.mean(scaled * normal, axis=-1, keepdims=True)
    )
    return (
        inner * factor,
        jnp.sum(upstream * normal, axis=0, keepdims=True),
        jnp.sum(upstream, axis=0, keepdims=True),
    )


def pick_rows(csel_ref, rows, store):
    place = iota((MOST, ROWS), 0).astype(f32)
    for group in range(EXPERTS // 4):
        parts = []
        for j in range(4):
            line = csel_ref[group * 4 + j : group * 4 + j + 1, :]
            parts.append((place == line).astype(f32).astype(bf16))
        hot = jnp.concatenate(parts, axis=0)
        store(group, dot(hot, rows).astype(bf16))


def pack_kernel(routes_ref, prio_ref, seg_ref, cot_ref, send_ref, csel_ref, cols_ref, wide_ref):
    routes = routes_ref[...]
    experts = iota((EXPERTS, ROWS), 0)
    first = routes[0:1] == experts
    second = routes[1:2] == experts
    either = jnp.logical_or(first, second)
    before = (iota((ROWS, ROWS), 0) < iota((ROWS, ROWS), 1)).astype(f32).astype(bf16)
    count = dot(either.astype(f32).astype(bf16), before)
    slot = count + (experts * MOST).astype(f32)
    wide_ref[...] = jnp.zeros_like(wide_ref)
    wide_ref[0:1, :] = jnp.sum(jnp.where(first, slot, 0.0), axis=0, keepdims=True)
    wide_ref[1:2, :] = jnp.sum(jnp.where(second, slot, 0.0), axis=0, keepdims=True)
    wide_ref[2:3, :] = prio_ref[...].astype(f32)
    wide_ref[3:4, :] = seg_ref[...].astype(f32)
    csel_ref[...] = jnp.where(either, count, -1.0)
    cols = wide_ref[...].T
    cols_ref[...] = cols
    cols_int = cols[:, 0:3].astype(jnp.int32)
    pos0, pos1, key = cols_int[:, 0:1], cols_int[:, 1:2], cols_int[:, 2:3] + 1
    zeros = jnp.zeros((EXTRA, D), bf16)
    digit = iota((EXTRA, 256), 0)

    def store(group, rows):
        send_ref[group * 4 : group * 4 + 4, 0:MOST, :] = rows.reshape(4, MOST, D)
        spot = iota((ROWS, 256), 1) + group * 256
        keys = jnp.sum(
            jnp.where(spot == pos0, key, 0) + jnp.where(spot == pos1, key + TOKENS, 0),
            axis=0,
            keepdims=True,
        )
        low = jnp.bitwise_and(keys, 255)
        mid = jnp.bitwise_and(jnp.right_shift(keys, 8), 255)
        high = jnp.right_shift(keys, 16)
        digits = jnp.where(
            digit == 0, low, jnp.where(digit == 1, mid, jnp.where(digit == 2, high, 0))
        ).astype(f32)
        for j in range(4):
            send_ref[group * 4 + j, MOST : MOST + EXTRA, :] = zeros
            send_ref[group * 4 + j, MOST : MOST + EXTRA, 0:MOST] = digits[
                :, j * MOST : (j + 1) * MOST
            ].astype(bf16)

    pick_rows(csel_ref, cot_ref[...], store)


def stacked(pair):
    lanes = iota(pair.shape, 1)
    zero = jnp.zeros_like(pair)
    return jnp.concatenate(
        [jnp.where(lanes < HDIM, pair, zero), jnp.where(lanes >= HDIM, pair, zero)], axis=0
    )


def band_bias(cols_ref, seg_ref, block):
    start = STARTS[block]
    same = (
        cols_ref[block * 128 : block * 128 + 128, 3:4]
        == seg_ref[:, start : start + 256].astype(f32)
    )
    bias = jnp.where(same, 0.0, -1e30)
    return jnp.concatenate([bias, bias], axis=0)


def attend_kernel(
    tokens_ref,
    seg_ref,
    cols_ref,
    csel_ref,
    gain1_ref,
    bias1_ref,
    w_qkv_ref,
    w_out_ref,
    gain2_ref,
    bias2_ref,
    packed_ref,
    attended_ref,
    lse_ref,
    residual_ref,
    send_ref,
):
    inputs = tokens_ref[...].astype(f32)
    normal, _ = normalize(inputs)
    first = (normal * gain1_ref[...] + bias1_ref[...]).astype(bf16)
    for part in range(3):
        packed_ref[:, part * D : (part + 1) * D] = dot(
            first, w_qkv_ref[:, part * D : (part + 1) * D]
        ).astype(bf16)
    lanes = iota((128, 128), 1)
    for block in range(4):
        here = slice(block * 128, block * 128 + 128)
        window = slice(STARTS[block], STARTS[block] + 256)
        bias = band_bias(cols_ref, seg_ref, block)
        lse = jnp.zeros((128, 128), f32)
        for pair in range(4):
            at = pair * 128
            query = stacked(packed_ref[here, at : at + 128])
            scores = dot_nt(query, packed_ref[window, D + at : D + at + 128]) * SCALE + bias
            highest = jnp.max(scores, axis=-1, keepdims=True)
            raised = jnp.exp(scores - highest)
            total = jnp.sum(raised, axis=-1, keepdims=True)
            weights = (raised * (1.0 / total)).astype(bf16)
            mixed = dot(weights, packed_ref[window, 2 * D + at : 2 * D + at + 128])
            attended_ref[here, at : at + 128] = jnp.where(
                lanes < HDIM, mixed[0:128], mixed[128:256]
            ).astype(bf16)
            logsum = highest + jnp.log(total)
            lse = jnp.where(lanes == 2 * pair, logsum[0:128], lse)
            lse = jnp.where(lanes == 2 * pair + 1, logsum[128:256], lse)
        lse_ref[here, :] = lse
    residual = inputs + dot(attended_ref[...], w_out_ref[...])
    residual_ref[...] = residual
    normal2, _ = normalize(residual)
    second = (normal2 * gain2_ref[...] + bias2_ref[...]).astype(bf16)

    def store(group, rows):
        send_ref[group * 4 : group * 4 + 4] = rows.reshape(4, MOST, D)

    pick_rows(csel_ref, second, store)


def keep_kernel(own_ref, a_ref, b_ref, c_ref, d_ref, kept_ref):
    empty = 2 * TOKENS + 1
    keys = jnp.concatenate([a_ref[...], b_ref[...], c_ref[...], d_ref[...]], axis=0)
    keys = jnp.where(keys == 0, empty, keys)

    def step(_, bounds):
        low, high = bounds
        middle = jnp.right_shift(low + high, 1)
        enough = jnp.sum((keys <= middle).astype(jnp.int32), keepdims=True) >= CAP
        return jnp.where(enough, low, middle + 1), jnp.where(enough, middle, high)

    low = jnp.zeros((1, 1), jnp.int32)
    high = jnp.full((1, 1), 2 * TOKENS, jnp.int32)
    low, high = lax.fori_loop(0, 18, step, (low, high))
    own = own_ref[...]
    kept_ref[...] = jnp.logical_and(own > 0, own <= high).astype(f32)


def back_kernel(grad_ref, *refs):
    *w2_refs, out_ref = refs
    rows = grad_ref[...].reshape(BLOCK, D)
    for part, w2_ref in enumerate(w2_refs):
        out_ref[:, part * 512 : part * 512 + 512] = dot_nt(rows, w2_ref[...]).astype(bf16)


def slot_kernel(
    expert_ref,
    x_ref,
    gw_ref,
    w1a_ref,
    w1b_ref,
    w1c_ref,
    w1d_ref,
    kept_ref,
    w_router_ref,
    dslot_ref,
    act_ref,
    dpre_ref,
    scale_ref,
    dprob_ref,
):
    rows = x_ref[...].reshape(BLOCK, D)
    w_router = w_router_ref[...]
    logits = dot_nt(w_router, rows)
    raised = jnp.exp(logits - jnp.max(logits, axis=0, keepdims=True))
    prob = raised / jnp.sum(raised, axis=0, keepdims=True)
    mine = iota((EXPERTS, BLOCK), 0) == expert_ref[0]
    scale = kept_ref[...] * jnp.sum(jnp.where(mine, prob, 0.0), axis=0, keepdims=True)
    scale_ref[...] = scale
    scale_col = jnp.broadcast_to(scale, (8, BLOCK)).T[:, 0:1]
    dslot = jnp.zeros((BLOCK, D), f32)
    dgate = jnp.zeros((BLOCK, 128), f32)
    parts = (w1a_ref, w1b_ref, w1c_ref, w1d_ref)
    tiles = [ref[:, at : at + 256] for ref in parts for at in (0, 256)]
    pre = dot(rows, tiles[0])
    held = None
    for step, weight in enumerate(tiles):
        following = dot(rows, tiles[step + 1]) if step + 1 < len(tiles) else None
        span = slice(step * 256, step * 256 + 256)
        square = pre * pre
        half = 0.5 * jnp.tanh(pre * (square * (GELU_A * GELU_C) + GELU_C)) + 0.5
        act = pre * half
        slope = half + act * (1.0 - half) * (square * (6.0 * GELU_A * GELU_C) + 2.0 * GELU_C)
        upstream = gw_ref[:, span].astype(f32)
        product = upstream * act
        dgate = dgate + product[:, 0:128] + product[:, 128:256]
        dpre = (upstream * slope).astype(bf16)
        act_ref[:, span] = act.astype(bf16)
        dpre_ref[:, span] = dpre
        if held is not None:
            dslot = dslot + dot_nt(*held)
        held = dpre, weight
        pre = following
    dslot = dslot + dot_nt(*held)
    dgate = jnp.sum(dgate.T, axis=0, keepdims=True)
    dprob = dgate * (mine.astype(f32) - prob)
    dprob_ref[...] = dprob.astype(bf16)
    dslot = dslot * scale_col + dot_tn((scale * dprob).astype(bf16), w_router)
    dslot_ref[...] = dslot.astype(bf16).reshape(BLOCK // MOST, MOST, D)


def weight_kernel(
    x_ref,
    grad_ref,
    scale_ref,
    act_ref,
    dpre_ref,
    dprob_ref,
    w2a_ref,
    w2b_ref,
    w2c_ref,
    w2d_ref,
    y_ref,
    rows_ref,
    back_ref,
    down_in_ref,
    down_out_ref,
    far_in_ref,
    far_out_ref,
    up_in_ref,
    up_out_ref,
    d_router_ref,
    w2_ref,
    total_ref,
):
    step = pl.program_id(0)

    @pl.when(step == 0)
    def _():
        for at in range(0, SLOTS, 512):
            one = slice(at // MOST, at // MOST + 8)
            here = slice(at, at + 512)
            scale = scale_ref[:, here]
            rows_ref[:, here] = (x_ref[one].reshape(512, D).astype(f32).T * scale).astype(bf16)
            back_ref[:, here] = (
                grad_ref[one, 0:MOST, :].reshape(512, D).astype(f32).T * scale
            ).astype(bf16)
        d_router_ref[...] = dot_nt(rows_ref[...], dprob_ref[...])
        for part, part_ref in enumerate((w2a_ref, w2b_ref, w2c_ref, w2d_ref)):
            w2_ref[part] = part_ref[...]
        total_ref[...] = jnp.zeros_like(total_ref)

    total_ref[...] += dot(act_ref[...], w2_ref[step])

    @pl.when(step > 0)
    def _():
        d_in = dot(rows_ref[...], dpre_ref[...]).astype(bf16)
        d_out = dot(back_ref[...], act_ref[...]).T.astype(bf16)
        for part, (in_ref, out_ref) in enumerate(
            ((down_in_ref, down_out_ref), (far_in_ref, far_out_ref), (up_in_ref, up_out_ref))
        ):

            @pl.when(step == part + 1)
            def _():
                in_ref[...] = d_in
                out_ref[...] = d_out

    @pl.when(step == N_Z - 1)
    def _():
        for at in range(0, SLOTS, 512):
            one = slice(at // MOST, at // MOST + 8)
            here = slice(at, at + 512)
            scale_col = jnp.broadcast_to(scale_ref[:, here], (8, 512)).T[:, 0:1]
            y_ref[one] = (total_ref[here, :] * scale_col).astype(bf16).reshape(8, MOST, D)


def gather_slots(cols_ref, rows_ref):
    pos0 = cols_ref[:, 0:1].astype(jnp.int32)
    pos1 = cols_ref[:, 1:2].astype(jnp.int32)
    total = jnp.zeros((ROWS, D), f32)
    for part in range(4):
        spot = iota((ROWS, 512), 1) + part * 512
        hot = jnp.logical_or(spot == pos0, spot == pos1).astype(f32).astype(bf16)
        total = total + dot(hot, rows_ref[part * 8 : part * 8 + 8].reshape(512, D))
    return total


def backward_kernel(
    dslot_ref,
    cols_ref,
    seg_ref,
    tokens_ref,
    cot_ref,
    residual_ref,
    packed_ref,
    attended_ref,
    lse_ref,
    gain1_ref,
    bias1_ref,
    w_qkv_ref,
    w_out_ref,
    gain2_ref,
    d_router_ref,
    core_ref,
    keep_ref,
    send_ref,
    d_tokens_ref,
    datt_ref,
    dpacked_ref,
    dkey_ref,
    dvalue_ref,
    grads_ref,
    wide_ref,
):
    d_second = gather_slots(cols_ref, dslot_ref)
    normal2, factor2 = normalize(residual_ref[...])
    d_norm2, d_gain2, d_shift2 = norm_backward(d_second, normal2, factor2, gain2_ref[...])
    d_residual = cot_ref[...].astype(f32) + d_norm2
    d_tokens_ref[...] = d_residual
    d_branch = d_residual.astype(bf16)
    grads_ref[:, 3 * D : 4 * D] = dot_tn(attended_ref[...], d_branch).astype(bf16)
    datt_ref[...] = dot_nt(d_branch, w_out_ref[...]).astype(bf16)
    lanes = iota((128, 128), 1)
    for pair in range(4):
        at = pair * 128
        dkey_ref[...] = jnp.zeros_like(dkey_ref)
        dvalue_ref[...] = jnp.zeros_like(dvalue_ref)
        for block in range(4):
            here = slice(block * 128, block * 128 + 128)
            window = slice(STARTS[block], STARTS[block] + 256)
            bias = band_bias(cols_ref, seg_ref, block)
            query = stacked(packed_ref[here, at : at + 128])
            upstream = stacked(datt_ref[here, at : at + 128])
            keys = packed_ref[window, D + at : D + at + 128]
            values = packed_ref[window, 2 * D + at : 2 * D + at + 128]
            logsum = jnp.concatenate(
                [
                    lse_ref[here, 2 * pair : 2 * pair + 1],
                    lse_ref[here, 2 * pair + 1 : 2 * pair + 2],
                ],
                axis=0,
            )
            weights = jnp.exp(dot_nt(query, keys) * SCALE + bias - logsum)
            d_weights = dot_nt(upstream, values)
            inner = jnp.sum(weights * d_weights, axis=-1, keepdims=True)
            d_scores = (weights * (d_weights - inner)).astype(bf16)
            d_query = dot(d_scores, keys) * SCALE
            dpacked_ref[here, at : at + 128] = jnp.where(
                lanes < HDIM, d_query[0:128], d_query[128:256]
            ).astype(bf16)
            dkey_ref[window, :] += dot_tn(d_scores, query)
            dvalue_ref[window, :] += dot_tn(weights.astype(bf16), upstream)
        dpacked_ref[:, D + at : D + at + 128] = (dkey_ref[...] * SCALE).astype(bf16)
        dpacked_ref[:, 2 * D + at : 2 * D + at + 128] = dvalue_ref[...].astype(bf16)
    normal1, factor1 = normalize(tokens_ref[...].astype(f32))
    first = (normal1 * gain1_ref[...] + bias1_ref[...]).astype(bf16)
    for part in range(3):
        grads_ref[:, part * D : (part + 1) * D] = dot_tn(
            first, dpacked_ref[:, part * D : (part + 1) * D]
        ).astype(bf16)
    d_first = dot_nt(dpacked_ref[...], w_qkv_ref[...])
    d_norm1, d_gain1, d_shift1 = norm_backward(d_first, normal1, factor1, gain1_ref[...])
    d_tokens_ref[...] += d_norm1
    wide_ref[...] = jnp.zeros_like(wide_ref)
    wide_ref[0:1, :] = d_gain1
    wide_ref[1:2, :] = d_shift1
    wide_ref[2:3, :] = d_gain2
    wide_ref[3:4, :] = d_shift2
    grads_ref[:, 4 * D :] = wide_ref[...].T.astype(bf16)
    grads_ref[:, 4 * D + EXPERTS : 4 * D + 2 * EXPERTS] = d_router_ref[...].astype(bf16)
    core = core_ref[0]
    keep_ref[...] = grads_ref[pl.ds(pl.multiple_of(core * 256, 256), 256), :]
    send_ref[...] = grads_ref[pl.ds(pl.multiple_of((1 - core) * 256, 256), 256), :]


def finish_kernel(
    low_ref,
    other_ref,
    core_ref,
    qkv_ref,
    out_ref,
    router_ref,
    gain1_ref,
    shift1_ref,
    gain2_ref,
    shift2_ref,
    wide_ref,
):
    core = core_ref[0]
    for mine, half_ref in ((core, low_ref), (1 - core, other_ref)):
        here = pl.ds(pl.multiple_of(mine * 256, 256), 256)
        qkv_ref[here, :] = half_ref[:, 0 : 3 * D].astype(f32)
        out_ref[here, :] = half_ref[:, 3 * D : 4 * D].astype(f32)
        wide_ref[here, :] = half_ref[:, 4 * D :].astype(f32)
    lines = wide_ref[...].T
    router_ref[...] = lines[EXPERTS : 2 * EXPERTS]
    for row, out in enumerate((gain1_ref, shift1_ref, gain2_ref, shift2_ref)):
        out[...] = lines[row : row + 1]


def output_kernel(y_ref, cols_ref, residual_ref, out_ref):
    out_ref[...] = (residual_ref[...] + gather_slots(cols_ref, y_ref)).astype(bf16)


def own_kernel(
    rows_ref,
    back_ref,
    act_ref,
    dpre_ref,
    below_in_ref,
    above_in_ref,
    below_out_ref,
    above_out_ref,
    d_in_ref,
    d_out_ref,
):
    d_in = below_in_ref[...].astype(f32) + above_in_ref[...].astype(f32)
    d_in_ref[0] = d_in + dot(rows_ref[...], dpre_ref[...])
    d_out = below_out_ref[...].astype(f32) + above_out_ref[...].astype(f32)
    d_out_ref[0] = d_out + dot(back_ref[...], act_ref[...]).T


def params(mib):
    return pltpu.CompilerParams(vmem_limit_bytes=mib * MIB)


def after(values, *tokens):
    anywhere = pl.BlockSpec(memory_space=pl.ANY)
    return pl.pallas_call(
        lambda *refs: None,
        in_specs=[anywhere] * (1 + len(tokens)),
        out_specs=anywhere,
        out_shape=shape(values.shape, values.dtype),
        input_output_aliases={0: 0},
        cost_estimate=pl.CostEstimate(flops=0, bytes_accessed=0, transcendentals=0),
    )(values, *tokens)


def call(kernel, mib, out_shape, *args, flops=0, scratch=()):
    shapes = jax.tree.leaves(out_shape)
    moved = sum(a.size * a.dtype.itemsize for a in args) + sum(
        s.size * s.dtype.itemsize for s in shapes
    )
    return pl.pallas_call(
        kernel,
        out_shape=out_shape,
        scratch_shapes=list(scratch),
        compiler_params=params(mib),
        cost_estimate=pl.CostEstimate(flops=flops, bytes_accessed=moved, transcendentals=0),
    )(*args)


def shape(dims, dtype):
    return jax.ShapeDtypeStruct(dims, dtype)


DP = ("x", "y", "core")
CHIPS = ("z", "x", "y")
SWAP = [(0, 1), (1, 0)]


def ring(distance):
    return [(i, (i + distance) % 4) for i in range(4)]


def exchange(values, axes):
    return lax.all_to_all(values, axes, split_axis=0, concat_axis=0, tiled=True)


def sum_everywhere(keep, send, early, late):
    got = lax.ppermute(send, "core", SWAP)
    low = (after(keep, early).astype(f32) + got.astype(f32)).astype(bf16)
    parts = exchange(low.reshape(64, 4, WIDTH), CHIPS)
    low = after(jnp.sum(parts.astype(f32), axis=0).astype(bf16), *late)
    low = exchange(jnp.broadcast_to(low[None], (64, 4, WIDTH)), CHIPS).reshape(256, WIDTH)
    return low, lax.ppermute(low, "core", SWAP)


def per_device(
    tokens,
    segments,
    routes,
    priority,
    ln1_gain,
    ln1_bias,
    w_qkv,
    w_out,
    ln2_gain,
    ln2_bias,
    w_router,
    expert_in,
    expert_out,
    cotangent,
):
    gain1, bias1 = ln1_gain.reshape(1, D), ln1_bias.reshape(1, D)
    gain2, bias2 = ln2_gain.reshape(1, D), ln2_bias.reshape(1, D)
    w2_up = lax.ppermute(expert_out[0], "z", ring(1))
    w2_down = lax.ppermute(expert_out[0], "z", ring(3))
    w2_far = lax.ppermute(w2_down, "z", ring(3))
    w2 = [expert_out[0], w2_up, w2_far, w2_down]
    w1_up = lax.ppermute(expert_in[0], "z", ring(1))

    send_grad, csel, cols = call(
        pack_kernel,
        56,
        (
            shape((EXPERTS, MOST + EXTRA, D), bf16),
            shape((EXPERTS, ROWS), f32),
            shape((ROWS, 128), f32),
        ),
        routes.T,
        priority.reshape(1, ROWS),
        segments,
        cotangent,
        flops=2 * SLOTS * D * D,
        scratch=[pltpu.VMEM((128, ROWS), f32)],
    )
    grad = exchange(send_grad, DP)

    packed, attended, lse, residual, send_rows = call(
        attend_kernel,
        56,
        (
            shape((ROWS, 3 * D), bf16),
            shape((ROWS, D), bf16),
            shape((ROWS, 128), f32),
            shape((ROWS, D), f32),
            shape((EXPERTS, MOST, D), bf16),
        ),
        tokens,
        segments,
        cols,
        csel,
        gain1,
        bias1,
        w_qkv,
        w_out,
        gain2,
        bias2,
        flops=2 * SLOTS * D * D + 10 * ROWS * D * D,
    )
    send_rows = after(send_rows, w2_up, w2_far, w2_down, w1_up)
    rows = exchange(send_rows, DP)

    digits = grad[:, MOST : MOST + 3, 0:MOST].astype(jnp.int32)
    keys = (digits[:, 0] + 256 * digits[:, 1] + 65536 * digits[:, 2]).reshape(16, 128)
    planes = [lax.ppermute(keys, "z", ring(d)) for d in (1, 2, 3)]
    kept = call(keep_kernel, 56, shape((16, 128), f32), keys, keys, *planes).reshape(1, SLOTS)

    steps = SLOTS // BLOCK
    weight_spec = pl.BlockSpec((D, 512), lambda i: (0, 0))
    row_spec = pl.BlockSpec((BLOCK // MOST, MOST, D), lambda i: (i, 0, 0))
    wide_spec = pl.BlockSpec((BLOCK, 2048), lambda i: (i, 0))
    line_spec = pl.BlockSpec((1, BLOCK), lambda i: (0, i))
    smem = pl.BlockSpec(memory_space=pltpu.SMEM)
    vmem = pl.BlockSpec(memory_space=pltpu.VMEM)
    tie = pl.BlockSpec(memory_space=pl.ANY)
    big = 2 * SLOTS * D * 2048
    back = pl.pallas_call(
        back_kernel,
        grid=(steps,),
        in_specs=[row_spec] + [weight_spec] * 4,
        out_specs=wide_spec,
        out_shape=shape((SLOTS, 2048), bf16),
        compiler_params=params(56),
        cost_estimate=pl.CostEstimate(flops=big, bytes_accessed=12 << 20, transcendentals=0),
    )(grad, *w2)
    w1_down = lax.ppermute(expert_in[0], "z", ring(3))
    w1_far = lax.ppermute(w1_up, "z", ring(1))
    w1 = [expert_in[0], w1_up, w1_far, w1_down]
    expert = lax.axis_index(DP).astype(jnp.int32).reshape(1)
    dslot, act, dpre, scale, dprob = pl.pallas_call(
        slot_kernel,
        grid=(steps,),
        in_specs=[
            smem,
            row_spec,
            wide_spec,
        ]
        + [weight_spec] * 4
        + [
            line_spec,
            pl.BlockSpec((EXPERTS, D), lambda i: (0, 0)),
        ],
        out_specs=[
            row_spec,
            wide_spec,
            wide_spec,
            line_spec,
            pl.BlockSpec((EXPERTS, BLOCK), lambda i: (0, i)),
        ],
        out_shape=(
            shape((EXPERTS, MOST, D), bf16),
            shape((SLOTS, 2048), bf16),
            shape((SLOTS, 2048), bf16),
            shape((1, SLOTS), f32),
            shape((EXPERTS, SLOTS), bf16),
        ),
        compiler_params=params(56),
        cost_estimate=pl.CostEstimate(
            flops=2 * big, bytes_accessed=32 << 20, transcendentals=SLOTS * 2048
        ),
    )(expert, rows, back, *w1, kept, w_router.T)
    dslot_home = exchange(dslot, DP)

    whole = pl.BlockSpec((EXPERTS, MOST, D), lambda i: (0, 0, 0))
    slices = pl.BlockSpec((SLOTS, 512), lambda i: (0, i))
    y, rows_t, back_t, *d_weights, d_router = pl.pallas_call(
        weight_kernel,
        grid=(N_Z,),
        in_specs=[
            whole,
            whole,
            pl.BlockSpec((1, SLOTS), lambda i: (0, 0)),
            slices,
            slices,
            pl.BlockSpec((EXPERTS, SLOTS), lambda i: (0, 0)),
        ]
        + [weight_spec] * 4,
        out_specs=[whole]
        + [pl.BlockSpec((D, SLOTS), lambda i: (0, 0))] * 2
        + [weight_spec] * 6
        + [pl.BlockSpec((D, EXPERTS), lambda i: (0, 0))],
        out_shape=(shape((EXPERTS, MOST, D), bf16),)
        + (shape((D, SLOTS), bf16),) * 2
        + (shape((D, 512), bf16), shape((512, D), bf16)) * 3
        + (shape((D, EXPERTS), f32),),
        scratch_shapes=[
            pltpu.VMEM((N_Z, 512, D), bf16),
            pltpu.VMEM((SLOTS, D), f32),
        ],
        compiler_params=params(60),
        cost_estimate=pl.CostEstimate(flops=0, bytes_accessed=0, transcendentals=0),
    )(rows, grad, scale, act, dpre, dprob, *w2)
    y_home = exchange(y, DP)

    down_in, down_out, far_in, far_out, up_in, up_out = d_weights
    below_far = lax.ppermute(far_in, "z", ring(1))
    above_far = lax.ppermute(far_out, "z", ring(3))
    below_out = lax.ppermute(up_out, "z", ring(1))
    above_in = lax.ppermute(down_in, "z", ring(3))
    up_in = (up_in.astype(f32) + below_far.astype(f32)).astype(bf16)
    down_out = (down_out.astype(f32) + above_far.astype(f32)).astype(bf16)
    below_in = lax.ppermute(up_in, "z", ring(1))
    above_out = lax.ppermute(down_out, "z", ring(3))

    core = lax.axis_index("core").astype(jnp.int32).reshape(1)
    keep, send, d_tokens = pl.pallas_call(
        backward_kernel,
        in_specs=[vmem] * 15 + [smem],
        out_shape=(
            shape((ROWS // 2, WIDTH), bf16),
            shape((ROWS // 2, WIDTH), bf16),
            shape((ROWS, D), f32),
        ),
        scratch_shapes=[
            pltpu.VMEM((ROWS, D), bf16),
            pltpu.VMEM((ROWS, 3 * D), bf16),
            pltpu.VMEM((ROWS, 128), f32),
            pltpu.VMEM((ROWS, 128), f32),
            pltpu.VMEM((ROWS, WIDTH), bf16),
            pltpu.VMEM((128, ROWS), f32),
        ],
        compiler_params=params(56),
        cost_estimate=pl.CostEstimate(
            flops=3000000000, bytes_accessed=0, transcendentals=0
        ),
    )(
        dslot_home,
        cols,
        segments,
        tokens,
        cotangent,
        residual,
        packed,
        attended,
        lse,
        gain1,
        bias1,
        w_qkv,
        w_out,
        gain2,
        d_router,
        core,
    )
    output = call(
        output_kernel,
        56,
        shape((ROWS, D), bf16),
        y_home,
        cols,
        residual,
        flops=2 * SLOTS * D * D,
    )
    fixed = pl.BlockSpec((D, SLOTS), lambda i: (0, 0))
    slices = pl.BlockSpec((SLOTS, 512), lambda i: (0, 0))
    d_in, d_out = pl.pallas_call(
        own_kernel,
        grid=(1,),
        in_specs=[fixed, fixed, slices, slices] + [weight_spec] * 4,
        out_specs=[pl.BlockSpec((1, D, 512), lambda i: (0, 0, 0))] * 2,
        out_shape=(shape((1, D, 512), f32), shape((1, 512, D), f32)),
        compiler_params=params(56),
        cost_estimate=pl.CostEstimate(flops=big // 2, bytes_accessed=0, transcendentals=0),
    )(rows_t, back_t, act, dpre, below_in, above_in, below_out, above_out)
    low, other = sum_everywhere(
        keep, after(send, below_in, below_out, above_in, above_out), y_home, (output, d_in)
    )
    d_w_qkv, d_w_out, d_w_router, *norms = pl.pallas_call(
        finish_kernel,
        in_specs=[vmem] * 2 + [smem],
        out_shape=(
            shape((D, 3 * D), f32),
            shape((D, D), f32),
            shape((EXPERTS, D), f32),
        )
        + (shape((1, D), f32),) * 4,
        scratch_shapes=[pltpu.VMEM((D, 128), f32)],
        compiler_params=params(56),
        cost_estimate=pl.CostEstimate(flops=0, bytes_accessed=7 << 20, transcendentals=0),
    )(low, other, core)
    return (
        output,
        d_tokens,
        norms[0].reshape(D),
        norms[1].reshape(D),
        d_w_qkv,
        d_w_out,
        norms[2].reshape(D),
        norms[3].reshape(D),
        d_w_router.T,
        d_in,
        d_out,
    )


def solution(mesh):
    fine = Mesh(mesh.devices.reshape(4, 4, 4, 2), ("z", "x", "y", "core"))
    every = ("z", "x", "y", "core")
    both = P(every, None)
    in_specs = (
        both,
        both,
        both,
        P(every),
        P(),
        P(),
        P(),
        P(),
        P(),
        P(),
        P(),
        P(DP, None, "z"),
        P(DP, "z", None),
        both,
    )
    out_specs = (
        both,
        both,
        P(),
        P(),
        P(),
        P(),
        P(),
        P(),
        P(),
        P(DP, None, "z"),
        P(DP, "z", None),
    )
    return jax.shard_map(
        per_device, mesh=fine, in_specs=in_specs, out_specs=out_specs, check_vma=False
    )
```

```python
import functools

import jax
import jax.numpy as jnp
from jax import lax
from jax.experimental import pallas as pl
from jax.experimental.pallas import tpu as pltpu
from jax.sharding import Mesh
from jax.sharding import PartitionSpec as P

D = 512
HEADS = 8
HDIM = 64
EXPERTS = 32
MOST = 64
ROWS = 512
SLOTS = EXPERTS * MOST
N_Z = 4
N_DP = 32
CAP = (21 * N_Z * N_DP * ROWS + 319) // 320
TOKENS = N_Z * N_DP * ROWS
EXTRA = 8
BLOCK = 512
WIDTH = 1152
EPS = 1e-06
SCALE = HDIM ** (-0.5)
STARTS = (0, 64, 192, 256)
GELU_C = 0.7978845608028654
GELU_A = 0.044715

bf16 = jnp.bfloat16
f32 = jnp.float32
MIB = 1024 * 1024


def dot(a, b):
    return lax.dot_general(a, b, (((1,), (0,)), ((), ())), preferred_element_type=f32)


def dot_nt(a, b):
    return lax.dot_general(a, b, (((1,), (1,)), ((), ())), preferred_element_type=f32)


def dot_tn(a, b):
    return lax.dot_general(a, b, (((0,), (0,)), ((), ())), preferred_element_type=f32)


def iota(shape, dim):
    return lax.broadcasted_iota(jnp.int32, shape, dim)


def normalize(values):
    center = values - jnp.mean(values, axis=-1, keepdims=True)
    factor = lax.rsqrt(jnp.mean(center * center, axis=-1, keepdims=True) + EPS)
    return center * factor, factor


def norm_backward(upstream, normal, factor, gain):
    scaled = upstream * gain
    inner = (
        scaled
        - jnp.mean(scaled, axis=-1, keepdims=True)
        - normal * jnp.mean(scaled * normal, axis=-1, keepdims=True)
    )
    return (
        inner * factor,
        jnp.sum(upstream * normal, axis=0, keepdims=True),
        jnp.sum(upstream, axis=0, keepdims=True),
    )


def pick_rows(csel_ref, rows, store):
    place = iota((MOST, ROWS), 0).astype(f32)
    for group in range(EXPERTS // 4):
        parts = []
        for j in range(4):
            line = csel_ref[group * 4 + j : group * 4 + j + 1, :]
            parts.append((place == line).astype(f32).astype(bf16))
        hot = jnp.concatenate(parts, axis=0)
        store(group, dot(hot, rows).astype(bf16))


def pack_kernel(routes_ref, prio_ref, seg_ref, cot_ref, send_ref, csel_ref, cols_ref, wide_ref):
    routes = routes_ref[...]
    experts = iota((EXPERTS, ROWS), 0)
    first = routes[0:1] == experts
    second = routes[1:2] == experts
    either = jnp.logical_or(first, second)
    before = (iota((ROWS, ROWS), 0) < iota((ROWS, ROWS), 1)).astype(f32).astype(bf16)
    count = dot(either.astype(f32).astype(bf16), before)
    slot = count + (experts * MOST).astype(f32)
    wide_ref[...] = jnp.zeros_like(wide_ref)
    wide_ref[0:1, :] = jnp.sum(jnp.where(first, slot, 0.0), axis=0, keepdims=True)
    wide_ref[1:2, :] = jnp.sum(jnp.where(second, slot, 0.0), axis=0, keepdims=True)
    wide_ref[2:3, :] = prio_ref[...].astype(f32)
    wide_ref[3:4, :] = seg_ref[...].astype(f32)
    csel_ref[...] = jnp.where(either, count, -1.0)
    cols = wide_ref[...].T
    cols_ref[...] = cols
    cols_int = cols[:, 0:3].astype(jnp.int32)
    pos0, pos1, key = cols_int[:, 0:1], cols_int[:, 1:2], cols_int[:, 2:3] + 1
    zeros = jnp.zeros((EXTRA, D), bf16)
    digit = iota((EXTRA, 256), 0)

    def store(group, rows):
        send_ref[group * 4 : group * 4 + 4, 0:MOST, :] = rows.reshape(4, MOST, D)
        spot = iota((ROWS, 256), 1) + group * 256
        keys = jnp.sum(
            jnp.where(spot == pos0, key, 0) + jnp.where(spot == pos1, key + TOKENS, 0),
            axis=0,
            keepdims=True,
        )
        low = jnp.bitwise_and(keys, 255)
        mid = jnp.bitwise_and(jnp.right_shift(keys, 8), 255)
        high = jnp.right_shift(keys, 16)
        digits = jnp.where(
            digit == 0, low, jnp.where(digit == 1, mid, jnp.where(digit == 2, high, 0))
        ).astype(f32)
        for j in range(4):
            send_ref[group * 4 + j, MOST : MOST + EXTRA, :] = zeros
            send_ref[group * 4 + j, MOST : MOST + EXTRA, 0:MOST] = digits[
                :, j * MOST : (j + 1) * MOST
            ].astype(bf16)

    pick_rows(csel_ref, cot_ref[...], store)


def stacked(pair):
    lanes = iota(pair.shape, 1)
    zero = jnp.zeros_like(pair)
    return jnp.concatenate(
        [jnp.where(lanes < HDIM, pair, zero), jnp.where(lanes >= HDIM, pair, zero)], axis=0
    )


def band_bias(cols_ref, seg_ref, block):
    start = STARTS[block]
    same = (
        cols_ref[block * 128 : block * 128 + 128, 3:4]
        == seg_ref[:, start : start + 256].astype(f32)
    )
    bias = jnp.where(same, 0.0, -1e30)
    return jnp.concatenate([bias, bias], axis=0)


def attend_kernel(
    tokens_ref,
    seg_ref,
    cols_ref,
    csel_ref,
    gain1_ref,
    bias1_ref,
    w_qkv_ref,
    w_out_ref,
    gain2_ref,
    bias2_ref,
    packed_ref,
    attended_ref,
    lse_ref,
    residual_ref,
    send_ref,
):
    inputs = tokens_ref[...].astype(f32)
    normal, _ = normalize(inputs)
    first = (normal * gain1_ref[...] + bias1_ref[...]).astype(bf16)
    for part in range(3):
        packed_ref[:, part * D : (part + 1) * D] = dot(
            first, w_qkv_ref[:, part * D : (part + 1) * D]
        ).astype(bf16)
    lanes = iota((128, 128), 1)
    for block in range(4):
        here = slice(block * 128, block * 128 + 128)
        window = slice(STARTS[block], STARTS[block] + 256)
        bias = band_bias(cols_ref, seg_ref, block)
        lse = jnp.zeros((128, 128), f32)
        for pair in range(4):
            at = pair * 128
            query = stacked(packed_ref[here, at : at + 128])
            scores = dot_nt(query, packed_ref[window, D + at : D + at + 128]) * SCALE + bias
            highest = jnp.max(scores, axis=-1, keepdims=True)
            raised = jnp.exp(scores - highest)
            total = jnp.sum(raised, axis=-1, keepdims=True)
            weights = (raised * (1.0 / total)).astype(bf16)
            mixed = dot(weights, packed_ref[window, 2 * D + at : 2 * D + at + 128])
            attended_ref[here, at : at + 128] = jnp.where(
                lanes < HDIM, mixed[0:128], mixed[128:256]
            ).astype(bf16)
            logsum = highest + jnp.log(total)
            lse = jnp.where(lanes == 2 * pair, logsum[0:128], lse)
            lse = jnp.where(lanes == 2 * pair + 1, logsum[128:256], lse)
        lse_ref[here, :] = lse
    residual = inputs + dot(attended_ref[...], w_out_ref[...])
    residual_ref[...] = residual
    normal2, _ = normalize(residual)
    second = (normal2 * gain2_ref[...] + bias2_ref[...]).astype(bf16)

    def store(group, rows):
        send_ref[group * 4 : group * 4 + 4] = rows.reshape(4, MOST, D)

    pick_rows(csel_ref, second, store)


def keep_kernel(own_ref, a_ref, b_ref, c_ref, d_ref, kept_ref):
    empty = 2 * TOKENS + 1
    keys = jnp.concatenate([a_ref[...], b_ref[...], c_ref[...], d_ref[...]], axis=0)
    keys = jnp.where(keys == 0, empty, keys)

    def step(_, bounds):
        low, high = bounds
        middle = jnp.right_shift(low + high, 1)
        enough = jnp.sum((keys <= middle).astype(jnp.int32), keepdims=True) >= CAP
        return jnp.where(enough, low, middle + 1), jnp.where(enough, middle, high)

    low = jnp.zeros((1, 1), jnp.int32)
    high = jnp.full((1, 1), 2 * TOKENS, jnp.int32)
    low, high = lax.fori_loop(0, 18, step, (low, high))
    own = own_ref[...]
    kept_ref[...] = jnp.logical_and(own > 0, own <= high).astype(f32)


def back_kernel(grad_ref, *refs):
    *w2_refs, out_ref = refs
    rows = grad_ref[...].reshape(BLOCK, D)
    for part, w2_ref in enumerate(w2_refs):
        out_ref[:, part * 512 : part * 512 + 512] = dot_nt(rows, w2_ref[...]).astype(bf16)


def slot_kernel(
    expert_ref,
    x_ref,
    gw_ref,
    w1a_ref,
    w1b_ref,
    w1c_ref,
    w1d_ref,
    kept_ref,
    w_router_ref,
    dslot_ref,
    act_ref,
    dpre_ref,
    scale_ref,
    dprob_ref,
):
    rows = x_ref[...].reshape(BLOCK, D)
    w_router = w_router_ref[...]
    dslot = jnp.zeros((BLOCK, D), f32)
    dgate = jnp.zeros((BLOCK, 128), f32)
    parts = (w1a_ref, w1b_ref, w1c_ref, w1d_ref)
    tiles = [ref[:, at : at + 256] for ref in parts for at in (0, 256)]
    pre = dot(rows, tiles[0])
    held = None
    for step, weight in enumerate(tiles):
        following = dot(rows, tiles[step + 1]) if step + 1 < len(tiles) else None
        if step == 4:
            logits = dot_nt(w_router, rows)
            raised = jnp.exp(logits - jnp.max(logits, axis=0, keepdims=True))
            prob = raised / jnp.sum(raised, axis=0, keepdims=True)
            mine = iota((EXPERTS, BLOCK), 0) == expert_ref[0]
            scale = kept_ref[...] * jnp.sum(jnp.where(mine, prob, 0.0), axis=0, keepdims=True)
            scale_ref[...] = scale
            scale_col = jnp.broadcast_to(scale, (8, BLOCK)).T[:, 0:1]
        span = slice(step * 256, step * 256 + 256)
        square = pre * pre
        half = 0.5 * jnp.tanh(pre * (square * (GELU_A * GELU_C) + GELU_C)) + 0.5
        act = pre * half
        slope = half + act * (1.0 - half) * (square * (6.0 * GELU_A * GELU_C) + 2.0 * GELU_C)
        upstream = gw_ref[:, span].astype(f32)
        product = upstream * act
        dgate = dgate + product[:, 0:128] + product[:, 128:256]
        dpre = (upstream * slope).astype(bf16)
        act_ref[:, span] = act.astype(bf16)
        dpre_ref[:, span] = dpre
        if held is not None:
            dslot = dslot + dot_nt(*held)
        held = dpre, weight
        pre = following
    dslot = dslot + dot_nt(*held)
    dgate = jnp.sum(dgate.T, axis=0, keepdims=True)
    dprob = dgate * (mine.astype(f32) - prob)
    dprob_ref[...] = dprob.astype(bf16)
    dslot = dslot * scale_col + dot_tn((scale * dprob).astype(bf16), w_router)
    dslot_ref[...] = dslot.astype(bf16).reshape(BLOCK // MOST, MOST, D)


def weight_kernel(
    x_ref,
    grad_ref,
    scale_ref,
    act_ref,
    dpre_ref,
    dprob_ref,
    w2a_ref,
    w2b_ref,
    w2c_ref,
    w2d_ref,
    y_ref,
    rows_ref,
    back_ref,
    down_ref,
    far_ref,
    up_ref,
    d_router_ref,
    w2_ref,
    total_ref,
):
    step = pl.program_id(0)

    @pl.when(step == 0)
    def _():
        for at in range(0, SLOTS, 512):
            one = slice(at // MOST, at // MOST + 8)
            here = slice(at, at + 512)
            scale = scale_ref[:, here]
            rows_ref[:, here] = (x_ref[one].reshape(512, D).astype(f32).T * scale).astype(bf16)
            back_ref[:, here] = (
                grad_ref[one, 0:MOST, :].reshape(512, D).astype(f32).T * scale
            ).astype(bf16)
        d_router_ref[...] = dot_nt(rows_ref[...], dprob_ref[...])
        for part, part_ref in enumerate((w2a_ref, w2b_ref, w2c_ref, w2d_ref)):
            w2_ref[part] = part_ref[...]
        total_ref[...] = jnp.zeros_like(total_ref)

    total_ref[...] += dot(act_ref[...], w2_ref[step])

    @pl.when(step > 0)
    def _():
        d_in = dot(rows_ref[...], dpre_ref[...]).astype(bf16)
        d_out = dot(back_ref[...], act_ref[...]).T.astype(bf16)
        for part, out_ref in enumerate((down_ref, far_ref, up_ref)):

            @pl.when(step == part + 1)
            def _():
                out_ref[0] = d_in
                out_ref[1] = d_out

    @pl.when(step == N_Z - 1)
    def _():
        for at in range(0, SLOTS, 512):
            one = slice(at // MOST, at // MOST + 8)
            here = slice(at, at + 512)
            scale_col = jnp.broadcast_to(scale_ref[:, here], (8, 512)).T[:, 0:1]
            y_ref[one] = (total_ref[here, :] * scale_col).astype(bf16).reshape(8, MOST, D)


def gather_slots(cols_ref, rows_ref):
    pos0 = cols_ref[:, 0:1].astype(jnp.int32)
    pos1 = cols_ref[:, 1:2].astype(jnp.int32)
    total = jnp.zeros((ROWS, D), f32)
    for part in range(4):
        spot = iota((ROWS, 512), 1) + part * 512
        hot = jnp.logical_or(spot == pos0, spot == pos1).astype(f32).astype(bf16)
        total = total + dot(hot, rows_ref[part * 8 : part * 8 + 8].reshape(512, D))
    return total


def backward_kernel(
    dslot_ref,
    cols_ref,
    seg_ref,
    tokens_ref,
    cot_ref,
    residual_ref,
    packed_ref,
    attended_ref,
    lse_ref,
    gain1_ref,
    bias1_ref,
    w_qkv_ref,
    w_out_ref,
    gain2_ref,
    d_router_ref,
    core_ref,
    keep_ref,
    send_ref,
    d_tokens_ref,
    datt_ref,
    dpacked_ref,
    dkey_ref,
    dvalue_ref,
    grads_ref,
    wide_ref,
):
    d_second = gather_slots(cols_ref, dslot_ref)
    normal2, factor2 = normalize(residual_ref[...])
    d_norm2, d_gain2, d_shift2 = norm_backward(d_second, normal2, factor2, gain2_ref[...])
    d_residual = cot_ref[...].astype(f32) + d_norm2
    d_tokens_ref[...] = d_residual
    d_branch = d_residual.astype(bf16)
    grads_ref[:, 3 * D : 4 * D] = dot_tn(attended_ref[...], d_branch).astype(bf16)
    datt_ref[...] = dot_nt(d_branch, w_out_ref[...]).astype(bf16)
    lanes = iota((128, 128), 1)
    for pair in range(4):
        at = pair * 128
        dkey_ref[...] = jnp.zeros_like(dkey_ref)
        dvalue_ref[...] = jnp.zeros_like(dvalue_ref)
        for block in range(4):
            here = slice(block * 128, block * 128 + 128)
            window = slice(STARTS[block], STARTS[block] + 256)
            bias = band_bias(cols_ref, seg_ref, block)
            query = stacked(packed_ref[here, at : at + 128])
            upstream = stacked(datt_ref[here, at : at + 128])
            keys = packed_ref[window, D + at : D + at + 128]
            values = packed_ref[window, 2 * D + at : 2 * D + at + 128]
            logsum = jnp.concatenate(
                [
                    lse_ref[here, 2 * pair : 2 * pair + 1],
                    lse_ref[here, 2 * pair + 1 : 2 * pair + 2],
                ],
                axis=0,
            )
            weights = jnp.exp(dot_nt(query, keys) * SCALE + bias - logsum)
            d_weights = dot_nt(upstream, values)
            inner = jnp.sum(weights * d_weights, axis=-1, keepdims=True)
            d_scores = (weights * (d_weights - inner)).astype(bf16)
            d_query = dot(d_scores, keys) * SCALE
            dpacked_ref[here, at : at + 128] = jnp.where(
                lanes < HDIM, d_query[0:128], d_query[128:256]
            ).astype(bf16)
            dkey_ref[window, :] += dot_tn(d_scores, query)
            dvalue_ref[window, :] += dot_tn(weights.astype(bf16), upstream)
        dpacked_ref[:, D + at : D + at + 128] = (dkey_ref[...] * SCALE).astype(bf16)
        dpacked_ref[:, 2 * D + at : 2 * D + at + 128] = dvalue_ref[...].astype(bf16)
    normal1, factor1 = normalize(tokens_ref[...].astype(f32))
    first = (normal1 * gain1_ref[...] + bias1_ref[...]).astype(bf16)
    for part in range(3):
        grads_ref[:, part * D : (part + 1) * D] = dot_tn(
            first, dpacked_ref[:, part * D : (part + 1) * D]
        ).astype(bf16)
    d_first = dot_nt(dpacked_ref[...], w_qkv_ref[...])
    d_norm1, d_gain1, d_shift1 = norm_backward(d_first, normal1, factor1, gain1_ref[...])
    d_tokens_ref[...] += d_norm1
    wide_ref[...] = jnp.zeros_like(wide_ref)
    wide_ref[0:1, :] = d_gain1
    wide_ref[1:2, :] = d_shift1
    wide_ref[2:3, :] = d_gain2
    wide_ref[3:4, :] = d_shift2
    grads_ref[:, 4 * D + 128 :] = jnp.zeros((ROWS, 128), bf16)
    grads_ref[:, 4 * D : 4 * D + 128] = wide_ref[...].T.astype(bf16)
    grads_ref[:, 4 * D + EXPERTS : 4 * D + 2 * EXPERTS] = d_router_ref[...].astype(bf16)
    core = core_ref[0]
    for half in range(2):
        span = slice(half * WIDTH, half * WIDTH + WIDTH)
        keep_ref[half] = grads_ref[pl.ds(pl.multiple_of(core * 256, 256), 256), span]
        send_ref[half] = grads_ref[pl.ds(pl.multiple_of((1 - core) * 256, 256), 256), span]


def finish_kernel(
    low_ref,
    other_ref,
    core_ref,
    qkv_ref,
    out_ref,
    router_ref,
    gain1_ref,
    shift1_ref,
    gain2_ref,
    shift2_ref,
    wide_ref,
):
    core = core_ref[0]
    split = 3 * D - WIDTH
    for mine, half_ref in ((core, low_ref), (1 - core, other_ref)):
        here = pl.ds(pl.multiple_of(mine * 256, 256), 256)
        qkv_ref[here, 0:WIDTH] = half_ref[0].astype(f32)
        qkv_ref[here, WIDTH:] = half_ref[1, :, 0:split].astype(f32)
        out_ref[here, :] = half_ref[1, :, split : split + D].astype(f32)
        wide_ref[here, :] = half_ref[1, :, split + D : split + D + 128].astype(f32)
    lines = wide_ref[...].T
    router_ref[...] = lines[EXPERTS : 2 * EXPERTS]
    for row, out in enumerate((gain1_ref, shift1_ref, gain2_ref, shift2_ref)):
        out[...] = lines[row : row + 1]


def output_kernel(y_ref, cols_ref, residual_ref, out_ref):
    out_ref[...] = (residual_ref[...] + gather_slots(cols_ref, y_ref)).astype(bf16)


def own_kernel(
    rows_ref, back_ref, act_ref, dpre_ref, above_ref, below_ref, token_ref, d_in_ref, d_out_ref
):
    for half, out_ref in enumerate((d_in_ref, d_out_ref)):
        out_ref[0] = above_ref[half].astype(f32) + below_ref[half].astype(f32)
    d_in_ref[0] += dot(rows_ref[...], dpre_ref[...])
    d_out_ref[0] += dot(back_ref[...], act_ref[...]).T


def across_kernel(d_in_ref, d_out_ref, across_ref, token_ref, sum_in_ref, sum_out_ref):
    sum_in_ref[0] = d_in_ref[0] + across_ref[0].astype(f32)
    sum_out_ref[0] = d_out_ref[0] + across_ref[1].astype(f32)


def params(mib):
    return pltpu.CompilerParams(vmem_limit_bytes=mib * MIB)


def after(values, *tokens, flops=0):
    anywhere = pl.BlockSpec(memory_space=pl.ANY)
    return pl.pallas_call(
        lambda *refs: None,
        in_specs=[anywhere] * (1 + len(tokens)),
        out_specs=anywhere,
        out_shape=shape(values.shape, values.dtype),
        input_output_aliases={0: 0},
        cost_estimate=pl.CostEstimate(flops=flops, bytes_accessed=0, transcendentals=0),
    )(values, *tokens)


def call(kernel, mib, out_shape, *args, flops=0, scratch=()):
    shapes = jax.tree.leaves(out_shape)
    moved = sum(a.size * a.dtype.itemsize for a in args) + sum(
        s.size * s.dtype.itemsize for s in shapes
    )
    return pl.pallas_call(
        kernel,
        out_shape=out_shape,
        scratch_shapes=list(scratch),
        compiler_params=params(mib),
        cost_estimate=pl.CostEstimate(flops=flops, bytes_accessed=moved, transcendentals=0),
    )(*args)


def shape(dims, dtype):
    return jax.ShapeDtypeStruct(dims, dtype)


DP = ("x", "y", "core")
CHIPS = ("x", "y")
SWAP = [(0, 1), (1, 0)]


def ring(distance):
    return [(i, (i + distance) % 4) for i in range(4)]


def exchange(values, axes):
    return lax.all_to_all(values, axes, split_axis=0, concat_axis=0, tiled=True)


def add_cores(keep, send, token):
    got = lax.ppermute(send, "core", SWAP)
    return after((keep.astype(f32) + got.astype(f32)).astype(bf16), token)


def sum_chips(low, *tokens):
    parts = exchange(low.reshape(16, 32, WIDTH), CHIPS)
    low = after(jnp.sum(parts.astype(f32), axis=0).astype(bf16), *tokens)
    got = [lax.ppermute(low, "z", ring(d)).astype(f32) for d in (1, 2, 3)]
    low = ((low.astype(f32) + got[1]) + (got[0] + got[2])).astype(bf16)
    low = exchange(jnp.broadcast_to(low[None], (16, 32, WIDTH)), CHIPS).reshape(2, 256, WIDTH)
    return low, lax.ppermute(low, "core", SWAP)


def per_device(
    tokens,
    segments,
    routes,
    priority,
    ln1_gain,
    ln1_bias,
    w_qkv,
    w_out,
    ln2_gain,
    ln2_bias,
    w_router,
    expert_in,
    expert_out,
    cotangent,
):
    gain1, bias1 = ln1_gain.reshape(1, D), ln1_bias.reshape(1, D)
    gain2, bias2 = ln2_gain.reshape(1, D), ln2_bias.reshape(1, D)
    w2_up = lax.ppermute(expert_out[0], "z", ring(1))
    w2_down = lax.ppermute(expert_out[0], "z", ring(3))
    w2_far = lax.ppermute(w2_down, "z", ring(3))
    w2 = [expert_out[0], w2_up, w2_far, w2_down]
    w1_up = lax.ppermute(expert_in[0], "z", ring(1))

    send_grad, csel, cols = call(
        pack_kernel,
        62,
        (
            shape((EXPERTS, MOST + EXTRA, D), bf16),
            shape((EXPERTS, ROWS), f32),
            shape((ROWS, 128), f32),
        ),
        routes.T,
        priority.reshape(1, ROWS),
        segments,
        cotangent,
        flops=2 * SLOTS * D * D,
        scratch=[pltpu.VMEM((128, ROWS), f32)],
    )
    grad = exchange(send_grad, DP)

    packed, attended, lse, residual, send_rows = call(
        attend_kernel,
        62,
        (
            shape((ROWS, 3 * D), bf16),
            shape((ROWS, D), bf16),
            shape((ROWS, 128), f32),
            shape((ROWS, D), f32),
            shape((EXPERTS, MOST, D), bf16),
        ),
        tokens,
        segments,
        cols,
        csel,
        gain1,
        bias1,
        w_qkv,
        w_out,
        gain2,
        bias2,
        flops=2 * SLOTS * D * D + 10 * ROWS * D * D,
    )
    send_rows = after(send_rows, w2_up, w2_far, w2_down, w1_up)
    rows = exchange(send_rows, DP)

    digits = grad[:, MOST : MOST + 3, 0:MOST].astype(jnp.int32)
    keys = (digits[:, 0] + 256 * digits[:, 1] + 65536 * digits[:, 2]).reshape(16, 128)
    planes = [lax.ppermute(keys, "z", ring(d)) for d in (1, 2, 3)]
    kept = call(keep_kernel, 62, shape((16, 128), f32), keys, keys, *planes).reshape(1, SLOTS)

    steps = SLOTS // BLOCK
    weight_spec = pl.BlockSpec((D, 512), lambda i: (0, 0))
    row_spec = pl.BlockSpec((BLOCK // MOST, MOST, D), lambda i: (i, 0, 0))
    wide_spec = pl.BlockSpec((BLOCK, 2048), lambda i: (i, 0))
    line_spec = pl.BlockSpec((1, BLOCK), lambda i: (0, i))
    smem = pl.BlockSpec(memory_space=pltpu.SMEM)
    vmem = pl.BlockSpec(memory_space=pltpu.VMEM)
    tie = pl.BlockSpec(memory_space=pl.ANY)
    big = 2 * SLOTS * D * 2048
    back = pl.pallas_call(
        back_kernel,
        grid=(steps,),
        in_specs=[row_spec] + [weight_spec] * 4,
        out_specs=wide_spec,
        out_shape=shape((SLOTS, 2048), bf16),
        compiler_params=params(62),
        cost_estimate=pl.CostEstimate(flops=big, bytes_accessed=12 << 20, transcendentals=0),
    )(grad, *w2)
    w1_down = lax.ppermute(expert_in[0], "z", ring(3))
    w1_far = lax.ppermute(w1_up, "z", ring(1))
    w1 = [expert_in[0], w1_up, w1_far, w1_down]
    expert = lax.axis_index(DP).astype(jnp.int32).reshape(1)
    dslot, act, dpre, scale, dprob = pl.pallas_call(
        slot_kernel,
        grid=(steps,),
        in_specs=[
            smem,
            row_spec,
            wide_spec,
        ]
        + [weight_spec] * 4
        + [
            line_spec,
            pl.BlockSpec((EXPERTS, D), lambda i: (0, 0)),
        ],
        out_specs=[
            row_spec,
            wide_spec,
            wide_spec,
            line_spec,
            pl.BlockSpec((EXPERTS, BLOCK), lambda i: (0, i)),
        ],
        out_shape=(
            shape((EXPERTS, MOST, D), bf16),
            shape((SLOTS, 2048), bf16),
            shape((SLOTS, 2048), bf16),
            shape((1, SLOTS), f32),
            shape((EXPERTS, SLOTS), bf16),
        ),
        compiler_params=params(62),
        cost_estimate=pl.CostEstimate(
            flops=2 * big, bytes_accessed=32 << 20, transcendentals=SLOTS * 2048
        ),
    )(expert, rows, back, *w1, kept, w_router.T)
    dslot_home = after(exchange(dslot, DP), flops=60 * 10**9)

    whole = pl.BlockSpec((EXPERTS, MOST, D), lambda i: (0, 0, 0))
    slices = pl.BlockSpec((SLOTS, 512), lambda i: (0, i))
    y, rows_t, back_t, *d_weights, d_router = pl.pallas_call(
        weight_kernel,
        grid=(N_Z,),
        in_specs=[
            whole,
            whole,
            pl.BlockSpec((1, SLOTS), lambda i: (0, 0)),
            slices,
            slices,
            pl.BlockSpec((EXPERTS, SLOTS), lambda i: (0, 0)),
        ]
        + [weight_spec] * 4,
        out_specs=[whole]
        + [pl.BlockSpec((D, SLOTS), lambda i: (0, 0))] * 2
        + [pl.BlockSpec((2, D, 512), lambda i: (0, 0, 0))] * 3
        + [pl.BlockSpec((D, EXPERTS), lambda i: (0, 0))],
        out_shape=(shape((EXPERTS, MOST, D), bf16),)
        + (shape((D, SLOTS), bf16),) * 2
        + (shape((2, D, 512), bf16),) * 3
        + (shape((D, EXPERTS), f32),),
        scratch_shapes=[
            pltpu.VMEM((N_Z, 512, D), bf16),
            pltpu.VMEM((SLOTS, D), f32),
        ],
        compiler_params=params(62),
        cost_estimate=pl.CostEstimate(flops=0, bytes_accessed=0, transcendentals=0),
    )(rows, grad, scale, act, dpre, dprob, *w2)
    y_home = exchange(y, DP)

    down, far, up = d_weights
    received = [
        lax.ppermute(down, "z", ring(3)),
        lax.ppermute(far, "z", ring(2)),
        lax.ppermute(up, "z", ring(1)),
    ]

    core = lax.axis_index("core").astype(jnp.int32).reshape(1)
    keep, send, d_tokens = pl.pallas_call(
        backward_kernel,
        in_specs=[vmem] * 15 + [smem],
        out_shape=(
            shape((2, ROWS // 2, WIDTH), bf16),
            shape((2, ROWS // 2, WIDTH), bf16),
            shape((ROWS, D), f32),
        ),
        scratch_shapes=[
            pltpu.VMEM((ROWS, D), bf16),
            pltpu.VMEM((ROWS, 3 * D), bf16),
            pltpu.VMEM((ROWS, 128), f32),
            pltpu.VMEM((ROWS, 128), f32),
            pltpu.VMEM((ROWS, 2 * WIDTH), bf16),
            pltpu.VMEM((128, ROWS), f32),
        ],
        compiler_params=params(62),
        cost_estimate=pl.CostEstimate(
            flops=3000000000, bytes_accessed=0, transcendentals=0
        ),
    )(
        dslot_home,
        cols,
        segments,
        tokens,
        cotangent,
        residual,
        packed,
        attended,
        lse,
        gain1,
        bias1,
        w_qkv,
        w_out,
        gain2,
        d_router,
        core,
    )
    low = add_cores(keep, after(send, received[0], received[2]), y_home)
    output = call(output_kernel, 62, shape((ROWS, D), bf16), y_home, cols, residual)
    fixed = pl.BlockSpec((D, SLOTS), lambda i: (0, 0))
    slices = pl.BlockSpec((SLOTS, 512), lambda i: (0, 0))
    d_in, d_out = pl.pallas_call(
        own_kernel,
        grid=(1,),
        in_specs=[fixed, fixed, slices, slices]
        + [pl.BlockSpec((2, D, 512), lambda i: (0, 0, 0))] * 2
        + [tie],
        out_specs=[pl.BlockSpec((1, D, 512), lambda i: (0, 0, 0))] * 2,
        out_shape=(shape((1, D, 512), f32), shape((1, 512, D), f32)),
        compiler_params=params(62),
        cost_estimate=pl.CostEstimate(flops=0, bytes_accessed=0, transcendentals=0),
    )(rows_t, back_t, act, dpre, received[0], received[2], low)
    d_in, d_out = pl.pallas_call(
        across_kernel,
        in_specs=[vmem] * 3 + [tie],
        out_shape=(shape((1, D, 512), f32), shape((1, 512, D), f32)),
        compiler_params=params(62),
        cost_estimate=pl.CostEstimate(flops=6 * 10**9, bytes_accessed=0, transcendentals=0),
    )(d_in, d_out, received[1], output)
    low, other = sum_chips(low, d_in)
    d_w_qkv, d_w_out, d_w_router, *norms = pl.pallas_call(
        finish_kernel,
        in_specs=[vmem] * 2 + [smem],
        out_shape=(
            shape((D, 3 * D), f32),
            shape((D, D), f32),
            shape((EXPERTS, D), f32),
        )
        + (shape((1, D), f32),) * 4,
        scratch_shapes=[pltpu.VMEM((D, 128), f32)],
        compiler_params=params(62),
        cost_estimate=pl.CostEstimate(flops=0, bytes_accessed=7 << 20, transcendentals=0),
    )(low, other, core)
    return (
        output,
        d_tokens,
        norms[0].reshape(D),
        norms[1].reshape(D),
        d_w_qkv,
        d_w_out,
        norms[2].reshape(D),
        norms[3].reshape(D),
        d_w_router.T,
        d_in,
        d_out,
    )


def solution(mesh):
    fine = Mesh(mesh.devices.reshape(4, 4, 4, 2), ("z", "x", "y", "core"))
    every = ("z", "x", "y", "core")
    both = P(every, None)
    in_specs = (
        both,
        both,
        both,
        P(every),
        P(),
        P(),
        P(),
        P(),
        P(),
        P(),
        P(),
        P(DP, None, "z"),
        P(DP, "z", None),
        both,
    )
    out_specs = (
        both,
        both,
        P(),
        P(),
        P(),
        P(),
        P(),
        P(),
        P(),
        P(DP, None, "z"),
        P(DP, "z", None),
    )
    return jax.shard_map(
        per_device, mesh=fine, in_specs=in_specs, out_specs=out_specs, check_vma=False
    )
```

```python
import functools

import jax
import jax.numpy as jnp
from jax import lax
from jax.experimental import pallas as pl
from jax.experimental.pallas import tpu as pltpu
from jax.sharding import Mesh
from jax.sharding import PartitionSpec as P

D = 512
HEADS = 8
HDIM = 64
EXPERTS = 32
MOST = 64
ROWS = 512
SLOTS = EXPERTS * MOST
N_Z = 4
N_DP = 32
CAP = (21 * N_Z * N_DP * ROWS + 319) // 320
TOKENS = N_Z * N_DP * ROWS
EXTRA = 8
BLOCK = 512
WIDTH = 1152
EPS = 1e-06
SCALE = HDIM ** (-0.5)
STARTS = (0, 64, 192, 256)
GELU_C = 0.7978845608028654
GELU_A = 0.044715

bf16 = jnp.bfloat16
f32 = jnp.float32
MIB = 1024 * 1024


def dot(a, b):
    return lax.dot_general(a, b, (((1,), (0,)), ((), ())), preferred_element_type=f32)


def dot_nt(a, b):
    return lax.dot_general(a, b, (((1,), (1,)), ((), ())), preferred_element_type=f32)


def dot_tn(a, b):
    return lax.dot_general(a, b, (((0,), (0,)), ((), ())), preferred_element_type=f32)


def iota(shape, dim):
    return lax.broadcasted_iota(jnp.int32, shape, dim)


def normalize(values):
    center = values - jnp.mean(values, axis=-1, keepdims=True)
    factor = lax.rsqrt(jnp.mean(center * center, axis=-1, keepdims=True) + EPS)
    return center * factor, factor


def norm_backward(upstream, normal, factor, gain):
    scaled = upstream * gain
    inner = (
        scaled
        - jnp.mean(scaled, axis=-1, keepdims=True)
        - normal * jnp.mean(scaled * normal, axis=-1, keepdims=True)
    )
    return (
        inner * factor,
        jnp.sum(upstream * normal, axis=0, keepdims=True),
        jnp.sum(upstream, axis=0, keepdims=True),
    )


def pick_rows(csel_ref, rows, store):
    place = iota((MOST, ROWS), 0).astype(f32)
    for group in range(EXPERTS // 4):
        parts = []
        for j in range(4):
            line = csel_ref[group * 4 + j : group * 4 + j + 1, :]
            parts.append((place == line).astype(f32).astype(bf16))
        hot = jnp.concatenate(parts, axis=0)
        store(group, dot(hot, rows).astype(bf16))


def pack_kernel(routes_ref, prio_ref, seg_ref, cot_ref, send_ref, csel_ref, cols_ref, wide_ref):
    routes = routes_ref[...]
    experts = iota((EXPERTS, ROWS), 0)
    first = routes[0:1] == experts
    second = routes[1:2] == experts
    either = jnp.logical_or(first, second)
    before = (iota((ROWS, ROWS), 0) < iota((ROWS, ROWS), 1)).astype(f32).astype(bf16)
    count = dot(either.astype(f32).astype(bf16), before)
    slot = count + (experts * MOST).astype(f32)
    wide_ref[...] = jnp.zeros_like(wide_ref)
    wide_ref[0:1, :] = jnp.sum(jnp.where(first, slot, 0.0), axis=0, keepdims=True)
    wide_ref[1:2, :] = jnp.sum(jnp.where(second, slot, 0.0), axis=0, keepdims=True)
    wide_ref[2:3, :] = prio_ref[...].astype(f32)
    wide_ref[3:4, :] = seg_ref[...].astype(f32)
    csel_ref[...] = jnp.where(either, count, -1.0)
    cols = wide_ref[...].T
    cols_ref[...] = cols
    key = prio_ref[...] + 1
    digits = [
        jnp.bitwise_and(key, 255),
        jnp.bitwise_and(jnp.right_shift(key, 8), 255),
        jnp.right_shift(key, 16),
    ]
    digits = [line.astype(f32) for line in digits]
    later = second.astype(f32)
    empty = jnp.zeros((1, ROWS), f32)
    zeros = jnp.zeros((EXTRA, D), bf16)
    rows = cot_ref[...]
    place = iota((MOST, ROWS), 0).astype(f32)
    for group in range(EXPERTS // 4):
        four = range(group * 4, group * 4 + 4)
        hot = jnp.concatenate(
            [(place == csel_ref[e : e + 1, :]).astype(f32).astype(bf16) for e in four], axis=0
        )
        picked = dot(hot, rows).astype(bf16)
        send_ref[group * 4 : group * 4 + 4, 0:MOST, :] = picked.reshape(4, MOST, D)
        lines = jnp.concatenate(digits + [later[e : e + 1] for e in four] + [empty], axis=0)
        keys = dot_nt(lines.astype(bf16), hot)
        for j, e in enumerate(four):
            send_ref[e, MOST : MOST + EXTRA, :] = zeros
            send_ref[e, MOST : MOST + EXTRA, 0:MOST] = keys[
                :, j * MOST : (j + 1) * MOST
            ].astype(bf16)


def stacked(pair):
    lanes = iota(pair.shape, 1)
    zero = jnp.zeros_like(pair)
    return jnp.concatenate(
        [jnp.where(lanes < HDIM, pair, zero), jnp.where(lanes >= HDIM, pair, zero)], axis=0
    )


def band_bias(cols_ref, seg_ref, block):
    start = STARTS[block]
    same = (
        cols_ref[block * 128 : block * 128 + 128, 3:4]
        == seg_ref[:, start : start + 256].astype(f32)
    )
    bias = jnp.where(same, 0.0, -1e30)
    return jnp.concatenate([bias, bias], axis=0)


def attend_kernel(
    tokens_ref,
    seg_ref,
    cols_ref,
    csel_ref,
    gain1_ref,
    bias1_ref,
    w_qkv_ref,
    w_out_ref,
    gain2_ref,
    bias2_ref,
    packed_ref,
    attended_ref,
    lse_ref,
    residual_ref,
    send_ref,
):
    inputs = tokens_ref[...].astype(f32)
    normal, _ = normalize(inputs)
    first = (normal * gain1_ref[...] + bias1_ref[...]).astype(bf16)
    for part in range(3):
        packed_ref[:, part * D : (part + 1) * D] = dot(
            first, w_qkv_ref[:, part * D : (part + 1) * D]
        ).astype(bf16)
    lanes = iota((128, 128), 1)
    for block in range(4):
        here = slice(block * 128, block * 128 + 128)
        window = slice(STARTS[block], STARTS[block] + 256)
        bias = band_bias(cols_ref, seg_ref, block)
        lse = jnp.zeros((128, 128), f32)
        for pair in range(4):
            at = pair * 128
            query = stacked(packed_ref[here, at : at + 128])
            scores = dot_nt(query, packed_ref[window, D + at : D + at + 128]) * SCALE + bias
            highest = jnp.max(scores, axis=-1, keepdims=True)
            raised = jnp.exp(scores - highest)
            total = jnp.sum(raised, axis=-1, keepdims=True)
            weights = (raised * (1.0 / total)).astype(bf16)
            mixed = dot(weights, packed_ref[window, 2 * D + at : 2 * D + at + 128])
            attended_ref[here, at : at + 128] = jnp.where(
                lanes < HDIM, mixed[0:128], mixed[128:256]
            ).astype(bf16)
            logsum = highest + jnp.log(total)
            lse = jnp.where(lanes == 2 * pair, logsum[0:128], lse)
            lse = jnp.where(lanes == 2 * pair + 1, logsum[128:256], lse)
        lse_ref[here, :] = lse
    residual = inputs + dot(attended_ref[...], w_out_ref[...])
    residual_ref[...] = residual
    normal2, _ = normalize(residual)
    second = (normal2 * gain2_ref[...] + bias2_ref[...]).astype(bf16)

    def store(group, rows):
        send_ref[group * 4 : group * 4 + 4] = rows.reshape(4, MOST, D)

    pick_rows(csel_ref, second, store)


def keep_kernel(own_ref, a_ref, b_ref, c_ref, d_ref, kept_ref):
    empty = 2 * TOKENS + 1
    keys = jnp.concatenate([a_ref[...], b_ref[...], c_ref[...], d_ref[...]], axis=0)
    keys = jnp.where(keys == 0, empty, keys)

    def step(_, bounds):
        low, high = bounds
        middle = jnp.right_shift(low + high, 1)
        enough = jnp.sum((keys <= middle).astype(jnp.int32), keepdims=True) >= CAP
        return jnp.where(enough, low, middle + 1), jnp.where(enough, middle, high)

    low = jnp.zeros((1, 1), jnp.int32)
    high = jnp.full((1, 1), 2 * TOKENS, jnp.int32)
    low, high = lax.fori_loop(0, 18, step, (low, high))
    own = own_ref[...]
    kept_ref[...] = jnp.logical_and(own > 0, own <= high).astype(f32)


def back_kernel(grad_ref, *refs):
    *w2_refs, out_ref = refs
    rows = grad_ref[...].reshape(BLOCK, D)
    for part, w2_ref in enumerate(w2_refs):
        out_ref[:, part * 512 : part * 512 + 512] = dot_nt(rows, w2_ref[...]).astype(bf16)


def slot_kernel(
    expert_ref,
    x_ref,
    gw_ref,
    w1a_ref,
    w1b_ref,
    w1c_ref,
    w1d_ref,
    kept_ref,
    w_router_ref,
    dslot_ref,
    act_ref,
    dpre_ref,
    scale_ref,
    dprob_ref,
):
    rows = x_ref[...].reshape(BLOCK, D)
    w_router = w_router_ref[...]
    dslot = jnp.zeros((BLOCK, D), f32)
    dgate = jnp.zeros((BLOCK, 128), f32)
    parts = (w1a_ref, w1b_ref, w1c_ref, w1d_ref)
    tiles = [ref[:, at : at + 256] for ref in parts for at in (0, 256)]
    pre = dot(rows, tiles[0])
    held = None
    for step, weight in enumerate(tiles):
        following = dot(rows, tiles[step + 1]) if step + 1 < len(tiles) else None
        if step == 4:
            logits = dot_nt(w_router, rows)
            raised = jnp.exp(logits - jnp.max(logits, axis=0, keepdims=True))
            prob = raised / jnp.sum(raised, axis=0, keepdims=True)
            mine = iota((EXPERTS, BLOCK), 0) == expert_ref[0]
            scale = kept_ref[...] * jnp.sum(jnp.where(mine, prob, 0.0), axis=0, keepdims=True)
            scale_ref[...] = scale
            scale_col = jnp.broadcast_to(scale, (8, BLOCK)).T[:, 0:1]
        span = slice(step * 256, step * 256 + 256)
        square = pre * pre
        half = 0.5 * jnp.tanh(pre * (square * (GELU_A * GELU_C) + GELU_C)) + 0.5
        act = pre * half
        slope = half + act * (1.0 - half) * (square * (6.0 * GELU_A * GELU_C) + 2.0 * GELU_C)
        upstream = gw_ref[:, span].astype(f32)
        product = upstream * act
        dgate = dgate + product[:, 0:128] + product[:, 128:256]
        dpre = (upstream * slope).astype(bf16)
        act_ref[:, span] = act.astype(bf16)
        dpre_ref[:, span] = dpre
        if held is not None:
            dslot = dslot + dot_nt(*held)
        held = dpre, weight
        pre = following
    dslot = dslot + dot_nt(*held)
    dgate = jnp.sum(dgate.T, axis=0, keepdims=True)
    dprob = dgate * (mine.astype(f32) - prob)
    dprob_ref[...] = dprob.astype(bf16)
    dslot = dslot * scale_col + dot_tn((scale * dprob).astype(bf16), w_router)
    dslot_ref[...] = dslot.astype(bf16).reshape(BLOCK // MOST, MOST, D)


def weight_kernel(
    x_ref,
    grad_ref,
    scale_ref,
    act_ref,
    dpre_ref,
    dprob_ref,
    w2a_ref,
    w2b_ref,
    w2c_ref,
    w2d_ref,
    y_ref,
    rows_ref,
    back_ref,
    down_ref,
    far_ref,
    up_ref,
    d_router_ref,
    w2_ref,
    total_ref,
):
    step = pl.program_id(0)

    @pl.when(step == 0)
    def _():
        for at in range(0, SLOTS, 512):
            one = slice(at // MOST, at // MOST + 8)
            here = slice(at, at + 512)
            scale = scale_ref[:, here]
            rows_ref[:, here] = (x_ref[one].reshape(512, D).astype(f32).T * scale).astype(bf16)
            back_ref[:, here] = (
                grad_ref[one, 0:MOST, :].reshape(512, D).astype(f32).T * scale
            ).astype(bf16)
        d_router_ref[...] = dot_nt(rows_ref[...], dprob_ref[...])
        for part, part_ref in enumerate((w2a_ref, w2b_ref, w2c_ref, w2d_ref)):
            w2_ref[part] = part_ref[...]
        total_ref[...] = jnp.zeros_like(total_ref)

    total_ref[...] += dot(act_ref[...], w2_ref[step])

    @pl.when(step > 0)
    def _():
        d_in = dot(rows_ref[...], dpre_ref[...]).astype(bf16)
        d_out = dot(back_ref[...], act_ref[...]).T.astype(bf16)
        for part, out_ref in enumerate((down_ref, far_ref, up_ref)):

            @pl.when(step == part + 1)
            def _():
                out_ref[0] = d_in
                out_ref[1] = d_out

    @pl.when(step == N_Z - 1)
    def _():
        for at in range(0, SLOTS, 512):
            one = slice(at // MOST, at // MOST + 8)
            here = slice(at, at + 512)
            scale_col = jnp.broadcast_to(scale_ref[:, here], (8, 512)).T[:, 0:1]
            y_ref[one] = (total_ref[here, :] * scale_col).astype(bf16).reshape(8, MOST, D)


def gather_slots(cols_ref, rows_ref):
    pos0 = cols_ref[:, 0:1].astype(jnp.int32)
    pos1 = cols_ref[:, 1:2].astype(jnp.int32)
    total = jnp.zeros((ROWS, D), f32)
    for part in range(4):
        spot = iota((ROWS, 512), 1) + part * 512
        hot = jnp.logical_or(spot == pos0, spot == pos1).astype(f32).astype(bf16)
        total = total + dot(hot, rows_ref[part * 8 : part * 8 + 8].reshape(512, D))
    return total


def backward_kernel(
    dslot_ref,
    cols_ref,
    seg_ref,
    tokens_ref,
    cot_ref,
    residual_ref,
    packed_ref,
    attended_ref,
    lse_ref,
    gain1_ref,
    bias1_ref,
    w_qkv_ref,
    w_out_ref,
    gain2_ref,
    d_router_ref,
    core_ref,
    keep_ref,
    send_ref,
    d_tokens_ref,
    datt_ref,
    dpacked_ref,
    dkey_ref,
    dvalue_ref,
    grads_ref,
    wide_ref,
):
    d_second = gather_slots(cols_ref, dslot_ref)
    normal2, factor2 = normalize(residual_ref[...])
    d_norm2, d_gain2, d_shift2 = norm_backward(d_second, normal2, factor2, gain2_ref[...])
    d_residual = cot_ref[...].astype(f32) + d_norm2
    d_tokens_ref[...] = d_residual
    d_branch = d_residual.astype(bf16)
    grads_ref[:, 3 * D : 4 * D] = dot_tn(attended_ref[...], d_branch).astype(bf16)
    datt_ref[...] = dot_nt(d_branch, w_out_ref[...]).astype(bf16)
    lanes = iota((128, 128), 1)
    for pair in range(4):
        at = pair * 128
        dkey_ref[...] = jnp.zeros_like(dkey_ref)
        dvalue_ref[...] = jnp.zeros_like(dvalue_ref)
        for block in range(4):
            here = slice(block * 128, block * 128 + 128)
            window = slice(STARTS[block], STARTS[block] + 256)
            bias = band_bias(cols_ref, seg_ref, block)
            query = stacked(packed_ref[here, at : at + 128])
            upstream = stacked(datt_ref[here, at : at + 128])
            keys = packed_ref[window, D + at : D + at + 128]
            values = packed_ref[window, 2 * D + at : 2 * D + at + 128]
            logsum = jnp.concatenate(
                [
                    lse_ref[here, 2 * pair : 2 * pair + 1],
                    lse_ref[here, 2 * pair + 1 : 2 * pair + 2],
                ],
                axis=0,
            )
            weights = jnp.exp(dot_nt(query, keys) * SCALE + bias - logsum)
            d_weights = dot_nt(upstream, values)
            inner = jnp.sum(weights * d_weights, axis=-1, keepdims=True)
            d_scores = (weights * (d_weights - inner)).astype(bf16)
            d_query = dot(d_scores, keys) * SCALE
            dpacked_ref[here, at : at + 128] = jnp.where(
                lanes < HDIM, d_query[0:128], d_query[128:256]
            ).astype(bf16)
            dkey_ref[window, :] += dot_tn(d_scores, query)
            dvalue_ref[window, :] += dot_tn(weights.astype(bf16), upstream)
        dpacked_ref[:, D + at : D + at + 128] = (dkey_ref[...] * SCALE).astype(bf16)
        dpacked_ref[:, 2 * D + at : 2 * D + at + 128] = dvalue_ref[...].astype(bf16)
    normal1, factor1 = normalize(tokens_ref[...].astype(f32))
    first = (normal1 * gain1_ref[...] + bias1_ref[...]).astype(bf16)
    for part in range(3):
        grads_ref[:, part * D : (part + 1) * D] = dot_tn(
            first, dpacked_ref[:, part * D : (part + 1) * D]
        ).astype(bf16)
    d_first = dot_nt(dpacked_ref[...], w_qkv_ref[...])
    d_norm1, d_gain1, d_shift1 = norm_backward(d_first, normal1, factor1, gain1_ref[...])
    d_tokens_ref[...] += d_norm1
    wide_ref[...] = jnp.zeros_like(wide_ref)
    wide_ref[0:1, :] = d_gain1
    wide_ref[1:2, :] = d_shift1
    wide_ref[2:3, :] = d_gain2
    wide_ref[3:4, :] = d_shift2
    grads_ref[:, 4 * D + 128 :] = jnp.zeros((ROWS, 128), bf16)
    grads_ref[:, 4 * D : 4 * D + 128] = wide_ref[...].T.astype(bf16)
    grads_ref[:, 4 * D + EXPERTS : 4 * D + 2 * EXPERTS] = d_router_ref[...].astype(bf16)
    core = core_ref[0]
    for half in range(2):
        span = slice(half * WIDTH, half * WIDTH + WIDTH)
        keep_ref[half] = grads_ref[pl.ds(pl.multiple_of(core * 256, 256), 256), span]
        send_ref[half] = grads_ref[pl.ds(pl.multiple_of((1 - core) * 256, 256), 256), span]


def finish_kernel(which_ref, half_ref, *refs):
    qkv_ref, out_ref, router_ref, *norm_refs = refs[-7:]
    split = 3 * D - WIDTH
    qkv_ref[:, 0:WIDTH] = half_ref[0].astype(f32)
    qkv_ref[:, WIDTH:] = half_ref[1, :, 0:split].astype(f32)
    out_ref[...] = half_ref[1, :, split : split + D].astype(f32)
    lines = half_ref[1, :, split + D : split + D + 128].astype(f32).T
    router_ref[...] = lines[EXPERTS : 2 * EXPERTS]
    for row, norm_ref in enumerate(norm_refs):
        norm_ref[...] = lines[row : row + 1]


def output_kernel(y_ref, cols_ref, residual_ref, out_ref):
    out_ref[...] = (residual_ref[...] + gather_slots(cols_ref, y_ref)).astype(bf16)


def own_kernel(
    rows_ref, back_ref, act_ref, dpre_ref, above_ref, below_ref, token_ref, d_in_ref, d_out_ref
):
    for half, out_ref in enumerate((d_in_ref, d_out_ref)):
        out_ref[0] = above_ref[half].astype(f32) + below_ref[half].astype(f32)
    d_in_ref[0] += dot(rows_ref[...], dpre_ref[...])
    d_out_ref[0] += dot(back_ref[...], act_ref[...]).T


def across_kernel(d_in_ref, d_out_ref, across_ref, token_ref, sum_in_ref, sum_out_ref):
    sum_in_ref[0] = d_in_ref[0] + across_ref[0].astype(f32)
    sum_out_ref[0] = d_out_ref[0] + across_ref[1].astype(f32)


def params(mib):
    return pltpu.CompilerParams(vmem_limit_bytes=mib * MIB)


def after(values, *tokens, flops=0):
    anywhere = pl.BlockSpec(memory_space=pl.ANY)
    return pl.pallas_call(
        lambda *refs: None,
        in_specs=[anywhere] * (1 + len(tokens)),
        out_specs=anywhere,
        out_shape=shape(values.shape, values.dtype),
        input_output_aliases={0: 0},
        cost_estimate=pl.CostEstimate(flops=flops, bytes_accessed=0, transcendentals=0),
    )(values, *tokens)


def call(kernel, mib, out_shape, *args, flops=0, scratch=()):
    shapes = jax.tree.leaves(out_shape)
    moved = sum(a.size * a.dtype.itemsize for a in args) + sum(
        s.size * s.dtype.itemsize for s in shapes
    )
    return pl.pallas_call(
        kernel,
        out_shape=out_shape,
        scratch_shapes=list(scratch),
        compiler_params=params(mib),
        cost_estimate=pl.CostEstimate(flops=flops, bytes_accessed=moved, transcendentals=0),
    )(*args)


def shape(dims, dtype):
    return jax.ShapeDtypeStruct(dims, dtype)


DP = ("x", "y", "core")
CHIPS = ("x", "y")
SWAP = [(0, 1), (1, 0)]


def ring(distance):
    return [(i, (i + distance) % 4) for i in range(4)]


def exchange(values, axes):
    return lax.all_to_all(values, axes, split_axis=0, concat_axis=0, tiled=True)


def add_cores(keep, send, token):
    got = lax.ppermute(send, "core", SWAP)
    return after((keep.astype(f32) + got.astype(f32)).astype(bf16), token)


def sum_chips(low, *tokens):
    parts = exchange(low.reshape(16, 32, WIDTH), CHIPS)
    low = after(jnp.sum(parts.astype(f32), axis=0).astype(bf16), *tokens)
    got = [lax.ppermute(low, "z", ring(d)).astype(f32) for d in (1, 2, 3)]
    low = ((low.astype(f32) + got[1]) + (got[0] + got[2])).astype(bf16)
    low = exchange(jnp.broadcast_to(low[None], (16, 32, WIDTH)), CHIPS).reshape(2, 256, WIDTH)
    return low, lax.ppermute(low, "core", SWAP)


def per_device(
    tokens,
    segments,
    routes,
    priority,
    ln1_gain,
    ln1_bias,
    w_qkv,
    w_out,
    ln2_gain,
    ln2_bias,
    w_router,
    expert_in,
    expert_out,
    cotangent,
):
    gain1, bias1 = ln1_gain.reshape(1, D), ln1_bias.reshape(1, D)
    gain2, bias2 = ln2_gain.reshape(1, D), ln2_bias.reshape(1, D)
    w2_up = lax.ppermute(expert_out[0], "z", ring(1))
    w2_down = lax.ppermute(expert_out[0], "z", ring(3))
    w2_far = lax.ppermute(w2_down, "z", ring(3))
    w2 = [expert_out[0], w2_up, w2_far, w2_down]
    w1_up = lax.ppermute(expert_in[0], "z", ring(1))

    send_grad, csel, cols = call(
        pack_kernel,
        62,
        (
            shape((EXPERTS, MOST + EXTRA, D), bf16),
            shape((EXPERTS, ROWS), f32),
            shape((ROWS, 128), f32),
        ),
        routes.T,
        priority.reshape(1, ROWS),
        segments,
        cotangent,
        flops=2 * SLOTS * D * D,
        scratch=[pltpu.VMEM((128, ROWS), f32)],
    )
    grad = exchange(send_grad, DP)

    packed, attended, lse, residual, send_rows = call(
        attend_kernel,
        62,
        (
            shape((ROWS, 3 * D), bf16),
            shape((ROWS, D), bf16),
            shape((ROWS, 128), f32),
            shape((ROWS, D), f32),
            shape((EXPERTS, MOST, D), bf16),
        ),
        tokens,
        segments,
        cols,
        csel,
        gain1,
        bias1,
        w_qkv,
        w_out,
        gain2,
        bias2,
        flops=2 * SLOTS * D * D + 10 * ROWS * D * D,
    )
    send_rows = after(send_rows, w2_up, w2_far, w2_down, w1_up)
    rows = exchange(send_rows, DP)

    expert = lax.axis_index(DP).astype(jnp.int32).reshape(1)
    digits = grad[:, MOST : MOST + EXTRA, 0:MOST].astype(jnp.int32)
    later = lax.dynamic_index_in_dim(digits, 3 + expert[0] % 4, axis=1, keepdims=False)
    keys = digits[:, 0] + 256 * digits[:, 1] + 65536 * (digits[:, 2] + later)
    keys = keys.reshape(16, 128)
    planes = [lax.ppermute(keys, "z", ring(d)) for d in (1, 2, 3)]
    kept = call(keep_kernel, 62, shape((16, 128), f32), keys, keys, *planes).reshape(1, SLOTS)

    steps = SLOTS // BLOCK
    weight_spec = pl.BlockSpec((D, 512), lambda i: (0, 0))
    row_spec = pl.BlockSpec((BLOCK // MOST, MOST, D), lambda i: (i, 0, 0))
    wide_spec = pl.BlockSpec((BLOCK, 2048), lambda i: (i, 0))
    line_spec = pl.BlockSpec((1, BLOCK), lambda i: (0, i))
    smem = pl.BlockSpec(memory_space=pltpu.SMEM)
    vmem = pl.BlockSpec(memory_space=pltpu.VMEM)
    tie = pl.BlockSpec(memory_space=pl.ANY)
    big = 2 * SLOTS * D * 2048
    back = pl.pallas_call(
        back_kernel,
        grid=(steps,),
        in_specs=[row_spec] + [weight_spec] * 4,
        out_specs=wide_spec,
        out_shape=shape((SLOTS, 2048), bf16),
        compiler_params=params(62),
        cost_estimate=pl.CostEstimate(flops=big, bytes_accessed=12 << 20, transcendentals=0),
    )(grad, *w2)
    w1_down = lax.ppermute(expert_in[0], "z", ring(3))
    w1_far = lax.ppermute(w1_up, "z", ring(1))
    w1 = [expert_in[0], w1_up, w1_far, w1_down]
    dslot, act, dpre, scale, dprob = pl.pallas_call(
        slot_kernel,
        grid=(steps,),
        in_specs=[
            smem,
            row_spec,
            wide_spec,
        ]
        + [weight_spec] * 4
        + [
            line_spec,
            pl.BlockSpec((EXPERTS, D), lambda i: (0, 0)),
        ],
        out_specs=[
            row_spec,
            wide_spec,
            wide_spec,
            line_spec,
            pl.BlockSpec((EXPERTS, BLOCK), lambda i: (0, i)),
        ],
        out_shape=(
            shape((EXPERTS, MOST, D), bf16),
            shape((SLOTS, 2048), bf16),
            shape((SLOTS, 2048), bf16),
            shape((1, SLOTS), f32),
            shape((EXPERTS, SLOTS), bf16),
        ),
        compiler_params=params(62),
        cost_estimate=pl.CostEstimate(
            flops=2 * big, bytes_accessed=32 << 20, transcendentals=SLOTS * 2048
        ),
    )(expert, rows, back, *w1, kept, w_router.T)
    dslot_home = after(exchange(dslot, DP), flops=60 * 10**9)

    whole = pl.BlockSpec((EXPERTS, MOST, D), lambda i: (0, 0, 0))
    slices = pl.BlockSpec((SLOTS, 512), lambda i: (0, i))
    y, rows_t, back_t, *d_weights, d_router = pl.pallas_call(
        weight_kernel,
        grid=(N_Z,),
        in_specs=[
            whole,
            whole,
            pl.BlockSpec((1, SLOTS), lambda i: (0, 0)),
            slices,
            slices,
            pl.BlockSpec((EXPERTS, SLOTS), lambda i: (0, 0)),
        ]
        + [weight_spec] * 4,
        out_specs=[whole]
        + [pl.BlockSpec((D, SLOTS), lambda i: (0, 0))] * 2
        + [pl.BlockSpec((2, D, 512), lambda i: (0, 0, 0))] * 3
        + [pl.BlockSpec((D, EXPERTS), lambda i: (0, 0))],
        out_shape=(shape((EXPERTS, MOST, D), bf16),)
        + (shape((D, SLOTS), bf16),) * 2
        + (shape((2, D, 512), bf16),) * 3
        + (shape((D, EXPERTS), f32),),
        scratch_shapes=[
            pltpu.VMEM((N_Z, 512, D), bf16),
            pltpu.VMEM((SLOTS, D), f32),
        ],
        compiler_params=params(62),
        cost_estimate=pl.CostEstimate(flops=0, bytes_accessed=0, transcendentals=0),
    )(rows, grad, scale, act, dpre, dprob, *w2)
    y_home = exchange(y, DP)

    down, far, up = d_weights
    received = [
        lax.ppermute(down, "z", ring(3)),
        lax.ppermute(far, "z", ring(2)),
        lax.ppermute(up, "z", ring(1)),
    ]

    core = lax.axis_index("core").astype(jnp.int32).reshape(1)
    keep, send, d_tokens = pl.pallas_call(
        backward_kernel,
        in_specs=[vmem] * 15 + [smem],
        out_shape=(
            shape((2, ROWS // 2, WIDTH), bf16),
            shape((2, ROWS // 2, WIDTH), bf16),
            shape((ROWS, D), f32),
        ),
        scratch_shapes=[
            pltpu.VMEM((ROWS, D), bf16),
            pltpu.VMEM((ROWS, 3 * D), bf16),
            pltpu.VMEM((ROWS, 128), f32),
            pltpu.VMEM((ROWS, 128), f32),
            pltpu.VMEM((ROWS, 2 * WIDTH), bf16),
            pltpu.VMEM((128, ROWS), f32),
        ],
        compiler_params=params(62),
        cost_estimate=pl.CostEstimate(
            flops=3000000000, bytes_accessed=0, transcendentals=0
        ),
    )(
        dslot_home,
        cols,
        segments,
        tokens,
        cotangent,
        residual,
        packed,
        attended,
        lse,
        gain1,
        bias1,
        w_qkv,
        w_out,
        gain2,
        d_router,
        core,
    )
    low = add_cores(keep, after(send, received[0], received[2]), y_home)
    output = call(output_kernel, 62, shape((ROWS, D), bf16), y_home, cols, residual)
    fixed = pl.BlockSpec((D, SLOTS), lambda i: (0, 0))
    slices = pl.BlockSpec((SLOTS, 512), lambda i: (0, 0))
    d_in, d_out = pl.pallas_call(
        own_kernel,
        grid=(1,),
        in_specs=[fixed, fixed, slices, slices]
        + [pl.BlockSpec((2, D, 512), lambda i: (0, 0, 0))] * 2
        + [tie],
        out_specs=[pl.BlockSpec((1, D, 512), lambda i: (0, 0, 0))] * 2,
        out_shape=(shape((1, D, 512), f32), shape((1, 512, D), f32)),
        compiler_params=params(62),
        cost_estimate=pl.CostEstimate(flops=0, bytes_accessed=0, transcendentals=0),
    )(rows_t, back_t, act, dpre, received[0], received[2], low)
    d_in, d_out = pl.pallas_call(
        across_kernel,
        in_specs=[vmem] * 3 + [tie],
        out_shape=(shape((1, D, 512), f32), shape((1, 512, D), f32)),
        compiler_params=params(62),
        cost_estimate=pl.CostEstimate(flops=6 * 10**9, bytes_accessed=0, transcendentals=0),
    )(d_in, d_out, received[1], output)
    low, other = sum_chips(low, d_in)
    whole_half = pl.BlockSpec((2, ROWS // 2, WIDTH), lambda i, which: (0, 0, 0))
    down = lambda i, which: (which[0], 0)
    across = lambda i, which: (0, which[0])

    def finish(which, half, *earlier):
        return pl.pallas_call(
            finish_kernel,
            grid_spec=pltpu.PrefetchScalarGridSpec(
                num_scalar_prefetch=1,
                grid=(1,),
                in_specs=[whole_half] + [tie] * len(earlier),
                out_specs=[
                    pl.BlockSpec((ROWS // 2, 3 * D), down),
                    pl.BlockSpec((ROWS // 2, D), down),
                    pl.BlockSpec((EXPERTS, ROWS // 2), across),
                ]
                + [pl.BlockSpec((1, ROWS // 2), across)] * 4,
            ),
            out_shape=(shape((D, 3 * D), f32), shape((D, D), f32), shape((EXPERTS, D), f32))
            + (shape((1, D), f32),) * 4,
            input_output_aliases={2 + i: i for i in range(len(earlier))},
            compiler_params=params(62),
            cost_estimate=pl.CostEstimate(flops=0, bytes_accessed=0, transcendentals=0),
        )(which, half, *earlier)

    d_w_qkv, d_w_out, d_w_router, *norms = finish(1 - core, other, *finish(core, low))
    return (
        output,
        d_tokens,
        norms[0].reshape(D),
        norms[1].reshape(D),
        d_w_qkv,
        d_w_out,
        norms[2].reshape(D),
        norms[3].reshape(D),
        d_w_router.T,
        d_in,
        d_out,
    )


def solution(mesh):
    fine = Mesh(mesh.devices.reshape(4, 4, 4, 2), ("z", "x", "y", "core"))
    every = ("z", "x", "y", "core")
    both = P(every, None)
    in_specs = (
        both,
        both,
        both,
        P(every),
        P(),
        P(),
        P(),
        P(),
        P(),
        P(),
        P(),
        P(DP, None, "z"),
        P(DP, "z", None),
        both,
    )
    out_specs = (
        both,
        both,
        P(),
        P(),
        P(),
        P(),
        P(),
        P(),
        P(),
        P(DP, None, "z"),
        P(DP, "z", None),
    )
    return jax.shard_map(
        per_device, mesh=fine, in_specs=in_specs, out_specs=out_specs, check_vma=False
    )
```

```python
import functools

import jax
import jax.numpy as jnp
from jax import lax
from jax.experimental import pallas as pl
from jax.experimental.pallas import tpu as pltpu
from jax.sharding import Mesh
from jax.sharding import PartitionSpec as P

D = 512
HEADS = 8
HDIM = 64
EXPERTS = 32
MOST = 64
ROWS = 512
SLOTS = EXPERTS * MOST
N_Z = 4
N_DP = 32
CAP = (21 * N_Z * N_DP * ROWS + 319) // 320
TOKENS = N_Z * N_DP * ROWS
EXTRA = 8
BLOCK = 512
WIDTH = 4 * D + 128
EPS = 1e-06
SCALE = HDIM ** (-0.5)
STARTS = (0, 64, 192, 256)
GELU_C = 0.7978845608028654
GELU_A = 0.044715

bf16 = jnp.bfloat16
f32 = jnp.float32
MIB = 1024 * 1024


def dot(a, b):
    return lax.dot_general(a, b, (((1,), (0,)), ((), ())), preferred_element_type=f32)


def dot_nt(a, b):
    return lax.dot_general(a, b, (((1,), (1,)), ((), ())), preferred_element_type=f32)


def dot_tn(a, b):
    return lax.dot_general(a, b, (((0,), (0,)), ((), ())), preferred_element_type=f32)


def iota(shape, dim):
    return lax.broadcasted_iota(jnp.int32, shape, dim)


def normalize(values):
    center = values - jnp.mean(values, axis=-1, keepdims=True)
    factor = lax.rsqrt(jnp.mean(center * center, axis=-1, keepdims=True) + EPS)
    return center * factor, factor


def norm_backward(upstream, normal, factor, gain):
    scaled = upstream * gain
    inner = (
        scaled
        - jnp.mean(scaled, axis=-1, keepdims=True)
        - normal * jnp.mean(scaled * normal, axis=-1, keepdims=True)
    )
    return (
        inner * factor,
        jnp.sum(upstream * normal, axis=0, keepdims=True),
        jnp.sum(upstream, axis=0, keepdims=True),
    )


def pick_rows(csel_ref, rows, store):
    place = iota((MOST, ROWS), 0).astype(f32)
    for group in range(EXPERTS // 4):
        parts = []
        for j in range(4):
            line = csel_ref[group * 4 + j : group * 4 + j + 1, :]
            parts.append((place == line).astype(f32).astype(bf16))
        hot = jnp.concatenate(parts, axis=0)
        store(group, dot(hot, rows).astype(bf16))


def pack_kernel(routes_ref, prio_ref, seg_ref, cot_ref, send_ref, csel_ref, cols_ref, wide_ref):
    routes = routes_ref[...]
    experts = iota((EXPERTS, ROWS), 0)
    first = routes[0:1] == experts
    second = routes[1:2] == experts
    either = jnp.logical_or(first, second)
    before = (iota((ROWS, ROWS), 0) < iota((ROWS, ROWS), 1)).astype(f32).astype(bf16)
    count = dot(either.astype(f32).astype(bf16), before)
    slot = count + (experts * MOST).astype(f32)
    wide_ref[...] = jnp.zeros_like(wide_ref)
    wide_ref[0:1, :] = jnp.sum(jnp.where(first, slot, 0.0), axis=0, keepdims=True)
    wide_ref[1:2, :] = jnp.sum(jnp.where(second, slot, 0.0), axis=0, keepdims=True)
    wide_ref[2:3, :] = prio_ref[...].astype(f32)
    wide_ref[3:4, :] = seg_ref[...].astype(f32)
    csel_ref[...] = jnp.where(either, count, -1.0)
    cols = wide_ref[...].T
    cols_ref[...] = cols
    key = prio_ref[...] + 1
    digits = [
        jnp.bitwise_and(key, 255),
        jnp.bitwise_and(jnp.right_shift(key, 8), 255),
        jnp.right_shift(key, 16),
    ]
    digits = [line.astype(f32) for line in digits]
    later = second.astype(f32)
    empty = jnp.zeros((1, ROWS), f32)
    zeros = jnp.zeros((EXTRA, D), bf16)
    rows = cot_ref[...]
    place = iota((MOST, ROWS), 0).astype(f32)
    for group in range(EXPERTS // 4):
        four = range(group * 4, group * 4 + 4)
        hot = jnp.concatenate(
            [(place == csel_ref[e : e + 1, :]).astype(f32).astype(bf16) for e in four], axis=0
        )
        picked = dot(hot, rows).astype(bf16)
        send_ref[group * 4 : group * 4 + 4, 0:MOST, :] = picked.reshape(4, MOST, D)
        lines = jnp.concatenate(digits + [later[e : e + 1] for e in four] + [empty], axis=0)
        keys = dot_nt(lines.astype(bf16), hot)
        for j, e in enumerate(four):
            send_ref[e, MOST : MOST + EXTRA, :] = zeros
            send_ref[e, MOST : MOST + EXTRA, 0:MOST] = keys[
                :, j * MOST : (j + 1) * MOST
            ].astype(bf16)


def stacked(pair):
    lanes = iota(pair.shape, 1)
    zero = jnp.zeros_like(pair)
    return jnp.concatenate(
        [jnp.where(lanes < HDIM, pair, zero), jnp.where(lanes >= HDIM, pair, zero)], axis=0
    )


def band_bias(cols_ref, seg_ref, block):
    start = STARTS[block]
    same = (
        cols_ref[block * 128 : block * 128 + 128, 3:4]
        == seg_ref[:, start : start + 256].astype(f32)
    )
    bias = jnp.where(same, 0.0, -1e30)
    return jnp.concatenate([bias, bias], axis=0)


def attend_kernel(
    tokens_ref,
    seg_ref,
    cols_ref,
    csel_ref,
    gain1_ref,
    bias1_ref,
    w_qkv_ref,
    w_out_ref,
    gain2_ref,
    bias2_ref,
    packed_ref,
    attended_ref,
    lse_ref,
    residual_ref,
    send_ref,
):
    inputs = tokens_ref[...].astype(f32)
    normal, _ = normalize(inputs)
    first = (normal * gain1_ref[...] + bias1_ref[...]).astype(bf16)
    for part in range(3):
        packed_ref[:, part * D : (part + 1) * D] = dot(
            first, w_qkv_ref[:, part * D : (part + 1) * D]
        ).astype(bf16)
    lanes = iota((128, 128), 1)
    for block in range(4):
        here = slice(block * 128, block * 128 + 128)
        window = slice(STARTS[block], STARTS[block] + 256)
        bias = band_bias(cols_ref, seg_ref, block)
        lse = jnp.zeros((128, 128), f32)
        for pair in range(4):
            at = pair * 128
            query = stacked(packed_ref[here, at : at + 128])
            scores = dot_nt(query, packed_ref[window, D + at : D + at + 128]) * SCALE + bias
            highest = jnp.max(scores, axis=-1, keepdims=True)
            raised = jnp.exp(scores - highest)
            total = jnp.sum(raised, axis=-1, keepdims=True)
            weights = (raised * (1.0 / total)).astype(bf16)
            mixed = dot(weights, packed_ref[window, 2 * D + at : 2 * D + at + 128])
            attended_ref[here, at : at + 128] = jnp.where(
                lanes < HDIM, mixed[0:128], mixed[128:256]
            ).astype(bf16)
            logsum = highest + jnp.log(total)
            lse = jnp.where(lanes == 2 * pair, logsum[0:128], lse)
            lse = jnp.where(lanes == 2 * pair + 1, logsum[128:256], lse)
        lse_ref[here, :] = lse
    residual = inputs + dot(attended_ref[...], w_out_ref[...])
    residual_ref[...] = residual
    normal2, _ = normalize(residual)
    second = (normal2 * gain2_ref[...] + bias2_ref[...]).astype(bf16)

    def store(group, rows):
        send_ref[group * 4 : group * 4 + 4] = rows.reshape(4, MOST, D)

    pick_rows(csel_ref, second, store)


def keep_kernel(own_ref, a_ref, b_ref, c_ref, d_ref, kept_ref):
    empty = 2 * TOKENS + 1
    keys = jnp.concatenate([a_ref[...], b_ref[...], c_ref[...], d_ref[...]], axis=0)
    keys = jnp.where(keys == 0, empty, keys)

    def step(_, bounds):
        low, high = bounds
        middle = jnp.right_shift(low + high, 1)
        enough = jnp.sum((keys <= middle).astype(jnp.int32), keepdims=True) >= CAP
        return jnp.where(enough, low, middle + 1), jnp.where(enough, middle, high)

    low = jnp.zeros((1, 1), jnp.int32)
    high = jnp.full((1, 1), 2 * TOKENS, jnp.int32)
    low, high = lax.fori_loop(0, 18, step, (low, high))
    own = own_ref[...]
    kept_ref[...] = jnp.logical_and(own > 0, own <= high).astype(f32)


def back_kernel(grad_ref, *refs):
    *w2_refs, out_ref = refs
    rows = grad_ref[...].reshape(BLOCK, D)
    for part, w2_ref in enumerate(w2_refs):
        out_ref[:, part * 512 : part * 512 + 512] = dot_nt(rows, w2_ref[...]).astype(bf16)


def slot_kernel(
    expert_ref,
    x_ref,
    gw_ref,
    w1a_ref,
    w1b_ref,
    w1c_ref,
    w1d_ref,
    kept_ref,
    w_router_ref,
    dslot_ref,
    act_ref,
    dpre_ref,
    scale_ref,
    dprob_ref,
):
    rows = x_ref[...].reshape(BLOCK, D)
    w_router = w_router_ref[...]
    dslot = jnp.zeros((BLOCK, D), f32)
    dgate = jnp.zeros((BLOCK, 128), f32)
    parts = (w1a_ref, w1b_ref, w1c_ref, w1d_ref)
    tiles = [ref[:, at : at + 256] for ref in parts for at in (0, 256)]
    pre = dot(rows, tiles[0])
    held = None
    for step, weight in enumerate(tiles):
        following = dot(rows, tiles[step + 1]) if step + 1 < len(tiles) else None
        if step == 4:
            logits = dot_nt(w_router, rows)
            raised = jnp.exp(logits - jnp.max(logits, axis=0, keepdims=True))
            prob = raised / jnp.sum(raised, axis=0, keepdims=True)
            mine = iota((EXPERTS, BLOCK), 0) == expert_ref[0]
            scale = kept_ref[...] * jnp.sum(jnp.where(mine, prob, 0.0), axis=0, keepdims=True)
            scale_ref[...] = scale
            scale_col = jnp.broadcast_to(scale, (8, BLOCK)).T[:, 0:1]
        span = slice(step * 256, step * 256 + 256)
        square = pre * pre
        half = 0.5 * jnp.tanh(pre * (square * (GELU_A * GELU_C) + GELU_C)) + 0.5
        act = pre * half
        slope = half + act * (1.0 - half) * (square * (6.0 * GELU_A * GELU_C) + 2.0 * GELU_C)
        upstream = gw_ref[:, span].astype(f32)
        product = upstream * act
        dgate = dgate + product[:, 0:128] + product[:, 128:256]
        dpre = (upstream * slope).astype(bf16)
        act_ref[:, span] = act.astype(bf16)
        dpre_ref[:, span] = dpre
        if held is not None:
            dslot = dslot + dot_nt(*held)
        held = dpre, weight
        pre = following
    dslot = dslot + dot_nt(*held)
    dgate = jnp.sum(dgate.T, axis=0, keepdims=True)
    dprob = dgate * (mine.astype(f32) - prob)
    dprob_ref[...] = dprob.astype(bf16)
    dslot = dslot * scale_col + dot_tn((scale * dprob).astype(bf16), w_router)
    dslot_ref[...] = dslot.astype(bf16).reshape(BLOCK // MOST, MOST, D)


def weight_kernel(
    x_ref,
    grad_ref,
    scale_ref,
    act_ref,
    dpre_ref,
    dprob_ref,
    w2a_ref,
    w2b_ref,
    w2c_ref,
    w2d_ref,
    y_ref,
    rows_ref,
    back_ref,
    down_ref,
    far_ref,
    up_ref,
    d_router_ref,
    w2_ref,
    total_ref,
):
    step = pl.program_id(0)

    @pl.when(step == 0)
    def _():
        for at in range(0, SLOTS, 512):
            one = slice(at // MOST, at // MOST + 8)
            here = slice(at, at + 512)
            scale = scale_ref[:, here]
            rows_ref[:, here] = (x_ref[one].reshape(512, D).astype(f32).T * scale).astype(bf16)
            back_ref[:, here] = (
                grad_ref[one, 0:MOST, :].reshape(512, D).astype(f32).T * scale
            ).astype(bf16)
        d_router_ref[...] = dot_nt(rows_ref[...], dprob_ref[...])
        for part, part_ref in enumerate((w2a_ref, w2b_ref, w2c_ref, w2d_ref)):
            w2_ref[part] = part_ref[...]
        total_ref[...] = jnp.zeros_like(total_ref)

    total_ref[...] += dot(act_ref[...], w2_ref[step])

    @pl.when(step > 0)
    def _():
        d_in = dot(rows_ref[...], dpre_ref[...]).astype(bf16)
        d_out = dot(back_ref[...], act_ref[...]).T.astype(bf16)
        for part, out_ref in enumerate((down_ref, far_ref, up_ref)):

            @pl.when(step == part + 1)
            def _():
                out_ref[0] = d_in
                out_ref[1] = d_out

    @pl.when(step == N_Z - 1)
    def _():
        for at in range(0, SLOTS, 512):
            one = slice(at // MOST, at // MOST + 8)
            here = slice(at, at + 512)
            scale_col = jnp.broadcast_to(scale_ref[:, here], (8, 512)).T[:, 0:1]
            y_ref[one] = (total_ref[here, :] * scale_col).astype(bf16).reshape(8, MOST, D)


def gather_slots(cols_ref, rows_ref):
    pos0 = cols_ref[:, 0:1].astype(jnp.int32)
    pos1 = cols_ref[:, 1:2].astype(jnp.int32)
    total = jnp.zeros((ROWS, D), f32)
    for part in range(4):
        spot = iota((ROWS, 512), 1) + part * 512
        hot = jnp.logical_or(spot == pos0, spot == pos1).astype(f32).astype(bf16)
        total = total + dot(hot, rows_ref[part * 8 : part * 8 + 8].reshape(512, D))
    return total


def backward_kernel(
    dslot_ref,
    cols_ref,
    seg_ref,
    tokens_ref,
    cot_ref,
    residual_ref,
    packed_ref,
    attended_ref,
    lse_ref,
    gain1_ref,
    bias1_ref,
    w_qkv_ref,
    w_out_ref,
    gain2_ref,
    d_router_ref,
    core_ref,
    keep_ref,
    send_ref,
    d_tokens_ref,
    datt_ref,
    dpacked_ref,
    dkey_ref,
    dvalue_ref,
    grads_ref,
    wide_ref,
):
    d_second = gather_slots(cols_ref, dslot_ref)
    normal2, factor2 = normalize(residual_ref[...])
    d_norm2, d_gain2, d_shift2 = norm_backward(d_second, normal2, factor2, gain2_ref[...])
    d_residual = cot_ref[...].astype(f32) + d_norm2
    d_tokens_ref[...] = d_residual
    d_branch = d_residual.astype(bf16)
    grads_ref[:, 3 * D : 4 * D] = dot_tn(attended_ref[...], d_branch).astype(bf16)
    datt_ref[...] = dot_nt(d_branch, w_out_ref[...]).astype(bf16)
    lanes = iota((128, 128), 1)
    for pair in range(4):
        at = pair * 128
        dkey_ref[...] = jnp.zeros_like(dkey_ref)
        dvalue_ref[...] = jnp.zeros_like(dvalue_ref)
        for block in range(4):
            here = slice(block * 128, block * 128 + 128)
            window = slice(STARTS[block], STARTS[block] + 256)
            bias = band_bias(cols_ref, seg_ref, block)
            query = stacked(packed_ref[here, at : at + 128])
            upstream = stacked(datt_ref[here, at : at + 128])
            keys = packed_ref[window, D + at : D + at + 128]
            values = packed_ref[window, 2 * D + at : 2 * D + at + 128]
            logsum = jnp.concatenate(
                [
                    lse_ref[here, 2 * pair : 2 * pair + 1],
                    lse_ref[here, 2 * pair + 1 : 2 * pair + 2],
                ],
                axis=0,
            )
            weights = jnp.exp(dot_nt(query, keys) * SCALE + bias - logsum)
            d_weights = dot_nt(upstream, values)
            inner = jnp.sum(weights * d_weights, axis=-1, keepdims=True)
            d_scores = (weights * (d_weights - inner)).astype(bf16)
            d_query = dot(d_scores, keys) * SCALE
            dpacked_ref[here, at : at + 128] = jnp.where(
                lanes < HDIM, d_query[0:128], d_query[128:256]
            ).astype(bf16)
            dkey_ref[window, :] += dot_tn(d_scores, query)
            dvalue_ref[window, :] += dot_tn(weights.astype(bf16), upstream)
        dpacked_ref[:, D + at : D + at + 128] = (dkey_ref[...] * SCALE).astype(bf16)
        dpacked_ref[:, 2 * D + at : 2 * D + at + 128] = dvalue_ref[...].astype(bf16)
    normal1, factor1 = normalize(tokens_ref[...].astype(f32))
    first = (normal1 * gain1_ref[...] + bias1_ref[...]).astype(bf16)
    for part in range(3):
        grads_ref[:, part * D : (part + 1) * D] = dot_tn(
            first, dpacked_ref[:, part * D : (part + 1) * D]
        ).astype(bf16)
    d_first = dot_nt(dpacked_ref[...], w_qkv_ref[...])
    d_norm1, d_gain1, d_shift1 = norm_backward(d_first, normal1, factor1, gain1_ref[...])
    d_tokens_ref[...] += d_norm1
    wide_ref[...] = jnp.zeros_like(wide_ref)
    wide_ref[0:1, :] = d_gain1
    wide_ref[1:2, :] = d_shift1
    wide_ref[2:3, :] = d_gain2
    wide_ref[3:4, :] = d_shift2
    grads_ref[:, 4 * D :] = wide_ref[...].T.astype(bf16)
    grads_ref[:, 4 * D + EXPERTS : 4 * D + 2 * EXPERTS] = d_router_ref[...].astype(bf16)
    core = core_ref[0]
    keep_ref[...] = grads_ref[pl.ds(pl.multiple_of(core * 256, 256), 256), :]
    send_ref[...] = grads_ref[pl.ds(pl.multiple_of((1 - core) * 256, 256), 256), :]


def finish_kernel(which_ref, half_ref, *refs):
    qkv_ref, out_ref, router_ref, *norm_refs = refs[-7:]
    qkv_ref[...] = half_ref[:, 0 : 3 * D].astype(f32)
    out_ref[...] = half_ref[:, 3 * D : 4 * D].astype(f32)
    lines = half_ref[:, 4 * D :].astype(f32).T
    router_ref[...] = lines[EXPERTS : 2 * EXPERTS]
    for row, norm_ref in enumerate(norm_refs):
        norm_ref[...] = lines[row : row + 1]


def output_kernel(y_ref, cols_ref, residual_ref, out_ref):
    out_ref[...] = (residual_ref[...] + gather_slots(cols_ref, y_ref)).astype(bf16)


def own_kernel(
    rows_ref, back_ref, act_ref, dpre_ref, above_ref, below_ref, token_ref, d_in_ref, d_out_ref
):
    for half, out_ref in enumerate((d_in_ref, d_out_ref)):
        out_ref[0] = above_ref[half].astype(f32) + below_ref[half].astype(f32)
    d_in_ref[0] += dot(rows_ref[...], dpre_ref[...])
    d_out_ref[0] += dot(back_ref[...], act_ref[...]).T


def across_kernel(d_in_ref, d_out_ref, across_ref, sum_in_ref, sum_out_ref):
    sum_in_ref[0] = d_in_ref[0] + across_ref[0].astype(f32)
    sum_out_ref[0] = d_out_ref[0] + across_ref[1].astype(f32)


def params(mib):
    return pltpu.CompilerParams(vmem_limit_bytes=mib * MIB)


def after(values, *tokens, flops=0):
    anywhere = pl.BlockSpec(memory_space=pl.ANY)
    return pl.pallas_call(
        lambda *refs: None,
        in_specs=[anywhere] * (1 + len(tokens)),
        out_specs=anywhere,
        out_shape=shape(values.shape, values.dtype),
        input_output_aliases={0: 0},
        cost_estimate=pl.CostEstimate(flops=flops, bytes_accessed=0, transcendentals=0),
    )(values, *tokens)


def call(kernel, mib, out_shape, *args, flops=0, scratch=()):
    shapes = jax.tree.leaves(out_shape)
    moved = sum(a.size * a.dtype.itemsize for a in args) + sum(
        s.size * s.dtype.itemsize for s in shapes
    )
    return pl.pallas_call(
        kernel,
        out_shape=out_shape,
        scratch_shapes=list(scratch),
        compiler_params=params(mib),
        cost_estimate=pl.CostEstimate(flops=flops, bytes_accessed=moved, transcendentals=0),
    )(*args)


def shape(dims, dtype):
    return jax.ShapeDtypeStruct(dims, dtype)


DP = ("x", "y", "core")
CHIPS = ("x", "y")
SWAP = [(0, 1), (1, 0)]


def ring(distance):
    return [(i, (i + distance) % 4) for i in range(4)]


def exchange(values, axes):
    return lax.all_to_all(values, axes, split_axis=0, concat_axis=0, tiled=True)


def add_cores(keep, send, token):
    got = lax.ppermute(send, "core", SWAP)
    return after((keep.astype(f32) + got.astype(f32)).astype(bf16), token)


def sum_chips(low, early, late):
    parts = exchange(low.reshape(16, 16, WIDTH), CHIPS)
    low = after(jnp.sum(parts.astype(f32), axis=0).astype(bf16), early)
    got = [lax.ppermute(low, "z", ring(d)) for d in (1, 2, 3)]
    got = [after(got[0], late).astype(f32), got[1].astype(f32), got[2].astype(f32)]
    low = ((low.astype(f32) + got[1]) + (got[0] + got[2])).astype(bf16)
    low = exchange(jnp.broadcast_to(low[None], (16, 16, WIDTH)), CHIPS).reshape(256, WIDTH)
    return low, lax.ppermute(low, "core", SWAP)


def per_device(
    tokens,
    segments,
    routes,
    priority,
    ln1_gain,
    ln1_bias,
    w_qkv,
    w_out,
    ln2_gain,
    ln2_bias,
    w_router,
    expert_in,
    expert_out,
    cotangent,
):
    gain1, bias1 = ln1_gain.reshape(1, D), ln1_bias.reshape(1, D)
    gain2, bias2 = ln2_gain.reshape(1, D), ln2_bias.reshape(1, D)
    w2_up = lax.ppermute(expert_out[0], "z", ring(1))
    w2_down = lax.ppermute(expert_out[0], "z", ring(3))
    w2_far = lax.ppermute(w2_down, "z", ring(3))
    w2 = [expert_out[0], w2_up, w2_far, w2_down]
    w1_up = lax.ppermute(expert_in[0], "z", ring(1))

    send_grad, csel, cols = call(
        pack_kernel,
        62,
        (
            shape((EXPERTS, MOST + EXTRA, D), bf16),
            shape((EXPERTS, ROWS), f32),
            shape((ROWS, 128), f32),
        ),
        routes.T,
        priority.reshape(1, ROWS),
        segments,
        cotangent,
        flops=2 * SLOTS * D * D,
        scratch=[pltpu.VMEM((128, ROWS), f32)],
    )
    grad = exchange(send_grad, DP)

    packed, attended, lse, residual, send_rows = call(
        attend_kernel,
        62,
        (
            shape((ROWS, 3 * D), bf16),
            shape((ROWS, D), bf16),
            shape((ROWS, 128), f32),
            shape((ROWS, D), f32),
            shape((EXPERTS, MOST, D), bf16),
        ),
        tokens,
        segments,
        cols,
        csel,
        gain1,
        bias1,
        w_qkv,
        w_out,
        gain2,
        bias2,
        flops=2 * SLOTS * D * D + 10 * ROWS * D * D,
    )
    send_rows = after(send_rows, w2_up, w2_far, w2_down, w1_up)
    rows = exchange(send_rows, DP)

    expert = lax.axis_index(DP).astype(jnp.int32).reshape(1)
    digits = grad[:, MOST : MOST + EXTRA, 0:MOST].astype(jnp.int32)
    later = lax.dynamic_index_in_dim(digits, 3 + expert[0] % 4, axis=1, keepdims=False)
    keys = digits[:, 0] + 256 * digits[:, 1] + 65536 * (digits[:, 2] + later)
    keys = keys.reshape(16, 128)
    planes = [lax.ppermute(keys, "z", ring(d)) for d in (1, 2, 3)]
    kept = call(keep_kernel, 62, shape((16, 128), f32), keys, keys, *planes).reshape(1, SLOTS)

    steps = SLOTS // BLOCK
    weight_spec = pl.BlockSpec((D, 512), lambda i: (0, 0))
    row_spec = pl.BlockSpec((BLOCK // MOST, MOST, D), lambda i: (i, 0, 0))
    wide_spec = pl.BlockSpec((BLOCK, 2048), lambda i: (i, 0))
    line_spec = pl.BlockSpec((1, BLOCK), lambda i: (0, i))
    smem = pl.BlockSpec(memory_space=pltpu.SMEM)
    vmem = pl.BlockSpec(memory_space=pltpu.VMEM)
    tie = pl.BlockSpec(memory_space=pl.ANY)
    big = 2 * SLOTS * D * 2048
    back = pl.pallas_call(
        back_kernel,
        grid=(steps,),
        in_specs=[row_spec] + [weight_spec] * 4,
        out_specs=wide_spec,
        out_shape=shape((SLOTS, 2048), bf16),
        compiler_params=params(62),
        cost_estimate=pl.CostEstimate(flops=big, bytes_accessed=12 << 20, transcendentals=0),
    )(grad, *w2)
    w1_down = lax.ppermute(expert_in[0], "z", ring(3))
    w1_far = lax.ppermute(w1_up, "z", ring(1))
    w1 = [expert_in[0], w1_up, w1_far, w1_down]
    dslot, act, dpre, scale, dprob = pl.pallas_call(
        slot_kernel,
        grid=(steps,),
        in_specs=[
            smem,
            row_spec,
            wide_spec,
        ]
        + [weight_spec] * 4
        + [
            line_spec,
            pl.BlockSpec((EXPERTS, D), lambda i: (0, 0)),
        ],
        out_specs=[
            row_spec,
            wide_spec,
            wide_spec,
            line_spec,
            pl.BlockSpec((EXPERTS, BLOCK), lambda i: (0, i)),
        ],
        out_shape=(
            shape((EXPERTS, MOST, D), bf16),
            shape((SLOTS, 2048), bf16),
            shape((SLOTS, 2048), bf16),
            shape((1, SLOTS), f32),
            shape((EXPERTS, SLOTS), bf16),
        ),
        compiler_params=params(62),
        cost_estimate=pl.CostEstimate(
            flops=2 * big, bytes_accessed=32 << 20, transcendentals=SLOTS * 2048
        ),
    )(expert, rows, back, *w1, kept, w_router.T)
    dslot_home = after(exchange(dslot, DP), flops=60 * 10**9)

    whole = pl.BlockSpec((EXPERTS, MOST, D), lambda i: (0, 0, 0))
    slices = pl.BlockSpec((SLOTS, 512), lambda i: (0, i))
    y, rows_t, back_t, *d_weights, d_router = pl.pallas_call(
        weight_kernel,
        grid=(N_Z,),
        in_specs=[
            whole,
            whole,
            pl.BlockSpec((1, SLOTS), lambda i: (0, 0)),
            slices,
            slices,
            pl.BlockSpec((EXPERTS, SLOTS), lambda i: (0, 0)),
        ]
        + [weight_spec] * 4,
        out_specs=[whole]
        + [pl.BlockSpec((D, SLOTS), lambda i: (0, 0))] * 2
        + [pl.BlockSpec((2, D, 512), lambda i: (0, 0, 0))] * 3
        + [pl.BlockSpec((D, EXPERTS), lambda i: (0, 0))],
        out_shape=(shape((EXPERTS, MOST, D), bf16),)
        + (shape((D, SLOTS), bf16),) * 2
        + (shape((2, D, 512), bf16),) * 3
        + (shape((D, EXPERTS), f32),),
        scratch_shapes=[
            pltpu.VMEM((N_Z, 512, D), bf16),
            pltpu.VMEM((SLOTS, D), f32),
        ],
        compiler_params=params(62),
        cost_estimate=pl.CostEstimate(flops=0, bytes_accessed=0, transcendentals=0),
    )(rows, grad, scale, act, dpre, dprob, *w2)
    y_home = exchange(y, DP)

    down, far, up = d_weights
    received = [
        lax.ppermute(down, "z", ring(3)),
        lax.ppermute(far, "z", ring(2)),
        lax.ppermute(up, "z", ring(1)),
    ]

    core = lax.axis_index("core").astype(jnp.int32).reshape(1)
    keep, send, d_tokens = pl.pallas_call(
        backward_kernel,
        in_specs=[vmem] * 15 + [smem],
        out_shape=(
            shape((ROWS // 2, WIDTH), bf16),
            shape((ROWS // 2, WIDTH), bf16),
            shape((ROWS, D), f32),
        ),
        scratch_shapes=[
            pltpu.VMEM((ROWS, D), bf16),
            pltpu.VMEM((ROWS, 3 * D), bf16),
            pltpu.VMEM((ROWS, 128), f32),
            pltpu.VMEM((ROWS, 128), f32),
            pltpu.VMEM((ROWS, WIDTH), bf16),
            pltpu.VMEM((128, ROWS), f32),
        ],
        compiler_params=params(62),
        cost_estimate=pl.CostEstimate(
            flops=3000000000, bytes_accessed=0, transcendentals=0
        ),
    )(
        dslot_home,
        cols,
        segments,
        tokens,
        cotangent,
        residual,
        packed,
        attended,
        lse,
        gain1,
        bias1,
        w_qkv,
        w_out,
        gain2,
        d_router,
        core,
    )
    low = add_cores(keep, after(send, received[0], received[2]), y_home)
    output = call(output_kernel, 62, shape((ROWS, D), bf16), y_home, cols, residual)
    fixed = pl.BlockSpec((D, SLOTS), lambda i: (0, 0))
    slices = pl.BlockSpec((SLOTS, 512), lambda i: (0, 0))
    d_in, d_out = pl.pallas_call(
        own_kernel,
        grid=(1,),
        in_specs=[fixed, fixed, slices, slices]
        + [pl.BlockSpec((2, D, 512), lambda i: (0, 0, 0))] * 2
        + [tie],
        out_specs=[pl.BlockSpec((1, D, 512), lambda i: (0, 0, 0))] * 2,
        out_shape=(shape((1, D, 512), f32), shape((1, 512, D), f32)),
        compiler_params=params(62),
        cost_estimate=pl.CostEstimate(flops=0, bytes_accessed=0, transcendentals=0),
    )(rows_t, back_t, act, dpre, received[0], received[2], low)
    across = after(received[1], output, d_in, flops=6 * 10**9)
    d_in, d_out = pl.pallas_call(
        across_kernel,
        out_shape=(shape((1, D, 512), f32), shape((1, 512, D), f32)),
        compiler_params=params(62),
        cost_estimate=pl.CostEstimate(flops=0, bytes_accessed=0, transcendentals=0),
    )(d_in, d_out, across)
    low, other = sum_chips(low, across, d_in)
    whole_half = pl.BlockSpec((ROWS // 2, WIDTH), lambda i, which: (0, 0))
    down = lambda i, which: (which[0], 0)
    across = lambda i, which: (0, which[0])

    def finish(which, half, *earlier):
        return pl.pallas_call(
            finish_kernel,
            grid_spec=pltpu.PrefetchScalarGridSpec(
                num_scalar_prefetch=1,
                grid=(1,),
                in_specs=[whole_half] + [tie] * len(earlier),
                out_specs=[
                    pl.BlockSpec((ROWS // 2, 3 * D), down),
                    pl.BlockSpec((ROWS // 2, D), down),
                    pl.BlockSpec((EXPERTS, ROWS // 2), across),
                ]
                + [pl.BlockSpec((1, ROWS // 2), across)] * 4,
            ),
            out_shape=(shape((D, 3 * D), f32), shape((D, D), f32), shape((EXPERTS, D), f32))
            + (shape((1, D), f32),) * 4,
            input_output_aliases={2 + i: i for i in range(len(earlier))},
            compiler_params=params(62),
            cost_estimate=pl.CostEstimate(flops=0, bytes_accessed=0, transcendentals=0),
        )(which, half, *earlier)

    d_w_qkv, d_w_out, d_w_router, *norms = finish(1 - core, other, *finish(core, low))
    return (
        output,
        d_tokens,
        norms[0].reshape(D),
        norms[1].reshape(D),
        d_w_qkv,
        d_w_out,
        norms[2].reshape(D),
        norms[3].reshape(D),
        d_w_router.T,
        d_in,
        d_out,
    )


def solution(mesh):
    fine = Mesh(mesh.devices.reshape(4, 4, 4, 2), ("z", "x", "y", "core"))
    every = ("z", "x", "y", "core")
    both = P(every, None)
    in_specs = (
        both,
        both,
        both,
        P(every),
        P(),
        P(),
        P(),
        P(),
        P(),
        P(),
        P(),
        P(DP, None, "z"),
        P(DP, "z", None),
        both,
    )
    out_specs = (
        both,
        both,
        P(),
        P(),
        P(),
        P(),
        P(),
        P(),
        P(),
        P(DP, None, "z"),
        P(DP, "z", None),
    )
    return jax.shard_map(
        per_device, mesh=fine, in_specs=in_specs, out_specs=out_specs, check_vma=False
    )
```

```python
import functools

import jax
import jax.numpy as jnp
from jax import lax
from jax.experimental import pallas as pl
from jax.experimental.pallas import tpu as pltpu
from jax.sharding import Mesh
from jax.sharding import PartitionSpec as P

D = 512
HEADS = 8
HDIM = 64
EXPERTS = 32
MOST = 64
ROWS = 512
SLOTS = EXPERTS * MOST
N_Z = 4
N_DP = 32
CAP = (21 * N_Z * N_DP * ROWS + 319) // 320
TOKENS = N_Z * N_DP * ROWS
EXTRA = 8
BLOCK = 512
WIDTH = 4 * D + 128
EPS = 1e-06
SCALE = HDIM ** (-0.5)
STARTS = (0, 64, 192, 256)
GELU_C = 0.7978845608028654
GELU_A = 0.044715

bf16 = jnp.bfloat16
f32 = jnp.float32
MIB = 1024 * 1024


def dot(a, b):
    return lax.dot_general(a, b, (((1,), (0,)), ((), ())), preferred_element_type=f32)


def dot_nt(a, b):
    return lax.dot_general(a, b, (((1,), (1,)), ((), ())), preferred_element_type=f32)


def dot_tn(a, b):
    return lax.dot_general(a, b, (((0,), (0,)), ((), ())), preferred_element_type=f32)


def iota(shape, dim):
    return lax.broadcasted_iota(jnp.int32, shape, dim)


def normalize(values):
    center = values - jnp.mean(values, axis=-1, keepdims=True)
    factor = lax.rsqrt(jnp.mean(center * center, axis=-1, keepdims=True) + EPS)
    return center * factor, factor


def norm_backward(upstream, normal, factor, gain):
    scaled = upstream * gain
    inner = (
        scaled
        - jnp.mean(scaled, axis=-1, keepdims=True)
        - normal * jnp.mean(scaled * normal, axis=-1, keepdims=True)
    )
    return (
        inner * factor,
        jnp.sum(upstream * normal, axis=0, keepdims=True),
        jnp.sum(upstream, axis=0, keepdims=True),
    )


def pick_rows(csel_ref, rows, store):
    place = iota((MOST, ROWS), 0).astype(f32)
    for group in range(EXPERTS // 4):
        parts = []
        for j in range(4):
            line = csel_ref[group * 4 + j : group * 4 + j + 1, :]
            parts.append((place == line).astype(f32).astype(bf16))
        hot = jnp.concatenate(parts, axis=0)
        store(group, dot(hot, rows).astype(bf16))


def pack_kernel(routes_ref, prio_ref, seg_ref, cot_ref, send_ref, csel_ref, cols_ref, wide_ref):
    routes = routes_ref[...]
    experts = iota((EXPERTS, ROWS), 0)
    first = routes[0:1] == experts
    second = routes[1:2] == experts
    either = jnp.logical_or(first, second)
    before = (iota((ROWS, ROWS), 0) < iota((ROWS, ROWS), 1)).astype(f32).astype(bf16)
    count = dot(either.astype(f32).astype(bf16), before)
    slot = count + (experts * MOST).astype(f32)
    wide_ref[...] = jnp.zeros_like(wide_ref)
    wide_ref[0:1, :] = jnp.sum(jnp.where(first, slot, 0.0), axis=0, keepdims=True)
    wide_ref[1:2, :] = jnp.sum(jnp.where(second, slot, 0.0), axis=0, keepdims=True)
    wide_ref[2:3, :] = prio_ref[...].astype(f32)
    wide_ref[3:4, :] = seg_ref[...].astype(f32)
    csel_ref[...] = jnp.where(either, count, -1.0)
    cols = wide_ref[...].T
    cols_ref[...] = cols
    key = prio_ref[...] + 1
    digits = [
        jnp.bitwise_and(key, 255),
        jnp.bitwise_and(jnp.right_shift(key, 8), 255),
        jnp.right_shift(key, 16),
    ]
    digits = [line.astype(f32) for line in digits]
    later = second.astype(f32)
    empty = jnp.zeros((1, ROWS), f32)
    blank = jnp.zeros((EXTRA, 128 - MOST), f32)
    rows = cot_ref[...]
    place = iota((MOST, ROWS), 0).astype(f32)
    for group in range(EXPERTS // 4):
        four = range(group * 4, group * 4 + 4)
        hot = jnp.concatenate(
            [(place == csel_ref[e : e + 1, :]).astype(f32).astype(bf16) for e in four], axis=0
        )
        picked = dot(hot, rows).astype(bf16)
        quarters = picked.reshape(4, 4, MOST // 4, D)
        for quarter in range(4):
            send_ref[group * 4 : group * 4 + 4, :, quarter * D : quarter * D + D] = quarters[
                :, quarter
            ]
        lines = jnp.concatenate(digits + [later[e : e + 1] for e in four] + [empty], axis=0)
        keys = dot_nt(lines.astype(bf16), hot)
        for j, e in enumerate(four):
            send_ref[e, :, 4 * D :] = jnp.concatenate(
                [
                    jnp.concatenate([keys[:, j * MOST : (j + 1) * MOST], blank], axis=1),
                    jnp.zeros((8, 128), f32),
                ],
                axis=0,
            ).astype(bf16)


def stacked(pair):
    lanes = iota(pair.shape, 1)
    zero = jnp.zeros_like(pair)
    return jnp.concatenate(
        [jnp.where(lanes < HDIM, pair, zero), jnp.where(lanes >= HDIM, pair, zero)], axis=0
    )


def band_bias(cols_ref, seg_ref, block):
    start = STARTS[block]
    same = (
        cols_ref[block * 128 : block * 128 + 128, 3:4]
        == seg_ref[:, start : start + 256].astype(f32)
    )
    bias = jnp.where(same, 0.0, -1e30)
    return jnp.concatenate([bias, bias], axis=0)


def attend_kernel(
    tokens_ref,
    seg_ref,
    cols_ref,
    csel_ref,
    gain1_ref,
    bias1_ref,
    w_qkv_ref,
    w_out_ref,
    gain2_ref,
    bias2_ref,
    packed_ref,
    attended_ref,
    lse_ref,
    residual_ref,
    send_ref,
):
    inputs = tokens_ref[...].astype(f32)
    normal, _ = normalize(inputs)
    first = (normal * gain1_ref[...] + bias1_ref[...]).astype(bf16)
    for part in range(3):
        packed_ref[:, part * D : (part + 1) * D] = dot(
            first, w_qkv_ref[:, part * D : (part + 1) * D]
        ).astype(bf16)
    lanes = iota((128, 128), 1)
    for block in range(4):
        here = slice(block * 128, block * 128 + 128)
        window = slice(STARTS[block], STARTS[block] + 256)
        bias = band_bias(cols_ref, seg_ref, block)
        lse = jnp.zeros((128, 128), f32)
        for pair in range(4):
            at = pair * 128
            query = stacked(packed_ref[here, at : at + 128])
            scores = dot_nt(query, packed_ref[window, D + at : D + at + 128]) * SCALE + bias
            highest = jnp.max(scores, axis=-1, keepdims=True)
            raised = jnp.exp(scores - highest)
            total = jnp.sum(raised, axis=-1, keepdims=True)
            weights = (raised * (1.0 / total)).astype(bf16)
            mixed = dot(weights, packed_ref[window, 2 * D + at : 2 * D + at + 128])
            attended_ref[here, at : at + 128] = jnp.where(
                lanes < HDIM, mixed[0:128], mixed[128:256]
            ).astype(bf16)
            logsum = highest + jnp.log(total)
            lse = jnp.where(lanes == 2 * pair, logsum[0:128], lse)
            lse = jnp.where(lanes == 2 * pair + 1, logsum[128:256], lse)
        lse_ref[here, :] = lse
    residual = inputs + dot(attended_ref[...], w_out_ref[...])
    residual_ref[...] = residual
    normal2, _ = normalize(residual)
    second = (normal2 * gain2_ref[...] + bias2_ref[...]).astype(bf16)

    def store(group, rows):
        send_ref[group * 4 : group * 4 + 4] = rows.reshape(4, MOST, D)

    pick_rows(csel_ref, second, store)


def keep_kernel(own_ref, a_ref, b_ref, c_ref, d_ref, kept_ref):
    empty = 2 * TOKENS + 1
    keys = jnp.concatenate([a_ref[...], b_ref[...], c_ref[...], d_ref[...]], axis=0)
    keys = jnp.where(keys == 0, empty, keys)

    def step(_, bounds):
        low, high = bounds
        middle = jnp.right_shift(low + high, 1)
        enough = jnp.sum((keys <= middle).astype(jnp.int32), keepdims=True) >= CAP
        return jnp.where(enough, low, middle + 1), jnp.where(enough, middle, high)

    low = jnp.zeros((1, 1), jnp.int32)
    high = jnp.full((1, 1), 2 * TOKENS, jnp.int32)
    low, high = lax.fori_loop(0, 18, step, (low, high))
    own = own_ref[...]
    kept_ref[...] = jnp.logical_and(own > 0, own <= high).astype(f32)


def unpacked(grad_ref, sources):
    quarters = [grad_ref[sources, :, at : at + D] for at in range(0, 4 * D, D)]
    return jnp.concatenate([q[:, None] for q in quarters], axis=1).reshape(-1, D)


def back_kernel(grad_ref, *refs):
    *w2_refs, out_ref = refs
    rows = unpacked(grad_ref, slice(None))
    for part, w2_ref in enumerate(w2_refs):
        out_ref[:, part * 512 : part * 512 + 512] = dot_nt(rows, w2_ref[...]).astype(bf16)


def slot_kernel(
    expert_ref,
    x_ref,
    gw_ref,
    w1a_ref,
    w1b_ref,
    w1c_ref,
    w1d_ref,
    kept_ref,
    w_router_ref,
    dslot_ref,
    act_ref,
    dpre_ref,
    scale_ref,
    dprob_ref,
):
    rows = x_ref[...].reshape(BLOCK, D)
    w_router = w_router_ref[...]
    dslot = jnp.zeros((BLOCK, D), f32)
    dgate = jnp.zeros((BLOCK, 128), f32)
    parts = (w1a_ref, w1b_ref, w1c_ref, w1d_ref)
    tiles = [ref[:, at : at + 256] for ref in parts for at in (0, 256)]
    pre = dot(rows, tiles[0])
    held = None
    for step, weight in enumerate(tiles):
        following = dot(rows, tiles[step + 1]) if step + 1 < len(tiles) else None
        if step == 4:
            logits = dot_nt(w_router, rows)
            raised = jnp.exp(logits - jnp.max(logits, axis=0, keepdims=True))
            prob = raised / jnp.sum(raised, axis=0, keepdims=True)
            mine = iota((EXPERTS, BLOCK), 0) == expert_ref[0]
            scale = kept_ref[...] * jnp.sum(jnp.where(mine, prob, 0.0), axis=0, keepdims=True)
            scale_ref[...] = scale
            scale_col = jnp.broadcast_to(scale, (8, BLOCK)).T[:, 0:1]
        span = slice(step * 256, step * 256 + 256)
        square = pre * pre
        half = 0.5 * jnp.tanh(pre * (square * (GELU_A * GELU_C) + GELU_C)) + 0.5
        act = pre * half
        slope = half + act * (1.0 - half) * (square * (6.0 * GELU_A * GELU_C) + 2.0 * GELU_C)
        upstream = gw_ref[:, span].astype(f32)
        product = upstream * act
        dgate = dgate + product[:, 0:128] + product[:, 128:256]
        dpre = (upstream * slope).astype(bf16)
        act_ref[:, span] = act.astype(bf16)
        dpre_ref[:, span] = dpre
        if held is not None:
            dslot = dslot + dot_nt(*held)
        held = dpre, weight
        pre = following
    dslot = dslot + dot_nt(*held)
    dgate = jnp.sum(dgate.T, axis=0, keepdims=True)
    dprob = dgate * (mine.astype(f32) - prob)
    dprob_ref[...] = dprob.astype(bf16)
    dslot = dslot * scale_col + dot_tn((scale * dprob).astype(bf16), w_router)
    dslot_ref[...] = dslot.astype(bf16).reshape(BLOCK // MOST, MOST, D)


def weight_kernel(
    x_ref,
    grad_ref,
    scale_ref,
    act_ref,
    dpre_ref,
    dprob_ref,
    w2a_ref,
    w2b_ref,
    w2c_ref,
    w2d_ref,
    y_ref,
    rows_ref,
    back_ref,
    down_ref,
    far_ref,
    up_ref,
    d_router_ref,
    w2_ref,
    total_ref,
):
    step = pl.program_id(0)

    @pl.when(step == 0)
    def _():
        for at in range(0, SLOTS, 512):
            one = slice(at // MOST, at // MOST + 8)
            here = slice(at, at + 512)
            scale = scale_ref[:, here]
            rows_ref[:, here] = (x_ref[one].reshape(512, D).astype(f32).T * scale).astype(bf16)
            back_ref[:, here] = (
                unpacked(grad_ref, one).astype(f32).T * scale
            ).astype(bf16)
        d_router_ref[...] = dot_nt(rows_ref[...], dprob_ref[...])
        for part, part_ref in enumerate((w2a_ref, w2b_ref, w2c_ref, w2d_ref)):
            w2_ref[part] = part_ref[...]
        total_ref[...] = jnp.zeros_like(total_ref)

    total_ref[...] += dot(act_ref[...], w2_ref[step])

    @pl.when(step > 0)
    def _():
        d_in = dot(rows_ref[...], dpre_ref[...]).astype(bf16)
        d_out = dot(back_ref[...], act_ref[...]).T.astype(bf16)
        for part, out_ref in enumerate((down_ref, far_ref, up_ref)):

            @pl.when(step == part + 1)
            def _():
                out_ref[0] = d_in
                out_ref[1] = d_out

    @pl.when(step == N_Z - 1)
    def _():
        for at in range(0, SLOTS, 512):
            one = slice(at // MOST, at // MOST + 8)
            here = slice(at, at + 512)
            scale_col = jnp.broadcast_to(scale_ref[:, here], (8, 512)).T[:, 0:1]
            y_ref[one] = (total_ref[here, :] * scale_col).astype(bf16).reshape(8, MOST, D)


def gather_slots(cols_ref, rows_ref):
    pos0 = cols_ref[:, 0:1].astype(jnp.int32)
    pos1 = cols_ref[:, 1:2].astype(jnp.int32)
    total = jnp.zeros((ROWS, D), f32)
    for part in range(4):
        spot = iota((ROWS, 512), 1) + part * 512
        hot = jnp.logical_or(spot == pos0, spot == pos1).astype(f32).astype(bf16)
        total = total + dot(hot, rows_ref[part * 8 : part * 8 + 8].reshape(512, D))
    return total


def backward_kernel(
    dslot_ref,
    cols_ref,
    seg_ref,
    tokens_ref,
    cot_ref,
    residual_ref,
    packed_ref,
    attended_ref,
    lse_ref,
    gain1_ref,
    bias1_ref,
    w_qkv_ref,
    w_out_ref,
    gain2_ref,
    d_router_ref,
    core_ref,
    keep_ref,
    send_ref,
    d_tokens_ref,
    datt_ref,
    dpacked_ref,
    dkey_ref,
    dvalue_ref,
    grads_ref,
    wide_ref,
):
    d_second = gather_slots(cols_ref, dslot_ref)
    normal2, factor2 = normalize(residual_ref[...])
    d_norm2, d_gain2, d_shift2 = norm_backward(d_second, normal2, factor2, gain2_ref[...])
    d_residual = cot_ref[...].astype(f32) + d_norm2
    d_tokens_ref[...] = d_residual
    d_branch = d_residual.astype(bf16)
    grads_ref[:, 3 * D : 4 * D] = dot_tn(attended_ref[...], d_branch).astype(bf16)
    datt_ref[...] = dot_nt(d_branch, w_out_ref[...]).astype(bf16)
    lanes = iota((128, 128), 1)
    for pair in range(4):
        at = pair * 128
        dkey_ref[...] = jnp.zeros_like(dkey_ref)
        dvalue_ref[...] = jnp.zeros_like(dvalue_ref)
        for block in range(4):
            here = slice(block * 128, block * 128 + 128)
            window = slice(STARTS[block], STARTS[block] + 256)
            bias = band_bias(cols_ref, seg_ref, block)
            query = stacked(packed_ref[here, at : at + 128])
            upstream = stacked(datt_ref[here, at : at + 128])
            keys = packed_ref[window, D + at : D + at + 128]
            values = packed_ref[window, 2 * D + at : 2 * D + at + 128]
            logsum = jnp.concatenate(
                [
                    lse_ref[here, 2 * pair : 2 * pair + 1],
                    lse_ref[here, 2 * pair + 1 : 2 * pair + 2],
                ],
                axis=0,
            )
            weights = jnp.exp(dot_nt(query, keys) * SCALE + bias - logsum)
            d_weights = dot_nt(upstream, values)
            inner = jnp.sum(weights * d_weights, axis=-1, keepdims=True)
            d_scores = (weights * (d_weights - inner)).astype(bf16)
            d_query = dot(d_scores, keys) * SCALE
            dpacked_ref[here, at : at + 128] = jnp.where(
                lanes < HDIM, d_query[0:128], d_query[128:256]
            ).astype(bf16)
            dkey_ref[window, :] += dot_tn(d_scores, query)
            dvalue_ref[window, :] += dot_tn(weights.astype(bf16), upstream)
        dpacked_ref[:, D + at : D + at + 128] = (dkey_ref[...] * SCALE).astype(bf16)
        dpacked_ref[:, 2 * D + at : 2 * D + at + 128] = dvalue_ref[...].astype(bf16)
    normal1, factor1 = normalize(tokens_ref[...].astype(f32))
    first = (normal1 * gain1_ref[...] + bias1_ref[...]).astype(bf16)
    for part in range(3):
        grads_ref[:, part * D : (part + 1) * D] = dot_tn(
            first, dpacked_ref[:, part * D : (part + 1) * D]
        ).astype(bf16)
    d_first = dot_nt(dpacked_ref[...], w_qkv_ref[...])
    d_norm1, d_gain1, d_shift1 = norm_backward(d_first, normal1, factor1, gain1_ref[...])
    d_tokens_ref[...] += d_norm1
    wide_ref[...] = jnp.zeros_like(wide_ref)
    wide_ref[0:1, :] = d_gain1
    wide_ref[1:2, :] = d_shift1
    wide_ref[2:3, :] = d_gain2
    wide_ref[3:4, :] = d_shift2
    grads_ref[:, 4 * D :] = wide_ref[...].T.astype(bf16)
    grads_ref[:, 4 * D + EXPERTS : 4 * D + 2 * EXPERTS] = d_router_ref[...].astype(bf16)
    core = core_ref[0]
    keep_ref[...] = grads_ref[pl.ds(pl.multiple_of(core * 256, 256), 256), :]
    send_ref[...] = grads_ref[pl.ds(pl.multiple_of((1 - core) * 256, 256), 256), :]


def finish_kernel(which_ref, half_ref, *refs):
    qkv_ref, out_ref, router_ref, *norm_refs = refs[-7:]
    qkv_ref[...] = half_ref[:, 0 : 3 * D].astype(f32)
    out_ref[...] = half_ref[:, 3 * D : 4 * D].astype(f32)
    lines = half_ref[:, 4 * D :].astype(f32).T
    router_ref[...] = lines[EXPERTS : 2 * EXPERTS]
    for row, norm_ref in enumerate(norm_refs):
        norm_ref[...] = lines[row : row + 1]


def output_kernel(y_ref, cols_ref, residual_ref, out_ref):
    out_ref[...] = (residual_ref[...] + gather_slots(cols_ref, y_ref)).astype(bf16)


def own_kernel(
    rows_ref, back_ref, act_ref, dpre_ref, above_ref, below_ref, token_ref, d_in_ref, d_out_ref
):
    for half, out_ref in enumerate((d_in_ref, d_out_ref)):
        out_ref[0] = above_ref[half].astype(f32) + below_ref[half].astype(f32)
    d_in_ref[0] += dot(rows_ref[...], dpre_ref[...])
    d_out_ref[0] += dot(back_ref[...], act_ref[...]).T


def across_kernel(d_in_ref, d_out_ref, across_ref, sum_in_ref, sum_out_ref):
    sum_in_ref[0] = d_in_ref[0] + across_ref[0].astype(f32)
    sum_out_ref[0] = d_out_ref[0] + across_ref[1].astype(f32)


def params(mib):
    return pltpu.CompilerParams(vmem_limit_bytes=mib * MIB)


def after(values, *tokens, flops=0):
    anywhere = pl.BlockSpec(memory_space=pl.ANY)
    return pl.pallas_call(
        lambda *refs: None,
        in_specs=[anywhere] * (1 + len(tokens)),
        out_specs=anywhere,
        out_shape=shape(values.shape, values.dtype),
        input_output_aliases={0: 0},
        cost_estimate=pl.CostEstimate(flops=flops, bytes_accessed=0, transcendentals=0),
    )(values, *tokens)


def call(kernel, mib, out_shape, *args, flops=0, scratch=()):
    shapes = jax.tree.leaves(out_shape)
    moved = sum(a.size * a.dtype.itemsize for a in args) + sum(
        s.size * s.dtype.itemsize for s in shapes
    )
    return pl.pallas_call(
        kernel,
        out_shape=out_shape,
        scratch_shapes=list(scratch),
        compiler_params=params(mib),
        cost_estimate=pl.CostEstimate(flops=flops, bytes_accessed=moved, transcendentals=0),
    )(*args)


def shape(dims, dtype):
    return jax.ShapeDtypeStruct(dims, dtype)


DP = ("x", "y", "core")
CHIPS = ("x", "y")
SWAP = [(0, 1), (1, 0)]


def ring(distance):
    return [(i, (i + distance) % 4) for i in range(4)]


def exchange(values, axes):
    return lax.all_to_all(values, axes, split_axis=0, concat_axis=0, tiled=True)


def add_cores(keep, send, token):
    got = lax.ppermute(send, "core", SWAP)
    return after((keep.astype(f32) + got.astype(f32)).astype(bf16), token)


def sum_chips(low, early, late):
    parts = exchange(low.reshape(16, 16, WIDTH), CHIPS)
    low = after(jnp.sum(parts.astype(f32), axis=0).astype(bf16), early)
    got = [lax.ppermute(low, "z", ring(d)) for d in (1, 2, 3)]
    got = [after(got[0], late).astype(f32), got[1].astype(f32), got[2].astype(f32)]
    low = ((low.astype(f32) + got[1]) + (got[0] + got[2])).astype(bf16)
    low = exchange(jnp.broadcast_to(low[None], (16, 16, WIDTH)), CHIPS).reshape(256, WIDTH)
    return low, lax.ppermute(low, "core", SWAP)


def per_device(
    tokens,
    segments,
    routes,
    priority,
    ln1_gain,
    ln1_bias,
    w_qkv,
    w_out,
    ln2_gain,
    ln2_bias,
    w_router,
    expert_in,
    expert_out,
    cotangent,
):
    gain1, bias1 = ln1_gain.reshape(1, D), ln1_bias.reshape(1, D)
    gain2, bias2 = ln2_gain.reshape(1, D), ln2_bias.reshape(1, D)
    w2_up = lax.ppermute(expert_out[0], "z", ring(1))
    w2_down = lax.ppermute(expert_out[0], "z", ring(3))
    w2_far = lax.ppermute(w2_down, "z", ring(3))
    w2 = [expert_out[0], w2_up, w2_far, w2_down]
    w1_up = lax.ppermute(expert_in[0], "z", ring(1))

    send_grad, csel, cols = call(
        pack_kernel,
        62,
        (
            shape((EXPERTS, MOST // 4, 4 * D + 128), bf16),
            shape((EXPERTS, ROWS), f32),
            shape((ROWS, 128), f32),
        ),
        routes.T,
        priority.reshape(1, ROWS),
        segments,
        cotangent,
        flops=2 * SLOTS * D * D,
        scratch=[pltpu.VMEM((128, ROWS), f32)],
    )
    grad = exchange(send_grad, DP)

    packed, attended, lse, residual, send_rows = call(
        attend_kernel,
        62,
        (
            shape((ROWS, 3 * D), bf16),
            shape((ROWS, D), bf16),
            shape((ROWS, 128), f32),
            shape((ROWS, D), f32),
            shape((EXPERTS, MOST, D), bf16),
        ),
        tokens,
        segments,
        cols,
        csel,
        gain1,
        bias1,
        w_qkv,
        w_out,
        gain2,
        bias2,
        flops=2 * SLOTS * D * D + 10 * ROWS * D * D,
    )
    send_rows = after(send_rows, w2_up, w2_far, w2_down, w1_up)
    rows = exchange(send_rows, DP)

    expert = lax.axis_index(DP).astype(jnp.int32).reshape(1)
    digits = grad[:, 0:EXTRA, 4 * D : 4 * D + MOST].astype(jnp.int32)
    later = lax.dynamic_index_in_dim(digits, 3 + expert[0] % 4, axis=1, keepdims=False)
    keys = digits[:, 0] + 256 * digits[:, 1] + 65536 * (digits[:, 2] + later)
    keys = keys.reshape(16, 128)
    planes = [lax.ppermute(keys, "z", ring(d)) for d in (1, 2, 3)]
    kept = call(keep_kernel, 62, shape((16, 128), f32), keys, keys, *planes).reshape(1, SLOTS)

    steps = SLOTS // BLOCK
    weight_spec = pl.BlockSpec((D, 512), lambda i: (0, 0))
    row_spec = pl.BlockSpec((BLOCK // MOST, MOST, D), lambda i: (i, 0, 0))
    wide_spec = pl.BlockSpec((BLOCK, 2048), lambda i: (i, 0))
    line_spec = pl.BlockSpec((1, BLOCK), lambda i: (0, i))
    smem = pl.BlockSpec(memory_space=pltpu.SMEM)
    vmem = pl.BlockSpec(memory_space=pltpu.VMEM)
    tie = pl.BlockSpec(memory_space=pl.ANY)
    big = 2 * SLOTS * D * 2048
    back = pl.pallas_call(
        back_kernel,
        grid=(steps,),
        in_specs=[pl.BlockSpec((BLOCK // MOST, MOST // 4, 4 * D + 128), lambda i: (i, 0, 0))]
        + [weight_spec] * 4,
        out_specs=wide_spec,
        out_shape=shape((SLOTS, 2048), bf16),
        compiler_params=params(62),
        cost_estimate=pl.CostEstimate(flops=big, bytes_accessed=12 << 20, transcendentals=0),
    )(grad, *w2)
    w1_down = lax.ppermute(expert_in[0], "z", ring(3))
    w1_far = lax.ppermute(w1_up, "z", ring(1))
    w1 = [expert_in[0], w1_up, w1_far, w1_down]
    dslot, act, dpre, scale, dprob = pl.pallas_call(
        slot_kernel,
        grid=(steps,),
        in_specs=[
            smem,
            row_spec,
            wide_spec,
        ]
        + [weight_spec] * 4
        + [
            line_spec,
            pl.BlockSpec((EXPERTS, D), lambda i: (0, 0)),
        ],
        out_specs=[
            row_spec,
            wide_spec,
            wide_spec,
            line_spec,
            pl.BlockSpec((EXPERTS, BLOCK), lambda i: (0, i)),
        ],
        out_shape=(
            shape((EXPERTS, MOST, D), bf16),
            shape((SLOTS, 2048), bf16),
            shape((SLOTS, 2048), bf16),
            shape((1, SLOTS), f32),
            shape((EXPERTS, SLOTS), bf16),
        ),
        compiler_params=params(62),
        cost_estimate=pl.CostEstimate(
            flops=2 * big, bytes_accessed=32 << 20, transcendentals=SLOTS * 2048
        ),
    )(expert, rows, back, *w1, kept, w_router.T)
    dslot_home = after(exchange(dslot, DP), flops=60 * 10**9)

    whole = pl.BlockSpec((EXPERTS, MOST, D), lambda i: (0, 0, 0))
    slices = pl.BlockSpec((SLOTS, 512), lambda i: (0, i))
    y, rows_t, back_t, *d_weights, d_router = pl.pallas_call(
        weight_kernel,
        grid=(N_Z,),
        in_specs=[
            whole,
            pl.BlockSpec((EXPERTS, MOST // 4, 4 * D + 128), lambda i: (0, 0, 0)),
            pl.BlockSpec((1, SLOTS), lambda i: (0, 0)),
            slices,
            slices,
            pl.BlockSpec((EXPERTS, SLOTS), lambda i: (0, 0)),
        ]
        + [weight_spec] * 4,
        out_specs=[whole]
        + [pl.BlockSpec((D, SLOTS), lambda i: (0, 0))] * 2
        + [pl.BlockSpec((2, D, 512), lambda i: (0, 0, 0))] * 3
        + [pl.BlockSpec((D, EXPERTS), lambda i: (0, 0))],
        out_shape=(shape((EXPERTS, MOST, D), bf16),)
        + (shape((D, SLOTS), bf16),) * 2
        + (shape((2, D, 512), bf16),) * 3
        + (shape((D, EXPERTS), f32),),
        scratch_shapes=[
            pltpu.VMEM((N_Z, 512, D), bf16),
            pltpu.VMEM((SLOTS, D), f32),
        ],
        compiler_params=params(62),
        cost_estimate=pl.CostEstimate(flops=0, bytes_accessed=0, transcendentals=0),
    )(rows, grad, scale, act, dpre, dprob, *w2)
    y_home = exchange(y, DP)

    down, far, up = d_weights
    received = [
        lax.ppermute(down, "z", ring(3)),
        lax.ppermute(far, "z", ring(2)),
        lax.ppermute(up, "z", ring(1)),
    ]

    core = lax.axis_index("core").astype(jnp.int32).reshape(1)
    keep, send, d_tokens = pl.pallas_call(
        backward_kernel,
        in_specs=[vmem] * 15 + [smem],
        out_shape=(
            shape((ROWS // 2, WIDTH), bf16),
            shape((ROWS // 2, WIDTH), bf16),
            shape((ROWS, D), f32),
        ),
        scratch_shapes=[
            pltpu.VMEM((ROWS, D), bf16),
            pltpu.VMEM((ROWS, 3 * D), bf16),
            pltpu.VMEM((ROWS, 128), f32),
            pltpu.VMEM((ROWS, 128), f32),
            pltpu.VMEM((ROWS, WIDTH), bf16),
            pltpu.VMEM((128, ROWS), f32),
        ],
        compiler_params=params(62),
        cost_estimate=pl.CostEstimate(
            flops=3000000000, bytes_accessed=0, transcendentals=0
        ),
    )(
        dslot_home,
        cols,
        segments,
        tokens,
        cotangent,
        residual,
        packed,
        attended,
        lse,
        gain1,
        bias1,
        w_qkv,
        w_out,
        gain2,
        d_router,
        core,
    )
    low = add_cores(keep, after(send, received[0], received[2]), y_home)
    output = call(output_kernel, 62, shape((ROWS, D), bf16), y_home, cols, residual)
    fixed = pl.BlockSpec((D, SLOTS), lambda i: (0, 0))
    slices = pl.BlockSpec((SLOTS, 512), lambda i: (0, 0))
    d_in, d_out = pl.pallas_call(
        own_kernel,
        grid=(1,),
        in_specs=[fixed, fixed, slices, slices]
        + [pl.BlockSpec((2, D, 512), lambda i: (0, 0, 0))] * 2
        + [tie],
        out_specs=[pl.BlockSpec((1, D, 512), lambda i: (0, 0, 0))] * 2,
        out_shape=(shape((1, D, 512), f32), shape((1, 512, D), f32)),
        compiler_params=params(62),
        cost_estimate=pl.CostEstimate(flops=0, bytes_accessed=0, transcendentals=0),
    )(rows_t, back_t, act, dpre, received[0], received[2], low)
    across = after(received[1], output, d_in, flops=6 * 10**9)
    d_in, d_out = pl.pallas_call(
        across_kernel,
        out_shape=(shape((1, D, 512), f32), shape((1, 512, D), f32)),
        compiler_params=params(62),
        cost_estimate=pl.CostEstimate(flops=0, bytes_accessed=0, transcendentals=0),
    )(d_in, d_out, across)
    low, other = sum_chips(low, across, d_in)
    whole_half = pl.BlockSpec((ROWS // 2, WIDTH), lambda i, which: (0, 0))
    down = lambda i, which: (which[0], 0)
    across = lambda i, which: (0, which[0])

    def finish(which, half, *earlier):
        return pl.pallas_call(
            finish_kernel,
            grid_spec=pltpu.PrefetchScalarGridSpec(
                num_scalar_prefetch=1,
                grid=(1,),
                in_specs=[whole_half] + [tie] * len(earlier),
                out_specs=[
                    pl.BlockSpec((ROWS // 2, 3 * D), down),
                    pl.BlockSpec((ROWS // 2, D), down),
                    pl.BlockSpec((EXPERTS, ROWS // 2), across),
                ]
                + [pl.BlockSpec((1, ROWS // 2), across)] * 4,
            ),
            out_shape=(shape((D, 3 * D), f32), shape((D, D), f32), shape((EXPERTS, D), f32))
            + (shape((1, D), f32),) * 4,
            input_output_aliases={2 + i: i for i in range(len(earlier))},
            compiler_params=params(62),
            cost_estimate=pl.CostEstimate(flops=0, bytes_accessed=0, transcendentals=0),
        )(which, half, *earlier)

    d_w_qkv, d_w_out, d_w_router, *norms = finish(1 - core, other, *finish(core, low))
    return (
        output,
        d_tokens,
        norms[0].reshape(D),
        norms[1].reshape(D),
        d_w_qkv,
        d_w_out,
        norms[2].reshape(D),
        norms[3].reshape(D),
        d_w_router.T,
        d_in,
        d_out,
    )


def solution(mesh):
    fine = Mesh(mesh.devices.reshape(4, 4, 4, 2), ("z", "x", "y", "core"))
    every = ("z", "x", "y", "core")
    both = P(every, None)
    in_specs = (
        both,
        both,
        both,
        P(every),
        P(),
        P(),
        P(),
        P(),
        P(),
        P(),
        P(),
        P(DP, None, "z"),
        P(DP, "z", None),
        both,
    )
    out_specs = (
        both,
        both,
        P(),
        P(),
        P(),
        P(),
        P(),
        P(),
        P(),
        P(DP, None, "z"),
        P(DP, "z", None),
    )
    return jax.shard_map(
        per_device, mesh=fine, in_specs=in_specs, out_specs=out_specs, check_vma=False
    )
```

```python
import functools

import jax
import jax.numpy as jnp
from jax import lax
from jax.experimental import pallas as pl
from jax.experimental.pallas import tpu as pltpu
from jax.sharding import Mesh
from jax.sharding import PartitionSpec as P

D = 512
HEADS = 8
HDIM = 64
EXPERTS = 32
MOST = 64
ROWS = 512
SLOTS = EXPERTS * MOST
N_Z = 4
N_DP = 32
CAP = (21 * N_Z * N_DP * ROWS + 319) // 320
TOKENS = N_Z * N_DP * ROWS
EXTRA = 8
BLOCK = 512
WIDTH = 4 * D + 128
EPS = 1e-06
SCALE = HDIM ** (-0.5)
STARTS = (0, 64, 192, 256)
GELU_C = 0.7978845608028654
GELU_A = 0.044715

bf16 = jnp.bfloat16
f32 = jnp.float32
MIB = 1024 * 1024


def dot(a, b):
    return lax.dot_general(a, b, (((1,), (0,)), ((), ())), preferred_element_type=f32)


def dot_nt(a, b):
    return lax.dot_general(a, b, (((1,), (1,)), ((), ())), preferred_element_type=f32)


def dot_tn(a, b):
    return lax.dot_general(a, b, (((0,), (0,)), ((), ())), preferred_element_type=f32)


def iota(shape, dim):
    return lax.broadcasted_iota(jnp.int32, shape, dim)


def normalize(values):
    center = values - jnp.mean(values, axis=-1, keepdims=True)
    factor = lax.rsqrt(jnp.mean(center * center, axis=-1, keepdims=True) + EPS)
    return center * factor, factor


def norm_backward(upstream, normal, factor, gain):
    scaled = upstream * gain
    inner = (
        scaled
        - jnp.mean(scaled, axis=-1, keepdims=True)
        - normal * jnp.mean(scaled * normal, axis=-1, keepdims=True)
    )
    return (
        inner * factor,
        jnp.sum(upstream * normal, axis=0, keepdims=True),
        jnp.sum(upstream, axis=0, keepdims=True),
    )


def pick_rows(csel_ref, rows, store):
    place = iota((MOST, ROWS), 0).astype(f32)
    for group in range(EXPERTS // 4):
        parts = []
        for j in range(4):
            line = csel_ref[group * 4 + j : group * 4 + j + 1, :]
            parts.append((place == line).astype(f32).astype(bf16))
        hot = jnp.concatenate(parts, axis=0)
        store(group, dot(hot, rows).astype(bf16))


def pack_kernel(routes_ref, prio_ref, seg_ref, cot_ref, send_ref, csel_ref, cols_ref, wide_ref):
    routes = routes_ref[...]
    experts = iota((EXPERTS, ROWS), 0)
    first = routes[0:1] == experts
    second = routes[1:2] == experts
    either = jnp.logical_or(first, second)
    before = (iota((ROWS, ROWS), 0) < iota((ROWS, ROWS), 1)).astype(f32).astype(bf16)
    count = dot(either.astype(f32).astype(bf16), before)
    slot = count + (experts * MOST).astype(f32)
    wide_ref[...] = jnp.zeros_like(wide_ref)
    wide_ref[0:1, :] = jnp.sum(jnp.where(first, slot, 0.0), axis=0, keepdims=True)
    wide_ref[1:2, :] = jnp.sum(jnp.where(second, slot, 0.0), axis=0, keepdims=True)
    wide_ref[2:3, :] = prio_ref[...].astype(f32)
    wide_ref[3:4, :] = seg_ref[...].astype(f32)
    csel_ref[...] = jnp.where(either, count, -1.0)
    cols = wide_ref[...].T
    cols_ref[...] = cols
    key = prio_ref[...] + 1
    digits = [
        jnp.bitwise_and(key, 255),
        jnp.bitwise_and(jnp.right_shift(key, 8), 255),
        jnp.right_shift(key, 16),
    ]
    digits = [line.astype(f32) for line in digits]
    later = second.astype(f32)
    empty = jnp.zeros((1, ROWS), f32)
    blank = jnp.zeros((EXTRA, 128 - MOST), f32)
    rows = cot_ref[...]
    place = iota((MOST, ROWS), 0).astype(f32)
    for group in range(EXPERTS // 4):
        four = range(group * 4, group * 4 + 4)
        hot = jnp.concatenate(
            [(place == csel_ref[e : e + 1, :]).astype(f32).astype(bf16) for e in four], axis=0
        )
        picked = dot(hot, rows).astype(bf16)
        quarters = picked.reshape(4, 4, MOST // 4, D)
        for quarter in range(4):
            send_ref[group * 4 : group * 4 + 4, :, quarter * D : quarter * D + D] = quarters[
                :, quarter
            ]
        lines = jnp.concatenate(digits + [later[e : e + 1] for e in four] + [empty], axis=0)
        keys = dot_nt(lines.astype(bf16), hot)
        for j, e in enumerate(four):
            send_ref[e, :, 4 * D :] = jnp.concatenate(
                [
                    jnp.concatenate([keys[:, j * MOST : (j + 1) * MOST], blank], axis=1),
                    jnp.zeros((8, 128), f32),
                ],
                axis=0,
            ).astype(bf16)


def stacked(pair):
    lanes = iota(pair.shape, 1)
    zero = jnp.zeros_like(pair)
    return jnp.concatenate(
        [jnp.where(lanes < HDIM, pair, zero), jnp.where(lanes >= HDIM, pair, zero)], axis=0
    )


def band_bias(cols_ref, seg_ref, block):
    start = STARTS[block]
    same = (
        cols_ref[block * 128 : block * 128 + 128, 3:4]
        == seg_ref[:, start : start + 256].astype(f32)
    )
    bias = jnp.where(same, 0.0, -1e30)
    return jnp.concatenate([bias, bias], axis=0)


def attend_kernel(
    tokens_ref,
    seg_ref,
    cols_ref,
    csel_ref,
    gain1_ref,
    bias1_ref,
    w_qkv_ref,
    w_out_ref,
    gain2_ref,
    bias2_ref,
    packed_ref,
    attended_ref,
    lse_ref,
    residual_ref,
    send_ref,
):
    inputs = tokens_ref[...].astype(f32)
    normal, _ = normalize(inputs)
    first = (normal * gain1_ref[...] + bias1_ref[...]).astype(bf16)
    for part in range(3):
        packed_ref[:, part * D : (part + 1) * D] = dot(
            first, w_qkv_ref[:, part * D : (part + 1) * D]
        ).astype(bf16)
    lanes = iota((128, 128), 1)
    for block in range(4):
        here = slice(block * 128, block * 128 + 128)
        window = slice(STARTS[block], STARTS[block] + 256)
        bias = band_bias(cols_ref, seg_ref, block)
        lse = jnp.zeros((128, 128), f32)
        for pair in range(4):
            at = pair * 128
            query = stacked(packed_ref[here, at : at + 128])
            scores = dot_nt(query, packed_ref[window, D + at : D + at + 128]) * SCALE + bias
            highest = jnp.max(scores, axis=-1, keepdims=True)
            raised = jnp.exp(scores - highest)
            total = jnp.sum(raised, axis=-1, keepdims=True)
            weights = (raised * (1.0 / total)).astype(bf16)
            mixed = dot(weights, packed_ref[window, 2 * D + at : 2 * D + at + 128])
            attended_ref[here, at : at + 128] = jnp.where(
                lanes < HDIM, mixed[0:128], mixed[128:256]
            ).astype(bf16)
            logsum = highest + jnp.log(total)
            lse = jnp.where(lanes == 2 * pair, logsum[0:128], lse)
            lse = jnp.where(lanes == 2 * pair + 1, logsum[128:256], lse)
        lse_ref[here, :] = lse
    residual = inputs + dot(attended_ref[...], w_out_ref[...])
    residual_ref[...] = residual
    normal2, _ = normalize(residual)
    second = (normal2 * gain2_ref[...] + bias2_ref[...]).astype(bf16)

    def store(group, rows):
        send_ref[group * 4 : group * 4 + 4] = rows.reshape(4, MOST, D)

    pick_rows(csel_ref, second, store)


def keep_kernel(own_ref, a_ref, b_ref, c_ref, d_ref, kept_ref):
    empty = 2 * TOKENS + 1
    keys = jnp.concatenate([a_ref[...], b_ref[...], c_ref[...], d_ref[...]], axis=0)
    keys = jnp.where(keys == 0, empty, keys)

    def step(_, bounds):
        low, high = bounds
        middle = jnp.right_shift(low + high, 1)
        enough = jnp.sum((keys <= middle).astype(jnp.int32), keepdims=True) >= CAP
        return jnp.where(enough, low, middle + 1), jnp.where(enough, middle, high)

    low = jnp.zeros((1, 1), jnp.int32)
    high = jnp.full((1, 1), 2 * TOKENS, jnp.int32)
    low, high = lax.fori_loop(0, 18, step, (low, high))
    own = own_ref[...]
    kept_ref[...] = jnp.logical_and(own > 0, own <= high).astype(f32)


def unpacked(grad_ref, sources):
    quarters = [grad_ref[sources, :, at : at + D] for at in range(0, 4 * D, D)]
    return jnp.concatenate([q[:, None] for q in quarters], axis=1).reshape(-1, D)


def back_kernel(grad_ref, *refs):
    *w2_refs, out_ref = refs
    rows = unpacked(grad_ref, slice(None))
    for part, w2_ref in enumerate(w2_refs):
        out_ref[:, part * 512 : part * 512 + 512] = dot_nt(rows, w2_ref[...]).astype(bf16)


def slot_kernel(
    expert_ref,
    x_ref,
    gw_ref,
    w1a_ref,
    w1b_ref,
    w1c_ref,
    w1d_ref,
    kept_ref,
    w_router_ref,
    dslot_ref,
    act_ref,
    dpre_ref,
    scale_ref,
    dprob_ref,
):
    rows = x_ref[...].reshape(BLOCK, D)
    w_router = w_router_ref[...]
    dslot = jnp.zeros((BLOCK, D), f32)
    dgate = jnp.zeros((BLOCK, 128), f32)
    parts = (w1a_ref, w1b_ref, w1c_ref, w1d_ref)
    tiles = [ref[:, at : at + 256] for ref in parts for at in (0, 256)]
    pre = dot(rows, tiles[0])
    held = None
    for step, weight in enumerate(tiles):
        following = dot(rows, tiles[step + 1]) if step + 1 < len(tiles) else None
        if step == 4:
            logits = dot_nt(w_router, rows)
            raised = jnp.exp(logits - jnp.max(logits, axis=0, keepdims=True))
            prob = raised / jnp.sum(raised, axis=0, keepdims=True)
            mine = iota((EXPERTS, BLOCK), 0) == expert_ref[0]
            scale = kept_ref[...] * jnp.sum(jnp.where(mine, prob, 0.0), axis=0, keepdims=True)
            half_scale = 0.5 * scale
            scale_ref[...] = half_scale
            scale_col = jnp.broadcast_to(half_scale, (8, BLOCK)).T[:, 0:1]
        span = slice(step * 256, step * 256 + 256)
        square = pre * pre
        bend = jnp.tanh(pre * (square * (GELU_A * GELU_C) + GELU_C))
        rise = 1.0 + bend
        act = pre * rise
        slope = rise + act * (1.0 - bend) * (square * (3.0 * GELU_A * GELU_C) + GELU_C)
        upstream = gw_ref[:, span].astype(f32)
        product = upstream * act
        dgate = dgate + product[:, 0:128] + product[:, 128:256]
        dpre = (upstream * slope).astype(bf16)
        act_ref[:, span] = act.astype(bf16)
        dpre_ref[:, span] = dpre
        if held is not None:
            dslot = dslot + dot_nt(*held)
        held = dpre, weight
        pre = following
    dslot = dslot + dot_nt(*held)
    dgate = jnp.sum(dgate.T, axis=0, keepdims=True)
    dprob = dgate * (mine.astype(f32) - prob)
    dprob_ref[...] = dprob.astype(bf16)
    dslot = dslot * scale_col + dot_tn((half_scale * dprob).astype(bf16), w_router)
    dslot_ref[...] = dslot.astype(bf16).reshape(BLOCK // MOST, MOST, D)


def weight_kernel(
    x_ref,
    grad_ref,
    scale_ref,
    act_ref,
    dpre_ref,
    dprob_ref,
    w2a_ref,
    w2b_ref,
    w2c_ref,
    w2d_ref,
    y_ref,
    rows_ref,
    back_ref,
    down_ref,
    far_ref,
    up_ref,
    d_router_ref,
    w2_ref,
    total_ref,
):
    step = pl.program_id(0)

    @pl.when(step == 0)
    def _():
        for at in range(0, SLOTS, 512):
            one = slice(at // MOST, at // MOST + 8)
            here = slice(at, at + 512)
            scale = scale_ref[:, here]
            rows_ref[:, here] = (x_ref[one].reshape(512, D).astype(f32).T * scale).astype(bf16)
            back_ref[:, here] = (
                unpacked(grad_ref, one).astype(f32).T * scale
            ).astype(bf16)
        d_router_ref[...] = dot_nt(rows_ref[...], dprob_ref[...])
        for part, part_ref in enumerate((w2a_ref, w2b_ref, w2c_ref, w2d_ref)):
            w2_ref[part] = part_ref[...]
        total_ref[...] = jnp.zeros_like(total_ref)

    total_ref[...] += dot(act_ref[...], w2_ref[step])

    @pl.when(step > 0)
    def _():
        d_in = dot(rows_ref[...], dpre_ref[...]).astype(bf16)
        d_out = dot(back_ref[...], act_ref[...]).T.astype(bf16)
        for part, out_ref in enumerate((down_ref, far_ref, up_ref)):

            @pl.when(step == part + 1)
            def _():
                out_ref[0] = d_in
                out_ref[1] = d_out

    @pl.when(step == N_Z - 1)
    def _():
        for at in range(0, SLOTS, 512):
            one = slice(at // MOST, at // MOST + 8)
            here = slice(at, at + 512)
            scale_col = jnp.broadcast_to(scale_ref[:, here], (8, 512)).T[:, 0:1]
            y_ref[one] = (total_ref[here, :] * scale_col).astype(bf16).reshape(8, MOST, D)


def gather_slots(cols_ref, rows_ref):
    pos0 = cols_ref[:, 0:1].astype(jnp.int32)
    pos1 = cols_ref[:, 1:2].astype(jnp.int32)
    total = jnp.zeros((ROWS, D), f32)
    for part in range(4):
        spot = iota((ROWS, 512), 1) + part * 512
        hot = jnp.logical_or(spot == pos0, spot == pos1).astype(f32).astype(bf16)
        total = total + dot(hot, rows_ref[part * 8 : part * 8 + 8].reshape(512, D))
    return total


def backward_kernel(
    dslot_ref,
    cols_ref,
    seg_ref,
    tokens_ref,
    cot_ref,
    residual_ref,
    packed_ref,
    attended_ref,
    lse_ref,
    gain1_ref,
    bias1_ref,
    w_qkv_ref,
    w_out_ref,
    gain2_ref,
    d_router_ref,
    core_ref,
    keep_ref,
    send_ref,
    d_tokens_ref,
    datt_ref,
    dpacked_ref,
    dkey_ref,
    dvalue_ref,
    grads_ref,
    wide_ref,
):
    d_second = gather_slots(cols_ref, dslot_ref)
    normal2, factor2 = normalize(residual_ref[...])
    d_norm2, d_gain2, d_shift2 = norm_backward(d_second, normal2, factor2, gain2_ref[...])
    d_residual = cot_ref[...].astype(f32) + d_norm2
    d_tokens_ref[...] = d_residual
    d_branch = d_residual.astype(bf16)
    grads_ref[:, 3 * D : 4 * D] = dot_tn(attended_ref[...], d_branch).astype(bf16)
    datt_ref[...] = dot_nt(d_branch, w_out_ref[...]).astype(bf16)
    lanes = iota((128, 128), 1)
    for pair in range(4):
        at = pair * 128
        dkey_ref[...] = jnp.zeros_like(dkey_ref)
        dvalue_ref[...] = jnp.zeros_like(dvalue_ref)
        for block in range(4):
            here = slice(block * 128, block * 128 + 128)
            window = slice(STARTS[block], STARTS[block] + 256)
            bias = band_bias(cols_ref, seg_ref, block)
            query = stacked(packed_ref[here, at : at + 128])
            upstream = stacked(datt_ref[here, at : at + 128])
            keys = packed_ref[window, D + at : D + at + 128]
            values = packed_ref[window, 2 * D + at : 2 * D + at + 128]
            logsum = jnp.concatenate(
                [
                    lse_ref[here, 2 * pair : 2 * pair + 1],
                    lse_ref[here, 2 * pair + 1 : 2 * pair + 2],
                ],
                axis=0,
            )
            weights = jnp.exp(dot_nt(query, keys) * SCALE + bias - logsum)
            d_weights = dot_nt(upstream, values)
            inner = jnp.sum(weights * d_weights, axis=-1, keepdims=True)
            d_scores = (weights * (d_weights - inner)).astype(bf16)
            d_query = dot(d_scores, keys) * SCALE
            dpacked_ref[here, at : at + 128] = jnp.where(
                lanes < HDIM, d_query[0:128], d_query[128:256]
            ).astype(bf16)
            dkey_ref[window, :] += dot_tn(d_scores, query)
            dvalue_ref[window, :] += dot_tn(weights.astype(bf16), upstream)
        dpacked_ref[:, D + at : D + at + 128] = (dkey_ref[...] * SCALE).astype(bf16)
        dpacked_ref[:, 2 * D + at : 2 * D + at + 128] = dvalue_ref[...].astype(bf16)
    normal1, factor1 = normalize(tokens_ref[...].astype(f32))
    first = (normal1 * gain1_ref[...] + bias1_ref[...]).astype(bf16)
    for part in range(3):
        grads_ref[:, part * D : (part + 1) * D] = dot_tn(
            first, dpacked_ref[:, part * D : (part + 1) * D]
        ).astype(bf16)
    d_first = dot_nt(dpacked_ref[...], w_qkv_ref[...])
    d_norm1, d_gain1, d_shift1 = norm_backward(d_first, normal1, factor1, gain1_ref[...])
    d_tokens_ref[...] += d_norm1
    wide_ref[...] = jnp.zeros_like(wide_ref)
    wide_ref[0:1, :] = d_gain1
    wide_ref[1:2, :] = d_shift1
    wide_ref[2:3, :] = d_gain2
    wide_ref[3:4, :] = d_shift2
    grads_ref[:, 4 * D :] = wide_ref[...].T.astype(bf16)
    grads_ref[:, 4 * D + EXPERTS : 4 * D + 2 * EXPERTS] = d_router_ref[...].astype(bf16)
    core = core_ref[0]
    keep_ref[...] = grads_ref[pl.ds(pl.multiple_of(core * 256, 256), 256), :]
    send_ref[...] = grads_ref[pl.ds(pl.multiple_of((1 - core) * 256, 256), 256), :]


def finish_kernel(which_ref, half_ref, *refs):
    qkv_ref, out_ref, router_ref, *norm_refs = refs[-7:]
    qkv_ref[...] = half_ref[:, 0 : 3 * D].astype(f32)
    out_ref[...] = half_ref[:, 3 * D : 4 * D].astype(f32)
    lines = half_ref[:, 4 * D :].astype(f32).T
    router_ref[...] = lines[EXPERTS : 2 * EXPERTS]
    for row, norm_ref in enumerate(norm_refs):
        norm_ref[...] = lines[row : row + 1]


def output_kernel(y_ref, cols_ref, residual_ref, out_ref):
    out_ref[...] = (residual_ref[...] + gather_slots(cols_ref, y_ref)).astype(bf16)


def own_kernel(
    rows_ref, back_ref, act_ref, dpre_ref, above_ref, below_ref, token_ref, d_in_ref, d_out_ref
):
    for half, out_ref in enumerate((d_in_ref, d_out_ref)):
        out_ref[0] = above_ref[half].astype(f32) + below_ref[half].astype(f32)
    d_in_ref[0] += dot(rows_ref[...], dpre_ref[...])
    d_out_ref[0] += dot(back_ref[...], act_ref[...]).T


def across_kernel(d_in_ref, d_out_ref, across_ref, sum_in_ref, sum_out_ref):
    sum_in_ref[0] = d_in_ref[0] + across_ref[0].astype(f32)
    sum_out_ref[0] = d_out_ref[0] + across_ref[1].astype(f32)


def params(mib):
    return pltpu.CompilerParams(vmem_limit_bytes=mib * MIB)


def after(values, *tokens, flops=0):
    anywhere = pl.BlockSpec(memory_space=pl.ANY)
    return pl.pallas_call(
        lambda *refs: None,
        in_specs=[anywhere] * (1 + len(tokens)),
        out_specs=anywhere,
        out_shape=shape(values.shape, values.dtype),
        input_output_aliases={0: 0},
        cost_estimate=pl.CostEstimate(flops=flops, bytes_accessed=0, transcendentals=0),
    )(values, *tokens)


def call(kernel, mib, out_shape, *args, flops=0, scratch=()):
    shapes = jax.tree.leaves(out_shape)
    moved = sum(a.size * a.dtype.itemsize for a in args) + sum(
        s.size * s.dtype.itemsize for s in shapes
    )
    return pl.pallas_call(
        kernel,
        out_shape=out_shape,
        scratch_shapes=list(scratch),
        compiler_params=params(mib),
        cost_estimate=pl.CostEstimate(flops=flops, bytes_accessed=moved, transcendentals=0),
    )(*args)


def shape(dims, dtype):
    return jax.ShapeDtypeStruct(dims, dtype)


DP = ("x", "y", "core")
CHIPS = ("x", "y")
SWAP = [(0, 1), (1, 0)]


def ring(distance):
    return [(i, (i + distance) % 4) for i in range(4)]


def exchange(values, axes):
    return lax.all_to_all(values, axes, split_axis=0, concat_axis=0, tiled=True)


def add_cores(keep, send, token):
    got = lax.ppermute(send, "core", SWAP)
    return after((keep.astype(f32) + got.astype(f32)).astype(bf16), token)


def sum_chips(low, early, late):
    parts = exchange(low.reshape(16, 16, WIDTH), CHIPS)
    low = after(jnp.sum(parts.astype(f32), axis=0).astype(bf16), early)
    got = [lax.ppermute(low, "z", ring(d)) for d in (1, 2, 3)]
    got = [after(got[0], late).astype(f32), got[1].astype(f32), got[2].astype(f32)]
    low = ((low.astype(f32) + got[1]) + (got[0] + got[2])).astype(bf16)
    low = exchange(jnp.broadcast_to(low[None], (16, 16, WIDTH)), CHIPS).reshape(256, WIDTH)
    return low, lax.ppermute(low, "core", SWAP)


def per_device(
    tokens,
    segments,
    routes,
    priority,
    ln1_gain,
    ln1_bias,
    w_qkv,
    w_out,
    ln2_gain,
    ln2_bias,
    w_router,
    expert_in,
    expert_out,
    cotangent,
):
    gain1, bias1 = ln1_gain.reshape(1, D), ln1_bias.reshape(1, D)
    gain2, bias2 = ln2_gain.reshape(1, D), ln2_bias.reshape(1, D)
    w2_up = lax.ppermute(expert_out[0], "z", ring(1))
    w2_down = lax.ppermute(expert_out[0], "z", ring(3))
    w2_far = lax.ppermute(w2_down, "z", ring(3))
    w2 = [expert_out[0], w2_up, w2_far, w2_down]
    w1_up = lax.ppermute(expert_in[0], "z", ring(1))

    send_grad, csel, cols = call(
        pack_kernel,
        62,
        (
            shape((EXPERTS, MOST // 4, 4 * D + 128), bf16),
            shape((EXPERTS, ROWS), f32),
            shape((ROWS, 128), f32),
        ),
        routes.T,
        priority.reshape(1, ROWS),
        segments,
        cotangent,
        flops=2 * SLOTS * D * D,
        scratch=[pltpu.VMEM((128, ROWS), f32)],
    )
    grad = exchange(send_grad, DP)

    packed, attended, lse, residual, send_rows = call(
        attend_kernel,
        62,
        (
            shape((ROWS, 3 * D), bf16),
            shape((ROWS, D), bf16),
            shape((ROWS, 128), f32),
            shape((ROWS, D), f32),
            shape((EXPERTS, MOST, D), bf16),
        ),
        tokens,
        segments,
        cols,
        csel,
        gain1,
        bias1,
        w_qkv,
        w_out,
        gain2,
        bias2,
        flops=2 * SLOTS * D * D + 10 * ROWS * D * D,
    )
    send_rows = after(send_rows, w2_up, w2_far, w2_down, w1_up)
    rows = exchange(send_rows, DP)

    expert = lax.axis_index(DP).astype(jnp.int32).reshape(1)
    digits = grad[:, 0:EXTRA, 4 * D : 4 * D + MOST].astype(jnp.int32)
    later = lax.dynamic_index_in_dim(digits, 3 + expert[0] % 4, axis=1, keepdims=False)
    keys = digits[:, 0] + 256 * digits[:, 1] + 65536 * (digits[:, 2] + later)
    keys = keys.reshape(16, 128)
    planes = [lax.ppermute(keys, "z", ring(d)) for d in (1, 2, 3)]
    kept = call(keep_kernel, 62, shape((16, 128), f32), keys, keys, *planes).reshape(1, SLOTS)

    steps = SLOTS // BLOCK
    weight_spec = pl.BlockSpec((D, 512), lambda i: (0, 0))
    row_spec = pl.BlockSpec((BLOCK // MOST, MOST, D), lambda i: (i, 0, 0))
    wide_spec = pl.BlockSpec((BLOCK, 2048), lambda i: (i, 0))
    line_spec = pl.BlockSpec((1, BLOCK), lambda i: (0, i))
    smem = pl.BlockSpec(memory_space=pltpu.SMEM)
    vmem = pl.BlockSpec(memory_space=pltpu.VMEM)
    tie = pl.BlockSpec(memory_space=pl.ANY)
    big = 2 * SLOTS * D * 2048
    back = pl.pallas_call(
        back_kernel,
        grid=(steps,),
        in_specs=[pl.BlockSpec((BLOCK // MOST, MOST // 4, 4 * D + 128), lambda i: (i, 0, 0))]
        + [weight_spec] * 4,
        out_specs=wide_spec,
        out_shape=shape((SLOTS, 2048), bf16),
        compiler_params=params(62),
        cost_estimate=pl.CostEstimate(flops=big, bytes_accessed=12 << 20, transcendentals=0),
    )(grad, *w2)
    w1_down = lax.ppermute(expert_in[0], "z", ring(3))
    w1_far = lax.ppermute(w1_up, "z", ring(1))
    w1 = [expert_in[0], w1_up, w1_far, w1_down]
    dslot, act, dpre, scale, dprob = pl.pallas_call(
        slot_kernel,
        grid=(steps,),
        in_specs=[
            smem,
            row_spec,
            wide_spec,
        ]
        + [weight_spec] * 4
        + [
            line_spec,
            pl.BlockSpec((EXPERTS, D), lambda i: (0, 0)),
        ],
        out_specs=[
            row_spec,
            wide_spec,
            wide_spec,
            line_spec,
            pl.BlockSpec((EXPERTS, BLOCK), lambda i: (0, i)),
        ],
        out_shape=(
            shape((EXPERTS, MOST, D), bf16),
            shape((SLOTS, 2048), bf16),
            shape((SLOTS, 2048), bf16),
            shape((1, SLOTS), f32),
            shape((EXPERTS, SLOTS), bf16),
        ),
        compiler_params=params(62),
        cost_estimate=pl.CostEstimate(
            flops=2 * big, bytes_accessed=32 << 20, transcendentals=SLOTS * 2048
        ),
    )(expert, rows, back, *w1, kept, w_router.T)
    dslot_home = after(exchange(dslot, DP), flops=60 * 10**9)

    whole = pl.BlockSpec((EXPERTS, MOST, D), lambda i: (0, 0, 0))
    slices = pl.BlockSpec((SLOTS, 512), lambda i: (0, i))
    y, rows_t, back_t, *d_weights, d_router = pl.pallas_call(
        weight_kernel,
        grid=(N_Z,),
        in_specs=[
            whole,
            pl.BlockSpec((EXPERTS, MOST // 4, 4 * D + 128), lambda i: (0, 0, 0)),
            pl.BlockSpec((1, SLOTS), lambda i: (0, 0)),
            slices,
            slices,
            pl.BlockSpec((EXPERTS, SLOTS), lambda i: (0, 0)),
        ]
        + [weight_spec] * 4,
        out_specs=[whole]
        + [pl.BlockSpec((D, SLOTS), lambda i: (0, 0))] * 2
        + [pl.BlockSpec((2, D, 512), lambda i: (0, 0, 0))] * 3
        + [pl.BlockSpec((D, EXPERTS), lambda i: (0, 0))],
        out_shape=(shape((EXPERTS, MOST, D), bf16),)
        + (shape((D, SLOTS), bf16),) * 2
        + (shape((2, D, 512), bf16),) * 3
        + (shape((D, EXPERTS), f32),),
        scratch_shapes=[
            pltpu.VMEM((N_Z, 512, D), bf16),
            pltpu.VMEM((SLOTS, D), f32),
        ],
        compiler_params=params(62),
        cost_estimate=pl.CostEstimate(flops=0, bytes_accessed=0, transcendentals=0),
    )(rows, grad, scale, act, dpre, dprob, *w2)
    y_home = exchange(y, DP)

    down, far, up = d_weights
    received = [
        lax.ppermute(down, "z", ring(3)),
        lax.ppermute(far, "z", ring(2)),
        lax.ppermute(up, "z", ring(1)),
    ]

    core = lax.axis_index("core").astype(jnp.int32).reshape(1)
    keep, send, d_tokens = pl.pallas_call(
        backward_kernel,
        in_specs=[vmem] * 15 + [smem],
        out_shape=(
            shape((ROWS // 2, WIDTH), bf16),
            shape((ROWS // 2, WIDTH), bf16),
            shape((ROWS, D), f32),
        ),
        scratch_shapes=[
            pltpu.VMEM((ROWS, D), bf16),
            pltpu.VMEM((ROWS, 3 * D), bf16),
            pltpu.VMEM((ROWS, 128), f32),
            pltpu.VMEM((ROWS, 128), f32),
            pltpu.VMEM((ROWS, WIDTH), bf16),
            pltpu.VMEM((128, ROWS), f32),
        ],
        compiler_params=params(62),
        cost_estimate=pl.CostEstimate(
            flops=3000000000, bytes_accessed=0, transcendentals=0
        ),
    )(
        dslot_home,
        cols,
        segments,
        tokens,
        cotangent,
        residual,
        packed,
        attended,
        lse,
        gain1,
        bias1,
        w_qkv,
        w_out,
        gain2,
        d_router,
        core,
    )
    low = add_cores(keep, after(send, received[0], received[2]), y_home)
    output = call(output_kernel, 62, shape((ROWS, D), bf16), y_home, cols, residual)
    fixed = pl.BlockSpec((D, SLOTS), lambda i: (0, 0))
    slices = pl.BlockSpec((SLOTS, 512), lambda i: (0, 0))
    d_in, d_out = pl.pallas_call(
        own_kernel,
        grid=(1,),
        in_specs=[fixed, fixed, slices, slices]
        + [pl.BlockSpec((2, D, 512), lambda i: (0, 0, 0))] * 2
        + [tie],
        out_specs=[pl.BlockSpec((1, D, 512), lambda i: (0, 0, 0))] * 2,
        out_shape=(shape((1, D, 512), f32), shape((1, 512, D), f32)),
        compiler_params=params(62),
        cost_estimate=pl.CostEstimate(flops=0, bytes_accessed=0, transcendentals=0),
    )(rows_t, back_t, act, dpre, received[0], received[2], low)
    across = after(received[1], output, d_in, flops=6 * 10**9)
    d_in, d_out = pl.pallas_call(
        across_kernel,
        out_shape=(shape((1, D, 512), f32), shape((1, 512, D), f32)),
        compiler_params=params(62),
        cost_estimate=pl.CostEstimate(flops=0, bytes_accessed=0, transcendentals=0),
    )(d_in, d_out, across)
    low, other = sum_chips(low, across, d_in)
    whole_half = pl.BlockSpec((ROWS // 2, WIDTH), lambda i, which: (0, 0))
    down = lambda i, which: (which[0], 0)
    across = lambda i, which: (0, which[0])

    def finish(which, half, *earlier):
        return pl.pallas_call(
            finish_kernel,
            grid_spec=pltpu.PrefetchScalarGridSpec(
                num_scalar_prefetch=1,
                grid=(1,),
                in_specs=[whole_half] + [tie] * len(earlier),
                out_specs=[
                    pl.BlockSpec((ROWS // 2, 3 * D), down),
                    pl.BlockSpec((ROWS // 2, D), down),
                    pl.BlockSpec((EXPERTS, ROWS // 2), across),
                ]
                + [pl.BlockSpec((1, ROWS // 2), across)] * 4,
            ),
            out_shape=(shape((D, 3 * D), f32), shape((D, D), f32), shape((EXPERTS, D), f32))
            + (shape((1, D), f32),) * 4,
            input_output_aliases={2 + i: i for i in range(len(earlier))},
            compiler_params=params(62),
            cost_estimate=pl.CostEstimate(flops=0, bytes_accessed=0, transcendentals=0),
        )(which, half, *earlier)

    d_w_qkv, d_w_out, d_w_router, *norms = finish(1 - core, other, *finish(core, low))
    return (
        output,
        d_tokens,
        norms[0].reshape(D),
        norms[1].reshape(D),
        d_w_qkv,
        d_w_out,
        norms[2].reshape(D),
        norms[3].reshape(D),
        d_w_router.T,
        d_in,
        d_out,
    )


def solution(mesh):
    fine = Mesh(mesh.devices.reshape(4, 4, 4, 2), ("z", "x", "y", "core"))
    every = ("z", "x", "y", "core")
    both = P(every, None)
    in_specs = (
        both,
        both,
        both,
        P(every),
        P(),
        P(),
        P(),
        P(),
        P(),
        P(),
        P(),
        P(DP, None, "z"),
        P(DP, "z", None),
        both,
    )
    out_specs = (
        both,
        both,
        P(),
        P(),
        P(),
        P(),
        P(),
        P(),
        P(),
        P(DP, None, "z"),
        P(DP, "z", None),
    )
    return jax.shard_map(
        per_device, mesh=fine, in_specs=in_specs, out_specs=out_specs, check_vma=False
    )
```
